128 devices in a mesh: lon: 16 (over z_lo, x, core), lat: 8 (over y, z_hi).
Axes of the slice: x: 4, y: 4, z: 4 (z_hi: 2, z_lo: 2; z = z_hi * 2 + z_lo), core: 2. Of those that a mesh axis runs over, the one named last changes fastest.
Arguments:
- final_cotangent: float32 [4, 256, 256, 256], P(None, 'lon', 'lat'), may hold values from -6 to 6
- saved_start: bfloat16 [4, 256, 256, 256], P(None, 'lon', 'lat'), may hold values from 0.049804688 to 2
- saved_middle: bfloat16 [4, 256, 256, 256], P(None, 'lon', 'lat'), may hold values from 0.049804688 to 2
- residuals: float32 [2, 4096], P(None, ('lon', 'lat')), may hold values from -6 to 6
- row_cells: int32 [4096, 16], P(('lon', 'lat')), may hold values from 0 to 65535, as said below
- row_count: int32 [4096], P(('lon', 'lat')), may hold values from 1 to 16, as said below
- ocean_mask: int32 [256, 256], P('lon', 'lat'), may hold values 0 or 1
- cell_eez: int32 [256, 256], P('lon', 'lat'), may hold values from 0 to 63
- effort: float32 [64], replicated, may hold values from 0.1 to 2
- kernel: bfloat16 [4, 256, 256], replicated, may hold values from 0.00038909912 to 0.015625
- mix: float32 [4, 4], replicated, may hold values from 0.1 to 1
- assim: float32 [4], replicated, may hold values from 0.2 to 0.8
- mortality: float32 [4, 256], replicated, may hold values from 0.02 to 0.5
- select: float32 [4, 256], replicated, may hold values from 0.05 to 1
- weight: float32 [256], replicated, may hold values from 0.1 to 4
- spread: float32 [256], replicated, may hold values from 0.01 to 0.2
Outputs:
- start_cotangent: float32 [4, 256, 256, 256], P(None, 'lon', 'lat')
- kernel_grad: float32 [4, 256, 256], replicated
- effort_grad: float32 [64], replicated
The draws below stay inside these ranges and needn't reach their ends.
Inputs may be any that keep to these rules, and one draw needn't show every extreme that they name: `row_cells`: all 16 entries of a row, counted or not, name cells. Of the 512 entries of the rows of one device, at most 8 name cells of one device's tile, and on every device some tile is named by exactly 8 of them. `row_count`: on every device some row uses all 16 cells.
All inputs are finite; a program needn't handle non-finite values. No bound on the sum of `ocean_mask` on one device may be relied on, other than what follows from the above.
Results may differ from the reference program's by a relative error of at most 0.0035.
Values sent between devices are 32-bit elements; how exact they have to be, the bound alone decides.
No kernel may reach another device: no remote copies, remote signals or barrier semaphores. Data moves between devices by JAX's collectives and lax.ppermute only.
A program may use at most 128 MiB of HBM per device.

```python
import math
import jax
import jax.numpy as jnp
from jax import lax

G = 4
Z = 256
CLON = 16
CLAT = 32
ROWS_DEV = 32
L = 16
EEZS = 64
NLON = 256
NLAT = 256
ROWS = 4096
N_LON = 16


def route_plan(key):
    owners = NLON // CLON * (NLAT // CLAT)
    lat_tiles = NLAT // CLAT
    capacity = max(2, 2 * ROWS_DEV * L // owners)
    per_dev = ROWS_DEV * L
    coastal_count = min(4, owners)
    base = jax.random.fold_in(key, 11)
    k_hub, k_pick, k_perm, k_shuffle, k_count, k_full, k_cell = jax.random.split(base, 7)
    coastal = jax.random.permutation(k_hub, owners)[:coastal_count]
    hubs = coastal[jax.random.randint(k_pick, (owners,), 0, coastal_count)]
    slots = jnp.arange(owners * capacity, dtype=jnp.int32)

    def order_for(perm_key, shuffle_key, hub):
        score = jax.random.permutation(perm_key, owners * capacity).astype(jnp.int32)
        score = jnp.where(slots // capacity == hub, slots - owners * capacity, score)
        chosen = jnp.argsort(score, stable=True)[:per_dev].astype(jnp.int32)
        return chosen[jax.random.permutation(shuffle_key, per_dev)]
    chosen = jax.vmap(order_for)(jax.random.split(k_perm, owners), jax.random.split(k_shuffle, owners), hubs)
    entry_owner = chosen // capacity
    local = jax.random.randint(k_cell, (owners, per_dev), 0, CLON * CLAT)
    owner_lon = entry_owner // lat_tiles
    owner_lat = entry_owner % lat_tiles
    cells = (owner_lon * CLON + local // CLAT) * NLAT + owner_lat * CLAT + local % CLAT
    counts = jax.random.randint(k_count, (owners, ROWS_DEV), 1, L + 1)
    full_row = jax.random.randint(k_full, (owners,), 0, ROWS_DEV)
    counts = jnp.where(jnp.arange(ROWS_DEV)[None, :] == full_row[:, None], L, counts)
    return (cells.reshape(owners * ROWS_DEV, L).astype(jnp.int32), counts.reshape(owners * ROWS_DEV).astype(jnp.int32))


def draw_row_cells(key, part):
    return route_plan(key)[0]


def draw_row_count(key, part):
    return route_plan(key)[1]


def place_ends(result, own_key, low, top_value):
    longest = result.shape.index(max(result.shape))
    spots = []
    for shift in (0, 1):
        where = [jax.random.randint(jax.random.fold_in(own_key, axis), (), 0, length) for axis, length in enumerate(result.shape)]
        where[longest] = (where[longest] + shift) % result.shape[longest]
        spots.append(tuple(where))
    return result.at[spots[0]].set(low).at[spots[1]].set(top_value)


def block_levels(stream_key, shape, cuts, least, largest):
    factor_of, own = 1.0, jax.random.fold_in(stream_key, 6)
    for axis_at, parts in cuts:
        steps = jnp.exp(jax.random.uniform(jax.random.fold_in(own, axis_at), (parts,), jnp.float32, least / len(cuts), largest / len(cuts)))
        factor_of = factor_of * jnp.repeat(steps, shape[axis_at] // parts).reshape([-1 if axis == axis_at else 1 for axis in range(len(shape))])
    return factor_of


def noise(key, dims, scale, most, shards=(), held_as=jnp.bfloat16):
    level = block_levels(key, dims, shards, -0.22, 0.18) if shards else 1.0
    drawn = jax.random.normal(key, dims, jnp.float32) * scale * level
    return jnp.minimum(jnp.maximum(drawn, -most), most).astype(held_as)


def setup_inputs(seed: int = 0) -> dict:
    streams_of = jax.random.split(jax.random.key(seed), 17)
    return {
        "final_cotangent": noise(streams_of[0], (G, NLON, NLAT, Z), 1.0, 6.0, ((1, 16), (2, 8)), jnp.float32),
        "saved_start": jnp.clip(jnp.exp(math.log(2.0) - 3.6927934 * jax.random.uniform(streams_of[1], (G, NLON, NLAT, Z), jnp.float32) ** block_levels(streams_of[1], (G, NLON, NLAT, Z), ((1, 16), (2, 8)), -0.2, 0.2)), 0.049804688, 2.0).astype(jnp.bfloat16),
        "saved_middle": jnp.clip(jnp.exp(math.log(2.0) - 3.6927934 * jax.random.uniform(streams_of[2], (G, NLON, NLAT, Z), jnp.float32) ** block_levels(streams_of[2], (G, NLON, NLAT, Z), ((1, 16), (2, 8)), -0.2, 0.2)), 0.049804688, 2.0).astype(jnp.bfloat16),
        "residuals": noise(streams_of[3], (2, ROWS), 1.0, 6.0, ((1, 128),), jnp.float32),
        "row_cells": draw_row_cells(jax.random.fold_in(streams_of[16], 71), 0),
        "row_count": draw_row_count(jax.random.fold_in(streams_of[16], 71), 0),
        "ocean_mask": place_ends((jax.random.randint(streams_of[6], (NLON, NLAT), 0, 5) < 4).astype(jnp.int32), jax.random.fold_in(streams_of[6], 1), 0, 1),
        "cell_eez": place_ends(jax.random.randint(streams_of[7], (NLON, NLAT), 0, EEZS), jax.random.fold_in(streams_of[7], 1), 0, EEZS - 1).astype(jnp.int32),
        "effort": jnp.clip(jnp.exp(jax.random.uniform(streams_of[8], (EEZS,), jnp.float32, math.log(0.1), math.log(2.0))), 0.1, 2.0),
        "kernel": jnp.clip(jnp.exp(jax.random.uniform(streams_of[9], (G, Z, Z), jnp.float32, math.log(0.00038909912), math.log(0.015625))), 0.00038909912, 0.015625).astype(jnp.bfloat16),
        "mix": jnp.clip(jax.random.uniform(streams_of[10], (G, G), jnp.float32, 0.1, 1.0), 0.1, 1.0),
        "assim": jnp.clip(jax.random.uniform(streams_of[11], (G,), jnp.float32, 0.2, 0.8), 0.2, 0.8),
        "mortality": jnp.clip(jnp.exp(jax.random.uniform(streams_of[12], (G, Z), jnp.float32, math.log(0.02), math.log(0.5))), 0.02, 0.5),
        "select": jnp.clip(jnp.exp(jax.random.uniform(streams_of[13], (G, Z), jnp.float32, math.log(0.05), math.log(1.0))), 0.05, 1.0),
        "weight": jnp.clip(jnp.exp(jax.random.uniform(streams_of[14], (Z,), jnp.float32, math.log(0.1), math.log(4.0))), 0.1, 4.0),
        "spread": jnp.clip(jnp.exp(jax.random.uniform(streams_of[15], (Z,), jnp.float32, math.log(0.01), math.log(0.2))), 0.01, 0.2),
    }


step_length = 0.5


def mix_groups(matrix, field):
    total = matrix[:, 0][:, None, None, None] * field[0]
    for source in range(1, field.shape[0]):
        total = total + matrix[:, source][:, None, None, None] * field[source]
    return total


def product(form, left, right):
    return jnp.einsum(form, left.astype(jnp.float32), right.astype(jnp.float32), precision=lax.Precision.HIGHEST)


def move_back(cotan, ocean, spread):
    lat_pad = ((0, 0), (0, 0), (1, 1), (0, 0))
    padded = jnp.pad(cotan, lat_pad)
    ocean_pad = jnp.pad(ocean, lat_pad)
    flux = jnp.roll(ocean, -1, 1) * (jnp.roll(cotan, -1, 1) - cotan) + jnp.roll(ocean, 1, 1) * (jnp.roll(cotan, 1, 1) - cotan)
    flux = flux + ocean_pad[:, :, 2:] * (padded[:, :, 2:] - cotan) + ocean_pad[:, :, :-2] * (padded[:, :, :-2] - cotan)
    return cotan + spread * ocean * flux


def local_adjoint(back, saved, ocean, effort_cell, catch_cot, kernel, mix, assim, mortality, select, weight):
    state = saved.astype(jnp.float32)
    prey = mix_groups(mix, state).astype(jnp.bfloat16)
    encounter = product("gxyz,gwz->gxyw", prey, kernel)
    feed = encounter / (encounter + 1.0)
    eaten = (state * feed).astype(jnp.bfloat16)
    removal = product("gxyw,gwz->gxyz", eaten, kernel)
    loss_rate = mix_groups(mix.T, removal)
    rate = assim[:, None, None, None] * feed - mortality[:, None, None, :] - loss_rate - select[:, None, None, :] * effort_cell
    masked = ocean * back
    grad_rate = step_length * masked * state
    grad_removal = mix_groups(mix, -grad_rate).astype(jnp.bfloat16)
    grad_eaten = product("gxyz,gwz->gxyw", grad_removal, kernel)
    grad_feed = assim[:, None, None, None] * grad_rate + grad_eaten * state
    grad_enc = (grad_feed / ((encounter + 1.0) * (encounter + 1.0))).astype(jnp.bfloat16)
    grad_prey = product("gxyw,gwz->gxyz", grad_enc, kernel)
    catch_gain = (select * weight[None, :])[:, None, None, :]
    grad_state = masked * (1.0 + step_length * rate) + grad_eaten * feed + mix_groups(mix.T, grad_prey)
    grad_state = grad_state + step_length * ocean * effort_cell * catch_gain * catch_cot
    kernel_part = product("gxyw,gxyz->gwz", eaten, grad_removal) + product("gxyw,gxyz->gwz", grad_enc, prey)
    cell_part = -jnp.sum(select[:, None, None, :] * grad_rate, axis=(0, 3), keepdims=True)
    cell_part = cell_part + step_length * ocean * catch_cot * jnp.sum(catch_gain * state, axis=(0, 3), keepdims=True)
    return grad_state, kernel_part, cell_part


def reference(final_cotangent, saved_start, saved_middle, residuals, row_cells, row_count, ocean_mask, cell_eez, effort, kernel, mix, assim, mortality, select, weight, spread):
    ocean = ocean_mask.astype(jnp.float32)[None, :, :, None]
    onehot = cell_eez[:, :, None] == jnp.arange(EEZS, dtype=jnp.int32)[None, None, :]
    effort_cell = jnp.sum(jnp.where(onehot, effort[None, None, :], 0.0), axis=-1)[None, :, :, None]
    valid = jnp.arange(L, dtype=jnp.int32)[None, :] < row_count[:, None]
    values = jnp.where(valid[None], residuals[:, :, None], 0.0)
    catch_cot = jnp.zeros((2, NLON * NLAT), jnp.float32).at[:, row_cells.reshape(-1)].add(values.reshape(2, -1))
    catch_cot = catch_cot.reshape(2, NLON, NLAT)
    starts = jnp.arange(N_LON, dtype=jnp.int32) * CLON
    cotan = final_cotangent
    kernel_total = jnp.zeros((G, Z, Z), jnp.float32)
    effort_total = jnp.zeros((EEZS,), jnp.float32)
    for step, saved in ((1, saved_middle), (0, saved_start)):
        back = move_back(cotan, ocean, spread)
        step_cot = catch_cot[step][None, :, :, None]

        def one_block(start, back=back, saved=saved, step_cot=step_cot):
            def cut(array):
                return lax.dynamic_slice_in_dim(array, start, CLON, 1)
            return local_adjoint(cut(back), cut(saved), cut(ocean), cut(effort_cell), cut(step_cot), kernel, mix, assim, mortality, select, weight)

        grads, kernel_parts, cell_parts = lax.map(one_block, starts)
        cotan = jnp.moveaxis(grads, 0, 1).reshape(G, NLON, NLAT, Z)
        cell_all = jnp.moveaxis(cell_parts, 0, 1).reshape(NLON, NLAT)
        kernel_total = kernel_total + jnp.sum(kernel_parts, axis=0)
        effort_total = effort_total + jnp.sum(jnp.where(onehot, cell_all[:, :, None], 0.0), axis=(0, 1))
    return cotan, kernel_total, effort_total
```

```python
import functools

import jax
import jax.numpy as jnp
from jax import lax
from jax.experimental import pallas as pl
from jax.experimental.pallas import tpu as pltpu
from jax.sharding import Mesh, PartitionSpec as P

G, Z = 4, 256
CI, CJ = 16, 32
N = CI * CJ
EEZS = 64
H = 0.5
SLOTS = 8
F32, BF16 = jnp.float32, jnp.bfloat16
LON, LAT = ("zl", "x", "c"), ("y", "zh")
ALL = LON + LAT
CHIPS = ("zl", "x", "y", "zh")
NCHIP = 64
MIB = 1024 * 1024
HI = lax.Precision.HIGHEST

LON_A = [(i, i ^ 1) for i in range(16)]
LON_B = [(i, (i + 1) % 16 if i % 2 else (i - 1) % 16) for i in range(16)]
LAT_A = [(i, i ^ 1) for i in range(8)]
LAT_B = [(i, i + 1 if i % 2 else i - 1) for i in range(1, 7)]
CORE = [(0, 1), (1, 0)]


def sds(shape, dtype=F32):
    return jax.ShapeDtypeStruct(shape, dtype)


def vm():
    return pl.BlockSpec(memory_space=pltpu.VMEM)


def sm():
    return pl.BlockSpec(memory_space=pltpu.SMEM)


def call(body, outs, ins, scratch=(), flops=0, nbytes=0, vmem=60):
    return pl.pallas_call(
        body,
        out_shape=outs,
        in_specs=ins,
        out_specs=jax.tree.map(lambda _: vm(), outs),
        scratch_shapes=list(scratch),
        compiler_params=pltpu.CompilerParams(vmem_limit_bytes=vmem * MIB),
        cost_estimate=pl.CostEstimate(flops=flops, bytes_accessed=nbytes, transcendentals=0),
    )


def nt(a, b, **kw):
    return lax.dot_general(a, b, (((1,), (1,)), ((), ())), preferred_element_type=F32, **kw)


def nn(a, b, **kw):
    return lax.dot_general(a, b, (((1,), (0,)), ((), ())), preferred_element_type=F32, **kw)


def tn(a, b, **kw):
    return lax.dot_general(a, b, (((0,), (0,)), ((), ())), preferred_element_type=F32, **kw)


def split(x):
    hi = x.astype(BF16).astype(F32)
    return hi, x - hi


def two(x):
    return jnp.concatenate([x, x], axis=1)


def column(row, n, width):
    eye = lax.broadcasted_iota(jnp.int32, (n, n), 0) == lax.broadcasted_iota(jnp.int32, (n, n), 1)
    col = jnp.sum(jnp.where(eye, jnp.broadcast_to(row, (n, n)), 0.0), axis=1, keepdims=True)
    return jnp.broadcast_to(col, (n, width))


def prep_body(c, ocean, cells, count, resid, la, lb, ta, tb, pay):
    par_i, par_j = lax.axis_index("c"), lax.axis_index("zh")
    oc = ocean[...].astype(F32)
    first_i = column(oc[0:1, :], CJ, Z)
    last_i = column(oc[CI - 1 : CI, :], CJ, Z)
    first_j = jnp.broadcast_to(oc[:, 0:1], (CI, Z))
    last_j = jnp.broadcast_to(oc[:, CJ - 1 : CJ], (CI, Z))

    def lon_rims(hi, lo):
        for g in range(G):
            hi[g] = c[g, CI - 1] * last_i
            lo[g] = c[g, 0] * first_i
        hi[G] = last_i
        lo[G] = first_i

    def lat_rims(hi, lo):
        for g in range(G):
            hi[g] = c[g, :, CJ - 1, :] * last_j
            lo[g] = c[g, :, 0, :] * first_j
        hi[G] = last_j
        lo[G] = first_j

    pl.when(par_i == 0)(lambda: lon_rims(la, lb))
    pl.when(par_i == 1)(lambda: lon_rims(lb, la))
    pl.when(par_j == 0)(lambda: lat_rims(ta, tb))
    pl.when(par_j == 1)(lambda: lat_rims(tb, ta))

    rows, ents = cells.shape
    ne = rows * ents
    devices = pay.shape[0]
    tile_e = lax.broadcasted_iota(jnp.int32, (ents, ne), 1) % ents == lax.broadcasted_iota(
        jnp.int32, (ents, ne), 0
    )
    tile_r = lax.broadcasted_iota(jnp.int32, (rows, ne), 1) // ents == lax.broadcasted_iota(
        jnp.int32, (rows, ne), 0
    )
    tile_ef, tile_rf = tile_e.astype(F32), tile_r.astype(F32)
    lon_i = (cells[...] // 256).astype(F32)
    lat_i = (cells[...] % 256).astype(F32)

    def flat(x):
        spread_out = nn(x, tile_ef, precision=HI)
        return jnp.sum(jnp.where(tile_r, spread_out, 0.0), axis=0, keepdims=True)

    i_row = flat(lon_i).astype(jnp.int32)
    j_row = flat(lat_i).astype(jnp.int32)
    n_row = nn(count[...].astype(F32), tile_rf, precision=HI)
    r_row = nn(resid[...], tile_rf, precision=HI)
    entry = (lax.broadcasted_iota(jnp.int32, (1, ne), 1) % ents).astype(F32)
    vals = jnp.where(entry < n_row, r_row, 0.0)
    owner = (i_row // CI) * 8 + j_row // CJ
    mine = lax.broadcasted_iota(jnp.int32, (devices, ne), 0) == owner
    mine_b = mine.astype(F32).astype(BF16)
    before = (
        lax.broadcasted_iota(jnp.int32, (ne, ne), 0) < lax.broadcasted_iota(jnp.int32, (ne, ne), 1)
    )
    ahead = nn(mine_b, before.astype(F32).astype(BF16))
    rank = jnp.sum(jnp.where(mine, ahead, 0.0), axis=0, keepdims=True).astype(jnp.int32)
    slot = lax.broadcasted_iota(jnp.int32, (SLOTS, ne), 0) == rank
    h0, l0 = split(vals[0:1])
    h1, l1 = split(vals[1:2])
    a_row = ((i_row % CI) * CJ).astype(F32)
    b_row = (j_row % CJ).astype(F32)

    def rows_of(parts):
        put = [jnp.where(slot, jnp.broadcast_to(p, (SLOTS, ne)), 0.0) for p in parts]
        put.append(jnp.zeros((128 - SLOTS * len(parts), ne), F32))
        return jnp.concatenate(put, axis=0).astype(BF16)

    pay[...] = nt(mine_b, rows_of((h0, h1, a_row))) + nt(mine_b, rows_of((l0, l1, b_row)))


def catch_body(pay, out, hot, hi, lo):
    got = pay[...]
    flip = got.T
    for k in range(SLOTS):
        where = flip[2 * SLOTS + k : 2 * SLOTS + k + 1, :].astype(jnp.int32)
        cell = lax.broadcasted_iota(jnp.int32, (N, 128), 0)
        hot[:, k * 128 : (k + 1) * 128] = (cell == where).astype(F32).astype(BF16)
        both = jnp.concatenate(
            [
                jnp.broadcast_to(got[:, k : k + 1], (128, 128)),
                jnp.broadcast_to(got[:, SLOTS + k : SLOTS + k + 1], (128, 128)),
            ],
            axis=1,
        )
        top, rest = split(both)
        hi[k * 128 : (k + 1) * 128, :] = top.astype(BF16)
        lo[k * 128 : (k + 1) * 128, :] = rest.astype(BF16)
    out[...] = nn(hot[...], hi[...]) + nn(hot[...], lo[...])


def cells_body(ocean, eez, effort, ocol, ecol, zone):
    oc = ocean[...].astype(F32)
    ez = eez[...].astype(F32)
    lane = lax.broadcasted_iota(jnp.int32, (CJ, 128), 1)
    eff = jnp.concatenate([effort[...], jnp.zeros((1, 128 - EEZS), F32)], axis=1)
    for i in range(CI):
        rows = slice(i * CJ, (i + 1) * CJ)
        ocol[rows] = column(oc[i : i + 1, :], CJ, 128)
        hot = (column(ez[i : i + 1, :], CJ, 128).astype(jnp.int32) == lane).astype(F32)
        zone[rows] = hot
        ecol[rows] = jnp.broadcast_to(jnp.sum(hot * eff, axis=1, keepdims=True), (CJ, 128))


def fwd_body(mix, assim, st, ker, mort, sel, wt, ecol, prey, eaten, feed, gain, gs, tmp):
    step = 16

    @pl.loop(0, N // step)
    def _(n):
        rows = pl.ds(n * step, step)
        s = [st[k, rows, :].astype(F32) for k in range(G)]
        part = None
        for k in range(G):
            term = (sel[k : k + 1, :] * wt[...]) * s[k]
            part = term if part is None else part + term
        gs[rows, :] = part[:, :128] + part[:, 128:]
        for g in range(G):
            tot = mix[g, 0] * s[0]
            for k in range(1, G):
                tot = tot + mix[g, k] * s[k]
            prey[g, rows, :] = tot.astype(BF16)

    for g in range(G):
        tmp[g] = nt(prey[g], ker[g])

    @pl.loop(0, N // step)
    def _(n):
        rows = pl.ds(n * step, step)
        for g in range(G):
            enc = tmp[g, rows, :]
            fd = enc / (enc + 1.0)
            feed[g, rows, :] = fd
            eaten[g, rows, :] = (st[g, rows, :].astype(F32) * fd).astype(BF16)

    for g in range(G):
        tmp[g] = nn(eaten[g], ker[g])

    @pl.loop(0, N // step)
    def _(n):
        rows = pl.ds(n * step, step)
        rem = [tmp[g, rows, :] for g in range(G)]
        ef = two(ecol[rows, :])
        for k in range(G):
            loss = mix[0, k] * rem[0]
            for g in range(1, G):
                loss = loss + mix[g, k] * rem[g]
            rate = assim[k] * feed[k, rows, :] - mort[k : k + 1, :] - loss - sel[k : k + 1, :] * ef
            gain[k, rows, :] = 1.0 + H * rate


def adj_body(last, t, *refs):
    (mix, assim, c, la, lb, ta, tb, ocol, ecol, catch, gs, zone, st, prey, eaten, feed, gain) = refs[:17]
    (ker, sel, wt, spr) = refs[17:21]
    refs = refs[21:]
    if last:
        near, kp_in, eff_in, c_out, keep, send = refs[:6]
        refs = refs[6:]
    else:
        c_out, kp, eff, near, ola, olb, ota, otb = refs[:8]
        opad = refs[8]
        refs = refs[9:]
    pad, m_scr, t_scr, grm, genc, y = refs
    par_i, par_j = lax.axis_index("c"), lax.axis_index("zh")
    at_a = jnp.where(par_i == 0, CI + 1, 0)
    at_b = CI + 1 - at_a
    row_a = jnp.where(par_j == 0, CJ + 8, 7)
    row_b = CJ + 15 - row_a

    for g in range(G):
        pad[g, at_a, 8 : 8 + CJ, :] = la[g]
        pad[g, at_b, 8 : 8 + CJ, :] = lb[g]
        for i in range(CI):
            pad[g, i + 1, pl.ds(row_a, 1), :] = ta[g, i : i + 1, :]
            pad[g, i + 1, pl.ds(row_b, 1), :] = tb[g, i : i + 1, :]
    if not last:
        opad[at_a, 8 : 8 + CJ, :] = la[G, :, :128]
        opad[at_b, 8 : 8 + CJ, :] = lb[G, :, :128]
        for i in range(CI):
            opad[i + 1, pl.ds(row_a, 1), :] = ta[G, i : i + 1, :128]
            opad[i + 1, pl.ds(row_b, 1), :] = tb[G, i : i + 1, :128]

    @pl.loop(0, CI)
    def _(i):
        rows = pl.ds(i * CJ, CJ)
        o = ocol[rows, :]
        if not last:
            opad[i + 1, 8 : 8 + CJ, :] = o
        o2 = two(o)
        for g in range(G):
            pad[g, i + 1, 8 : 8 + CJ, :] = c[g, i] * o2

    @pl.loop(0, CI)
    def _(i):
        rows = pl.ds(i * CJ, CJ)
        o = ocol[rows, :]
        if last:
            s4 = near[rows, :]
        else:
            s4 = (
                opad[i + 2, 8 : 8 + CJ, :]
                + opad[i, 8 : 8 + CJ, :]
                + opad[i + 1, 9 : 9 + CJ, :]
                + opad[i + 1, 7 : 7 + CJ, :]
            )
            near[rows, :] = s4
        acc = jnp.zeros((CJ, 128), F32)
        for z in range(2):
            lanes = slice(z * 128, (z + 1) * 128)
            gr = []
            for g in range(G):
                mid = pad[g, i + 1, 8 : 8 + CJ, lanes]
                around = (
                    pad[g, i + 2, 8 : 8 + CJ, lanes]
                    + pad[g, i, 8 : 8 + CJ, lanes]
                    + pad[g, i + 1, 9 : 9 + CJ, lanes]
                    + pad[g, i + 1, 7 : 7 + CJ, lanes]
                )
                m = mid + spr[:, lanes] * (o * around - s4 * mid)
                m_scr[g, rows, lanes] = m
                r = H * m * st[g, rows, lanes].astype(F32)
                acc = acc + sel[g : g + 1, lanes] * r
                gr.append(r)
            for g in range(G):
                tot = mix[g, 0] * gr[0]
                for k in range(1, G):
                    tot = tot + mix[g, k] * gr[k]
                grm[g, rows, lanes] = (-tot).astype(BF16)
        y[rows, :] = (H * o * catch[rows, t * 128 : (t + 1) * 128]) * gs[rows, :] - acc

    for g in range(G):
        t_scr[g] = nt(grm[g], ker[g])

    @pl.loop(0, CI)
    def _(i):
        rows = pl.ds(i * CJ, CJ)
        q = H * ocol[rows, :] * ecol[rows, :] * catch[rows, t * 128 : (t + 1) * 128]
        for g in range(G):
            for z in range(2):
                lanes = slice(z * 128, (z + 1) * 128)
                s = st[g, rows, lanes].astype(F32)
                m = m_scr[g, rows, lanes]
                ge = t_scr[g, rows, lanes]
                fd = feed[g, rows, lanes]
                inv = 1.0 - fd
                gf = assim[g] * (H * m * s) + ge * s
                genc[g, rows, lanes] = (gf * inv * inv).astype(BF16)
                gw = sel[g : g + 1, lanes] * wt[:, lanes]
                c_out[g, i, :, lanes] = m * gain[g, rows, lanes] + ge * fd + q * gw

    for g in range(G):
        t_scr[g] = nn(genc[g], ker[g])

    @pl.loop(0, CI)
    def _(i):
        rows = pl.ds(i * CJ, CJ)
        for z in range(2):
            lanes = slice(z * 128, (z + 1) * 128)
            gp = [t_scr[g, rows, lanes] for g in range(G)]
            for k in range(G):
                tot = mix[0, k] * gp[0]
                for g in range(1, G):
                    tot = tot + mix[g, k] * gp[g]
                c_out[k, i, :, lanes] = c_out[k, i, :, lanes] + tot

    part = jnp.sum(tn(y[...], zone[...], precision=HI), axis=0, keepdims=True)
    if not last:
        eff[...] = jnp.broadcast_to(part, (8, 128))

        def lon_rims(hi, lo):
            for g in range(G):
                hi[g] = c_out[g, CI - 1] * two(ocol[N - CJ : N, :])
                lo[g] = c_out[g, 0] * two(ocol[0:CJ, :])

        def lat_rims(hi, lo):
            for g in range(G):
                for i in range(CI):
                    hi[g, i : i + 1, :] = c_out[g, i, CJ - 1 : CJ, :] * two(
                        ocol[i * CJ + CJ - 1 : i * CJ + CJ, :]
                    )
                    lo[g, i : i + 1, :] = c_out[g, i, 0:1, :] * two(ocol[i * CJ : i * CJ + 1, :])

        pl.when(par_i == 0)(lambda: lon_rims(ola, olb))
        pl.when(par_i == 1)(lambda: lon_rims(olb, ola))
        pl.when(par_j == 0)(lambda: lat_rims(ota, otb))
        pl.when(par_j == 1)(lambda: lat_rims(otb, ota))
        for g in range(G):
            kp[g] = tn(eaten[g], grm[g]) + tn(genc[g], prey[g])
    else:
        both = eff_in[...] + part
        for dst, half in ((send, 1 - par_i), (keep, par_i)):
            dst[2 * Z :, :] = two(both)
            for s in range(2):
                g = 2 * half + s
                dst[s * Z : (s + 1) * Z, :] = kp_in[g] + tn(eaten[g], grm[g]) + tn(genc[g], prey[g])


CH = 17


def merge_body(keep, got, out):
    eff = keep[2 * Z : 2 * Z + 1, :128] + got[2 * Z : 2 * Z + 1, :128]
    for p in range(NCHIP):
        rows = slice(p * 8, p * 8 + 8)
        tot = keep[rows, :] + got[rows, :]
        out[p * CH : p * CH + 8, :] = tot[:, :128]
        out[p * CH + 8 : p * CH + 16, :] = tot[:, 128:]
        out[p * CH + 16 : p * CH + 17, :] = eff


def sum_body(parts, out, eff):
    tot = [None, None, None]
    for p in range(NCHIP):
        new = (
            parts[p * CH : p * CH + 8, :],
            parts[p * CH + 8 : p * CH + 16, :],
            parts[p * CH + 16 : p * CH + 17, :],
        )
        tot = [n if o is None else o + n for o, n in zip(tot, new)]
    both = jnp.concatenate(tot[:2], axis=1)
    eff[...] = tot[2]
    for p in range(NCHIP):
        out[p] = both


def join_body(own, got, out):
    core = lax.axis_index("c")
    for s in range(2):
        out[2 * core + s] = own[s * Z : (s + 1) * Z, :]
        out[2 * (1 - core) + s] = got[s * Z : (s + 1) * Z, :]


def exchange(la, lb, ta, tb):
    return (
        lax.ppermute(la, LON, LON_A),
        lax.ppermute(lb, LON, LON_B),
        lax.ppermute(ta, LAT, LAT_A),
        lax.ppermute(tb, LAT, LAT_B),
    )


def body(
    final_cotangent,
    saved_start,
    saved_middle,
    residuals,
    row_cells,
    row_count,
    ocean_mask,
    cell_eez,
    effort,
    kernel,
    mix,
    assim,
    mortality,
    select,
    weight,
    spread,
):
    devices = 128
    wt, spr = weight.reshape(1, Z), spread.reshape(1, Z)
    rims = [sds((G + 1, CJ, Z))] * 2 + [sds((G + 1, CI, Z))] * 2
    *rim, pay = call(
        prep_body, rims + [sds((devices, 128))], [vm()] * 5, flops=2**27, nbytes=3 * MIB
    )(final_cotangent, ocean_mask, row_cells, row_count.reshape(1, -1), residuals)
    rim = exchange(*rim)
    pay = lax.all_to_all(pay, ALL, 0, 0, tiled=True)

    ocol, ecol, zone = call(cells_body, [sds((N, 128))] * 3, [vm()] * 3, nbytes=MIB)(
        ocean_mask, cell_eez, effort.reshape(1, EEZS)
    )
    fwd = call(
        fwd_body,
        [sds((G, N, Z), BF16)] * 2 + [sds((G, N, Z))] * 2 + [sds((N, 128))],
        [sm(), sm()] + [vm()] * 6,
        [pltpu.VMEM((G, N, Z), F32)],
        flops=2**29,
        nbytes=8 * MIB,
    )
    states, parts = [], []
    for saved in (saved_start, saved_middle):
        st = saved.reshape(G, N, Z)
        states.append(st)
        parts.append(fwd(mix, assim, st, kernel, mortality, select, wt, ecol))
    catch = call(
        catch_body,
        sds((N, 256)),
        [vm()],
        [
            pltpu.VMEM((N, SLOTS * 128), BF16),
            pltpu.VMEM((SLOTS * 128, 256), BF16),
            pltpu.VMEM((SLOTS * 128, 256), BF16),
        ],
        flops=2**29,
        nbytes=MIB,
    )(pay)

    big = [
        pltpu.VMEM((G, CI + 2, CJ + 16, Z), F32),
        pltpu.VMEM((G, N, Z), F32),
        pltpu.VMEM((G, N, Z), F32),
        pltpu.VMEM((G, N, Z), BF16),
        pltpu.VMEM((G, N, Z), BF16),
        pltpu.VMEM((N, 128), F32),
    ]

    def operands(t, cot, rim):
        prey, eaten, feed, gain, gs = parts[t]
        return (mix, assim, cot, *rim, ocol, ecol, catch, gs, zone, states[t], prey, eaten, feed, gain) + (
            kernel,
            select,
            wt,
            spr,
        )

    cot, kp, eff, near, *rim = call(
        functools.partial(adj_body, False, 1),
        [sds((G, CI, CJ, Z)), sds((G, Z, Z)), sds((8, 128)), sds((N, 128))]
        + [sds((G, CJ, Z))] * 2
        + [sds((G, CI, Z))] * 2,
        [sm(), sm()] + [vm()] * 19,
        [pltpu.VMEM((CI + 2, CJ + 16, 128), F32)] + big,
        flops=2**30,
        nbytes=16 * MIB,
    )(*operands(1, final_cotangent, rim))
    rim = exchange(*rim)
    cot, keep, send = call(
        functools.partial(adj_body, True, 0),
        [sds((G, CI, CJ, Z)), sds((2 * Z + 8, Z)), sds((2 * Z + 8, Z))],
        [sm(), sm()] + [vm()] * 22,
        big,
        flops=2**30,
        nbytes=16 * MIB,
    )(*operands(0, cot, rim), near, kp, eff)

    got = lax.ppermute(send, "c", CORE)
    chunks = call(merge_body, sds((NCHIP * CH, 128)), [vm()] * 2, nbytes=2 * MIB)(keep, got)
    chunks = lax.all_to_all(chunks, CHIPS, 0, 0, tiled=True)
    own, eff = call(sum_body, [sds((NCHIP, 8, Z)), sds((1, 128))], [vm()], nbytes=MIB)(chunks)
    own = lax.all_to_all(own, CHIPS, 0, 0, tiled=True).reshape(2 * Z, Z)
    got = lax.ppermute(own, "c", CORE)
    total = call(join_body, sds((G, Z, Z)), [vm()] * 2, nbytes=2 * MIB)(own, got)
    return cot, total, eff[0, :EEZS]


def solution(mesh):
    fine = Mesh(mesh.devices.reshape(2, 4, 2, 4, 2), ("zl", "x", "c", "y", "zh"))
    field = P(None, LON, LAT, None)
    placed = (
        field,
        field,
        field,
        P(None, ALL),
        P(ALL, None),
        P(ALL),
        P(LON, LAT),
        P(LON, LAT),
    ) + (P(),) * 8
    return jax.shard_map(
        body,
        mesh=fine,
        in_specs=placed,
        out_specs=(field, P(), P()),
        check_vma=False,
    )
```

```python
import functools

import jax
import jax.numpy as jnp
from jax import lax
from jax.experimental import pallas as pl
from jax.experimental.pallas import tpu as pltpu
from jax.sharding import Mesh, PartitionSpec as P

G, Z = 4, 256
CI, CJ = 16, 32
N = CI * CJ
EEZS = 64
H = 0.5
SLOTS = 8
F32, BF16 = jnp.float32, jnp.bfloat16
LON, LAT = ("zl", "x", "c"), ("y", "zh")
ALL = LON + LAT
CHIPS = ("zl", "x", "y", "zh")
NCHIP = 64
MIB = 1024 * 1024
HI = lax.Precision.HIGHEST

LON_A = [(i, i ^ 1) for i in range(16)]
LON_B = [(i, (i + 1) % 16 if i % 2 else (i - 1) % 16) for i in range(16)]
LAT_A = [(i, i ^ 1) for i in range(8)]
LAT_B = [(i, i + 1 if i % 2 else i - 1) for i in range(1, 7)]
CORE = [(0, 1), (1, 0)]


def sds(shape, dtype=F32):
    return jax.ShapeDtypeStruct(shape, dtype)


def vmem(shape, dtype=F32):
    return pltpu.VMEM(shape, dtype)


def vm():
    return pl.BlockSpec(memory_space=pltpu.VMEM)


def sm():
    return pl.BlockSpec(memory_space=pltpu.SMEM)


def call(body, outs, ins, scratch=(), flops=0, nbytes=0, vmem=6, place=True, far=(), out_far=0):
    many = isinstance(outs, list)
    spots = [pl.BlockSpec(memory_space=pl.ANY) if n < out_far else vm() for n in range(len(outs) if many else 1)]
    run = pl.pallas_call(
        body,
        out_shape=outs,
        in_specs=ins,
        out_specs=spots if many else vm(),
        scratch_shapes=list(scratch),
        compiler_params=pltpu.CompilerParams(vmem_limit_bytes=vmem * MIB),
        cost_estimate=pl.CostEstimate(flops=flops, bytes_accessed=nbytes, transcendentals=0),
    )

    def go(*args):
        return run(
            *[
                in_hbm(a) if not place or n in far else near_core(a) if a.size >= 8192 else a
                for n, a in enumerate(args)
            ]
        )

    return go


def near_core(x):
    return pltpu.with_memory_space_constraint(x, pltpu.VMEM)


def in_hbm(x):
    return pltpu.with_memory_space_constraint(x, pltpu.HBM)


def nt(a, b, **kw):
    return lax.dot_general(a, b, (((1,), (1,)), ((), ())), preferred_element_type=F32, **kw)


def nn(a, b, **kw):
    return lax.dot_general(a, b, (((1,), (0,)), ((), ())), preferred_element_type=F32, **kw)


def tn(a, b, **kw):
    return lax.dot_general(a, b, (((0,), (0,)), ((), ())), preferred_element_type=F32, **kw)


def split(x):
    hi = x.astype(BF16).astype(F32)
    return hi, x - hi


def two(x):
    return jnp.concatenate([x, x], axis=1)


def column(row, n, width):
    eye = lax.broadcasted_iota(jnp.int32, (n, n), 0) == lax.broadcasted_iota(jnp.int32, (n, n), 1)
    col = jnp.sum(jnp.where(eye, jnp.broadcast_to(row, (n, n)), 0.0), axis=1, keepdims=True)
    return jnp.broadcast_to(col, (n, width))


def prep_body(c, ocean, cells, count, resid, la, lb, ta, tb, pay, rim_i, rim_j, sem):
    par_i, par_j = lax.axis_index("c"), lax.axis_index("zh")
    copies = [
        pltpu.make_async_copy(c.at[:, CI - 1], rim_i.at[0], sem.at[0]),
        pltpu.make_async_copy(c.at[:, 0], rim_i.at[1], sem.at[1]),
        pltpu.make_async_copy(c.at[:, :, CJ - 8 : CJ, :], rim_j.at[0], sem.at[2]),
        pltpu.make_async_copy(c.at[:, :, 0:8, :], rim_j.at[1], sem.at[3]),
    ]
    for copy in copies:
        copy.start()

    ents, rows = cells.shape
    ne = rows * ents
    devices = pay.shape[0]
    tile_e = lax.broadcasted_iota(jnp.int32, (ents, ne), 1) // rows == lax.broadcasted_iota(
        jnp.int32, (ents, ne), 0
    )
    tile_r = lax.broadcasted_iota(jnp.int32, (rows, ne), 1) % rows == lax.broadcasted_iota(
        jnp.int32, (rows, ne), 0
    )
    tile_rf = tile_r.astype(F32)
    lon_i = (cells[...] // 256).astype(F32)
    lat_i = (cells[...] % 256).astype(F32)

    def flat(x):
        spread_out = nn(x, tile_rf, precision=HI)
        return jnp.sum(jnp.where(tile_e, spread_out, 0.0), axis=0, keepdims=True)

    i_row = flat(lon_i).astype(jnp.int32)
    j_row = flat(lat_i).astype(jnp.int32)
    n_row = nn(count[...].astype(F32), tile_rf, precision=HI)
    r_row = nn(resid[...], tile_rf, precision=HI)
    entry = (lax.broadcasted_iota(jnp.int32, (1, ne), 1) // rows).astype(F32)
    vals = jnp.where(entry < n_row, r_row, 0.0)
    owner = (i_row // CI) * 8 + j_row // CJ
    mine = lax.broadcasted_iota(jnp.int32, (devices, ne), 0) == owner
    mine_b = mine.astype(F32).astype(BF16)
    before = (
        lax.broadcasted_iota(jnp.int32, (ne, ne), 0) < lax.broadcasted_iota(jnp.int32, (ne, ne), 1)
    )
    ahead = nn(mine_b, before.astype(F32).astype(BF16))
    rank = jnp.sum(jnp.where(mine, ahead, 0.0), axis=0, keepdims=True).astype(jnp.int32)
    slot = lax.broadcasted_iota(jnp.int32, (SLOTS, ne), 0) == rank
    h0, l0 = split(vals[0:1])
    h1, l1 = split(vals[1:2])
    a_row = ((i_row % CI) * CJ).astype(F32)
    b_row = (j_row % CJ).astype(F32)

    def rows_of(parts):
        put = [jnp.where(slot, jnp.broadcast_to(p, (SLOTS, ne)), 0.0) for p in parts]
        put.append(jnp.zeros((128 - SLOTS * len(parts), ne), F32))
        return jnp.concatenate(put, axis=0).astype(BF16)

    pay[...] = nt(mine_b, rows_of((h0, h1, a_row))) + nt(mine_b, rows_of((l0, l1, b_row)))

    oc = ocean[...].astype(F32)
    edge_i = (column(oc[CI - 1 : CI, :], CJ, Z), column(oc[0:1, :], CJ, Z))
    edge_j = (
        jnp.broadcast_to(oc[:, CJ - 1 : CJ], (CI, Z)),
        jnp.broadcast_to(oc[:, 0:1], (CI, Z)),
    )
    for copy in copies:
        copy.wait()

    def rims(odd, a, b, value):
        for n, (even_to, odd_to) in enumerate(((a, b), (b, a))):
            for g in range(G + 1):
                v = value(n, g)

                @pl.when(odd == 0)
                def _():
                    even_to[g] = v

                @pl.when(odd == 1)
                def _():
                    odd_to[g] = v

    rims(par_i, la, lb, lambda n, g: edge_i[n] if g == G else rim_i[n, g] * edge_i[n])
    rims(
        par_j,
        ta,
        tb,
        lambda n, g: edge_j[n] if g == G else rim_j[n, g, :, 7 if n == 0 else 0, :] * edge_j[n],
    )


def cells_body(ocean, eez, effort, pay, ker, ocol, ecol, zone, out, flipped, hot, hi, lo):
    for g in range(G):
        flipped[g] = ker[g].T
    oc = ocean[...].astype(F32)
    ez = eez[...].astype(F32)
    lane = lax.broadcasted_iota(jnp.int32, (CJ, 128), 1)
    eff = jnp.concatenate([effort[...], jnp.zeros((1, 128 - EEZS), F32)], axis=1)
    for i in range(CI):
        rows = slice(i * CJ, (i + 1) * CJ)
        ocol[rows] = column(oc[i : i + 1, :], CJ, 128)
        here = (column(ez[i : i + 1, :], CJ, 128).astype(jnp.int32) == lane).astype(F32)
        zone[rows] = here
        ecol[rows] = jnp.broadcast_to(jnp.sum(here * eff, axis=1, keepdims=True), (CJ, 128))

    got = pay[...]
    flip = got.T
    for k in range(SLOTS):
        where = flip[2 * SLOTS + k : 2 * SLOTS + k + 1, :].astype(jnp.int32)
        cell = lax.broadcasted_iota(jnp.int32, (N, 128), 0)
        hot[:, k * 128 : (k + 1) * 128] = (cell == where).astype(F32).astype(BF16)
        both = jnp.concatenate(
            [
                jnp.broadcast_to(got[:, k : k + 1], (128, 128)),
                jnp.broadcast_to(got[:, SLOTS + k : SLOTS + k + 1], (128, 128)),
            ],
            axis=1,
        )
        top, rest = split(both)
        hi[k * 128 : (k + 1) * 128, :] = top.astype(BF16)
        lo[k * 128 : (k + 1) * 128, :] = rest.astype(BF16)
    out[...] = nn(hot[...], hi[...]) + nn(hot[...], lo[...])


R = 128
CHUNKS = N // R


def recip(d):
    r = pltpu.reciprocal(d, approx=True)
    return r * (2.0 - d * r)


def mixed(rows_of, mix, k, turned=False):
    tot = None
    for g in range(G):
        term = (mix[g, k] if turned else mix[k, g]) * rows_of[g]
        tot = term if tot is None else tot + term
    return tot


def gain_of(k, mix, assim, mort, sel, ef, feed, rem):
    tot = (1.0 - H * mort[k : k + 1, :]) - (H * sel[k : k + 1, :]) * ef + (H * assim[k]) * feed
    for g in range(G):
        tot = tot + (-H * mix[g, k]) * rem[g]
    return tot


def fwd_body(full, *refs):
    if full:
        mix, assim, saved, ker, turn, mort, sel, wt, ecol, st, prey, eaten, feed, gs, gain, rem, sem = refs
    else:
        mix, assim, saved, ker, turn, mort, sel, wt, ecol, st, prey, eaten, feed, gs, sem = refs
    copies = []
    for n in range(CHUNKS):
        rows = slice(n * R, (n + 1) * R)
        copies.append(pltpu.make_async_copy(saved.at[:, rows, :], st.at[:, rows, :], sem.at[n]))
        copies[-1].start()
    for n in range(CHUNKS):
        rows = slice(n * R, (n + 1) * R)
        copies[n].wait()
        s = [st[k, rows, :].astype(F32) for k in range(G)]
        part = None
        for k in range(G):
            term = (sel[k : k + 1, :] * wt[...]) * s[k]
            part = term if part is None else part + term
        gs[rows, :] = part[:, :128] + part[:, 128:]
        for g in range(G):
            prey[g, rows, :] = mixed(s, mix, g).astype(BF16)
        for g in range(G):
            enc = nn(prey[g, rows, :], turn[g])
            fd = enc * recip(enc + 1.0)
            feed[g, rows, :] = fd
            eaten[g, rows, :] = (st[g, rows, :].astype(F32) * fd).astype(BF16)
        if full:
            for g in range(G):
                rem[g, rows, :] = nn(eaten[g, rows, :], ker[g])
            parts = [rem[g, rows, :] for g in range(G)]
            ef = two(ecol[rows, :])
            for k in range(G):
                gain[k, rows, :] = gain_of(k, mix, assim, mort, sel, ef, feed[k, rows, :], parts)


def fill(pad, opad, c, la, lb, ta, tb, ocol):
    par_i, par_j = lax.axis_index("c"), lax.axis_index("zh")
    at_a = jnp.where(par_i == 0, CI + 1, 0)
    at_b = CI + 1 - at_a
    row_a = jnp.where(par_j == 0, CJ + 8, 7)
    row_b = CJ + 15 - row_a
    for g in range(G):
        pad[g, at_a, 8 : 8 + CJ, :] = la[g]
        pad[g, at_b, 8 : 8 + CJ, :] = lb[g]
        for i in range(CI):
            pad[g, i + 1, pl.ds(row_a, 1), :] = ta[g, i : i + 1, :]
            pad[g, i + 1, pl.ds(row_b, 1), :] = tb[g, i : i + 1, :]
    if opad is not None:
        opad[at_a, 8 : 8 + CJ, :] = la[G, :, :128]
        opad[at_b, 8 : 8 + CJ, :] = lb[G, :, :128]
        for i in range(CI):
            opad[i + 1, pl.ds(row_a, 1), :] = ta[G, i : i + 1, :128]
            opad[i + 1, pl.ds(row_b, 1), :] = tb[G, i : i + 1, :128]
    for i in range(CI):
        o = ocol[i * CJ : (i + 1) * CJ, :]
        if opad is not None:
            opad[i + 1, 8 : 8 + CJ, :] = o
        for g in range(G):
            pad[g, i + 1, 8 : 8 + CJ, :] = c[g, i] * two(o)


def around(pad, i, lanes):
    return (pad[i + 2, 8 : 8 + CJ, lanes] + pad[i, 8 : 8 + CJ, lanes]) + (
        pad[i + 1, 9 : 9 + CJ, lanes] + pad[i + 1, 7 : 7 + CJ, lanes]
    )


def spread_row(i, t, pad, s4, mix, ocol, catch, gs, st, sel, spr, m_out, grm, y):
    rows = slice(i * CJ, (i + 1) * CJ)
    o = ocol[rows, :]
    acc = None
    for z in range(2):
        lanes = slice(z * 128, (z + 1) * 128)
        ms = []
        for g in range(G):
            mid = pad[g, i + 1, 8 : 8 + CJ, lanes]
            m = mid + spr[:, lanes] * (o * around(pad.at[g], i, lanes) - s4 * mid)
            m_out[g, rows, lanes] = m
            ms.append(m * st[g, rows, lanes].astype(F32))
            term = sel[g : g + 1, lanes] * ms[-1]
            acc = term if acc is None else acc + term
        for g in range(G):
            tot = None
            for k in range(G):
                term = (-H * mix[g, k]) * ms[k]
                tot = term if tot is None else tot + term
            grm[g, rows, lanes] = tot.astype(BF16)
    y[rows, :] = H * ((o * catch[rows, t * 128 : (t + 1) * 128]) * gs[rows, :] - acc)


def enc_grad(g, assim, m, s, ge, fd):
    inv = 1.0 - fd
    return (((H * assim[g]) * (m * s) + ge * s) * (inv * inv)).astype(BF16)


def adj_body(*refs):
    mix, assim, c, la, lb, ta, tb, ocol, ecol, catch, gs, zone, st, feed, gain, ker, turn, sel, wt, spr = refs[:20]
    c_out, grm, genc, eff, near, ola, olb, ota, otb, opad, pad, m_scr, t_scr, y = refs[20:]
    par_i, par_j = lax.axis_index("c"), lax.axis_index("zh")
    fill(pad, opad, c, la, lb, ta, tb, ocol)
    for n in range(CHUNKS):
        rows = slice(n * R, (n + 1) * R)
        for i in range(n * R // CJ, (n + 1) * R // CJ):
            s4 = around(opad, i, slice(None))
            near[i * CJ : (i + 1) * CJ, :] = s4
            spread_row(i, 1, pad, s4, mix, ocol, catch, gs, st, sel, spr, m_scr, grm, y)
        q = two(H * ocol[rows, :] * ecol[rows, :] * catch[rows, 128:])
        for g in range(G):
            ge = nn(grm[g, rows, :], turn[g])
            m, fd = m_scr[g, rows, :], feed[g, rows, :]
            genc[g, rows, :] = enc_grad(g, assim, m, st[g, rows, :].astype(F32), ge, fd)
            m_scr[g, rows, :] = m * gain[g, rows, :] + ge * fd + q * (sel[g : g + 1, :] * wt[...])
        for g in range(G):
            t_scr[g, rows, :] = nn(genc[g, rows, :], ker[g])
        for i in range(n * R // CJ, (n + 1) * R // CJ):
            here = slice(i * CJ, (i + 1) * CJ)
            gp = [t_scr[g, here, :] for g in range(G)]
            for k in range(G):
                c_out[k, i] = m_scr[k, here, :] + mixed(gp, mix, k, True)
    part = jnp.sum(tn(y[...], zone[...], precision=HI), axis=0, keepdims=True)
    eff[...] = jnp.broadcast_to(part, (8, 128))

    def lon_rims(hi, lo):
        for g in range(G):
            hi[g] = c_out[g, CI - 1] * two(ocol[N - CJ : N, :])
            lo[g] = c_out[g, 0] * two(ocol[0:CJ, :])

    def lat_rims(hi, lo):
        for g in range(G):
            for i in range(CI):
                at = i * CJ
                hi[g, i : i + 1, :] = c_out[g, i, CJ - 1 : CJ, :] * two(ocol[at + CJ - 1 : at + CJ, :])
                lo[g, i : i + 1, :] = c_out[g, i, 0:1, :] * two(ocol[at : at + 1, :])

    pl.when(par_i == 0)(lambda: lon_rims(ola, olb))
    pl.when(par_i == 1)(lambda: lon_rims(olb, ola))
    pl.when(par_j == 0)(lambda: lat_rims(ota, otb))
    pl.when(par_j == 1)(lambda: lat_rims(otb, ota))


def part_body(eaten, grm, genc, prey, kp):
    for g in range(G):
        kp[g] = tn(eaten[g], grm[g]) + tn(genc[g], prey[g])


def last_body(*refs):
    mix, assim, c, la, lb, ta, tb, ocol, ecol, catch, gs, zone, st, prey, eaten, feed, turn, sel, spr, near, kp, eff = refs[:22]
    m_hbm, ge_hbm, q_hbm, e_hbm, keep, send, pad, m_scr, ge_scr, grm, genc, y, q_scr, sem = refs[22:]
    core = lax.axis_index("c")
    fill(pad, None, c, la, lb, ta, tb, ocol)
    q_scr[...] = H * ocol[...] * ecol[...] * catch[:, :128]
    copies = [
        pltpu.make_async_copy(q_scr, q_hbm, sem.at[0]),
        pltpu.make_async_copy(ecol, e_hbm, sem.at[1]),
    ]
    for copy in copies:
        copy.start()
    for n in range(CHUNKS):
        rows = slice(n * R, (n + 1) * R)
        for i in range(n * R // CJ, (n + 1) * R // CJ):
            s4 = near[i * CJ : (i + 1) * CJ, :]
            spread_row(i, 0, pad, s4, mix, ocol, catch, gs, st, sel, spr, m_scr, grm, y)
        for g in range(G):
            ge = nn(grm[g, rows, :], turn[g])
            ge_scr[g, rows, :] = ge
            genc[g, rows, :] = enc_grad(
                g, assim, m_scr[g, rows, :], st[g, rows, :].astype(F32), ge, feed[g, rows, :]
            )
        for k, (src, dst) in enumerate(((m_scr, m_hbm), (ge_scr, ge_hbm))):
            copies.append(
                pltpu.make_async_copy(src.at[:, rows, :], dst.at[:, rows, :], sem.at[2 + 2 * n + k])
            )
            copies[-1].start()
    part = jnp.sum(tn(y[...], zone[...], precision=HI), axis=0, keepdims=True)
    both = two(eff[...] + part)
    for dst, half in ((send, 1 - core), (keep, core)):
        dst[2 * Z :, :] = both
        for s in range(2):
            g = 2 * half + s
            dst[s * Z : (s + 1) * Z, :] = kp[g] + tn(eaten[g], grm[g]) + tn(genc[g], prey[g])
    for copy in copies:
        copy.wait()


def rest_body(mix, assim, saved, m_in, ge_in, q_in, ecol, ker, mort, sel, wt, out, feed, rem, turn):
    @pl.when(pl.program_id(0) == 0)
    def _():
        for g in range(G):
            turn[g] = ker[g].T

    s = [saved[k].astype(F32) for k in range(G)]
    for g in range(G):
        enc = nn(mixed(s, mix, g).astype(BF16), turn[g])
        fd = enc * recip(enc + 1.0)
        feed[g] = fd
        rem[g] = nn((s[g] * fd).astype(BF16), ker[g])
    parts = [rem[g] for g in range(G)]
    ef, q = two(ecol[...]), two(q_in[...])
    for k in range(G):
        fd = feed[k]
        gain = gain_of(k, mix, assim, mort, sel, ef, fd, parts)
        out[k] = m_in[k] * gain + ge_in[k] * fd + q * (sel[k : k + 1, :] * wt[...])
    for g in range(G):
        rem[g] = nn(enc_grad(g, assim, m_in[g], saved[g].astype(F32), ge_in[g], feed[g]), ker[g])
    parts = [rem[g] for g in range(G)]
    for k in range(G):
        out[k] = out[k] + mixed(parts, mix, k, True)


CH = 17


def merge_body(keep, got, out):
    eff = keep[2 * Z : 2 * Z + 1, :128] + got[2 * Z : 2 * Z + 1, :128]
    for p in range(NCHIP):
        rows = slice(p * 8, p * 8 + 8)
        tot = keep[rows, :] + got[rows, :]
        out[p * CH : p * CH + 8, :] = tot[:, :128]
        out[p * CH + 8 : p * CH + 16, :] = tot[:, 128:]
        out[p * CH + 16 : p * CH + 17, :] = eff


def sum_body(parts, out, eff):
    tot = [None, None, None]
    for p in range(NCHIP):
        new = (
            parts[p * CH : p * CH + 8, :],
            parts[p * CH + 8 : p * CH + 16, :],
            parts[p * CH + 16 : p * CH + 17, :],
        )
        tot = [n if o is None else o + n for o, n in zip(tot, new)]
    both = jnp.concatenate(tot[:2], axis=1)
    eff[...] = tot[2]
    for p in range(NCHIP):
        out[p] = both


def join_body(own, got, out):
    core = lax.axis_index("c")
    for s in range(2):
        out[2 * core + s] = own[s * Z : (s + 1) * Z, :]
        out[2 * (1 - core) + s] = got[s * Z : (s + 1) * Z, :]


def exchange(la, lb, ta, tb):
    return (
        lax.ppermute(la, LON, LON_A),
        lax.ppermute(lb, LON, LON_B),
        lax.ppermute(ta, LAT, LAT_A),
        lax.ppermute(tb, LAT, LAT_B),
    )


def body(
    final_cotangent,
    saved_start,
    saved_middle,
    residuals,
    row_cells,
    row_count,
    ocean_mask,
    cell_eez,
    effort,
    kernel,
    mix,
    assim,
    mortality,
    select,
    weight,
    spread,
):
    devices = 128
    wt, spr = weight.reshape(1, Z), spread.reshape(1, Z)
    any_ = pl.BlockSpec(memory_space=pl.ANY)
    field = (G, N, Z)
    rims = [vmem((G + 1, CJ, Z))] * 2 + [vmem((G + 1, CI, Z))] * 2
    *rim, pay = call(
        prep_body,
        rims + [vmem((devices, 128))],
        [any_] + [vm()] * 4,
        [
            pltpu.VMEM((2, G, CJ, Z), F32),
            pltpu.VMEM((2, G, CI, 8, Z), F32),
            pltpu.SemaphoreType.DMA((4,)),
        ],
        flops=2**27,
        nbytes=3 * MIB,
        place=False,
    )(final_cotangent, ocean_mask, row_cells.T, row_count.reshape(1, -1), residuals)
    rim = exchange(*rim)
    pay = lax.all_to_all(pay, ALL, 0, 0, tiled=True)

    ocol, ecol, zone, catch, turn = call(
        cells_body,
        [vmem((N, 128))] * 3 + [vmem((N, 256)), vmem((G, Z, Z), BF16)],
        [vm()] * 5,
        [
            pltpu.VMEM((N, SLOTS * 128), BF16),
            pltpu.VMEM((SLOTS * 128, 256), BF16),
            pltpu.VMEM((SLOTS * 128, 256), BF16),
        ],
        flops=2**29,
        nbytes=MIB,
    )(ocean_mask, cell_eez, effort.reshape(1, EEZS), pay, kernel)

    def forward(saved, full):
        return call(
            functools.partial(fwd_body, full),
            [vmem(field, BF16)] * 3 + [vmem(field), vmem((N, 128))] + [vmem(field)] * full,
            [sm(), sm(), any_] + [vm()] * 6,
            [pltpu.VMEM(field, F32)] * full + [pltpu.SemaphoreType.DMA((CHUNKS,))],
            flops=2**29,
            nbytes=8 * MIB,
            vmem=8,
            far=(2,),
        )(mix, assim, saved.reshape(field), kernel, turn, mortality, select, wt, ecol)

    st, prey, eaten, feed, gs, gain = forward(saved_middle, True)
    pads = pltpu.VMEM((G, CI + 2, CJ + 16, Z), F32)
    cot, grm, genc, eff, near, *rim = call(
        adj_body,
        [vmem((G, CI, CJ, Z))]
        + [vmem(field, BF16)] * 2
        + [vmem((8, 128)), vmem((N, 128))]
        + [vmem((G, CJ, Z))] * 2
        + [vmem((G, CI, Z))] * 2,
        [sm(), sm()] + [vm()] * 18,
        [pltpu.VMEM((CI + 2, CJ + 16, 128), F32), pads]
        + [pltpu.VMEM(field, F32)] * 2
        + [pltpu.VMEM((N, 128), F32)],
        flops=2**30,
        nbytes=16 * MIB,
        vmem=16,
    )(
        *(mix, assim, final_cotangent, *rim, ocol, ecol, catch, gs, zone, st, feed, gain),
        *(kernel, turn, select, wt, spr),
    )
    rim = exchange(*rim)
    kp = call(part_body, vmem((G, Z, Z)), [vm()] * 4, flops=2**29, nbytes=5 * MIB)(
        eaten, grm, genc, prey
    )
    st, prey, eaten, feed, gs = forward(saved_start, False)
    m, ge, q, ef, keep, send = call(
        last_body,
        [pltpu.HBM(field, F32)] * 2 + [pltpu.HBM((N, 128), F32)] * 2 + [vmem((2 * Z + 8, Z))] * 2,
        [sm(), sm()] + [vm()] * 20,
        [pads]
        + [pltpu.VMEM(field, F32)] * 2
        + [pltpu.VMEM(field, BF16)] * 2
        + [pltpu.VMEM((N, 128), F32)] * 2
        + [pltpu.SemaphoreType.DMA((2 + 2 * CHUNKS,))],
        flops=2**30,
        nbytes=16 * MIB,
        vmem=16,
        out_far=4,
    )(
        *(mix, assim, cot, *rim, ocol, ecol, catch, gs, zone, st, prey, eaten, feed),
        *(turn, select, spr, near, kp, eff),
    )
    block = pl.BlockSpec((G, R, Z), lambda n: (0, n, 0))
    cells = pl.BlockSpec((R, 128), lambda n: (n, 0))
    whole = pl.BlockSpec((G, Z), lambda n: (0, 0))
    cot = pl.pallas_call(
        rest_body,
        grid=(CHUNKS,),
        out_shape=sds(field),
        in_specs=[sm(), sm(), block, block, block, cells, cells]
        + [pl.BlockSpec((G, Z, Z), lambda n: (0, 0, 0)), whole, whole]
        + [pl.BlockSpec((1, Z), lambda n: (0, 0))],
        out_specs=block,
        scratch_shapes=[pltpu.VMEM((G, R, Z), F32)] * 2 + [pltpu.VMEM((G, Z, Z), BF16)],
        compiler_params=pltpu.CompilerParams(vmem_limit_bytes=16 * MIB),
        cost_estimate=pl.CostEstimate(flops=2**30, bytes_accessed=12 * MIB, transcendentals=0),
    )(mix, assim, *map(in_hbm, (saved_start.reshape(field), m, ge, q, ef, kernel)), mortality, select, wt)
    cot = cot.reshape(G, CI, CJ, Z)

    got = lax.ppermute(send, "c", CORE)
    chunks = call(merge_body, vmem((NCHIP * CH, 128)), [vm()] * 2, nbytes=2 * MIB)(keep, got)
    chunks = lax.all_to_all(chunks.reshape(NCHIP, 1, CH * 128), CHIPS, 0, 0, tiled=True)
    chunks = chunks.reshape(NCHIP * CH, 128)
    own, eff = call(sum_body, [vmem((NCHIP, 8, Z)), vmem((1, 128))], [vm()], nbytes=MIB)(chunks)
    own, cot = lax.optimization_barrier((own, cot))
    own = lax.all_to_all(own, CHIPS, 0, 0, tiled=True).reshape(2 * Z, Z)
    got = lax.ppermute(own, "c", CORE)
    total = call(join_body, sds((G, Z, Z)), [vm()] * 2, nbytes=2 * MIB)(own, got)
    return cot, total, eff[0, :EEZS]


def solution(mesh):
    fine = Mesh(mesh.devices.reshape(2, 4, 2, 4, 2), ("zl", "x", "c", "y", "zh"))
    field = P(None, LON, LAT, None)
    placed = (
        field,
        field,
        field,
        P(None, ALL),
        P(ALL, None),
        P(ALL),
        P(LON, LAT),
        P(LON, LAT),
    ) + (P(),) * 8
    return jax.shard_map(
        body,
        mesh=fine,
        in_specs=placed,
        out_specs=(field, P(), P()),
        check_vma=False,
    )
```

```python
import functools

import jax
import jax.numpy as jnp
from jax import lax
from jax.experimental import pallas as pl
from jax.experimental.pallas import tpu as pltpu
from jax.sharding import Mesh, PartitionSpec as P

G, Z = 4, 256
CI, CJ = 16, 32
N = CI * CJ
EEZS = 64
H = 0.5
SLOTS = 8
F32, BF16 = jnp.float32, jnp.bfloat16
LON, LAT = ("zl", "x", "c"), ("y", "zh")
ALL = LON + LAT
CHIPS = ("zl", "x", "y", "zh")
NCHIP = 64
MIB = 1024 * 1024
HI = lax.Precision.HIGHEST

LON_A = [(i, i ^ 1) for i in range(16)]
LON_B = [(i, (i + 1) % 16 if i % 2 else (i - 1) % 16) for i in range(16)]
LAT_A = [(i, i ^ 1) for i in range(8)]
LAT_B = [(i, i + 1 if i % 2 else i - 1) for i in range(1, 7)]
CORE = [(0, 1), (1, 0)]


def sds(shape, dtype=F32):
    return jax.ShapeDtypeStruct(shape, dtype)


def vmem(shape, dtype=F32):
    return pltpu.VMEM(shape, dtype)


def vm():
    return pl.BlockSpec(memory_space=pltpu.VMEM)


def sm():
    return pl.BlockSpec(memory_space=pltpu.SMEM)


def call(body, outs, ins, scratch=(), flops=0, nbytes=0, vmem=6, place=True, far=(), out_far=0):
    many = isinstance(outs, list)
    spots = [pl.BlockSpec(memory_space=pl.ANY) if n < out_far else vm() for n in range(len(outs) if many else 1)]
    run = pl.pallas_call(
        body,
        out_shape=outs,
        in_specs=ins,
        out_specs=spots if many else vm(),
        scratch_shapes=list(scratch),
        compiler_params=pltpu.CompilerParams(vmem_limit_bytes=vmem * MIB),
        cost_estimate=pl.CostEstimate(flops=flops, bytes_accessed=nbytes, transcendentals=0),
    )

    def go(*args):
        return run(
            *[
                in_hbm(a) if not place or n in far else near_core(a) if a.size >= 8192 else a
                for n, a in enumerate(args)
            ]
        )

    return go


def near_core(x):
    return pltpu.with_memory_space_constraint(x, pltpu.VMEM)


def in_hbm(x):
    return pltpu.with_memory_space_constraint(x, pltpu.HBM)


def nt(a, b, **kw):
    return lax.dot_general(a, b, (((1,), (1,)), ((), ())), preferred_element_type=F32, **kw)


def nn(a, b, **kw):
    return lax.dot_general(a, b, (((1,), (0,)), ((), ())), preferred_element_type=F32, **kw)


def tn(a, b, **kw):
    return lax.dot_general(a, b, (((0,), (0,)), ((), ())), preferred_element_type=F32, **kw)


def split(x):
    hi = x.astype(BF16).astype(F32)
    return hi, x - hi


def two(x):
    return jnp.concatenate([x, x], axis=1)


def column(row, n, width):
    eye = lax.broadcasted_iota(jnp.int32, (n, n), 0) == lax.broadcasted_iota(jnp.int32, (n, n), 1)
    col = jnp.sum(jnp.where(eye, jnp.broadcast_to(row, (n, n)), 0.0), axis=1, keepdims=True)
    return jnp.broadcast_to(col, (n, width))


def prep_body(c, ocean, cells, count, resid, la, lb, ta, tb, pay, rim_i, rim_j, sem):
    par_i, par_j = lax.axis_index("c"), lax.axis_index("zh")
    copies = [
        pltpu.make_async_copy(c.at[:, CI - 1], rim_i.at[0], sem.at[0]),
        pltpu.make_async_copy(c.at[:, 0], rim_i.at[1], sem.at[1]),
        pltpu.make_async_copy(c.at[:, :, CJ - 8 : CJ, :], rim_j.at[0], sem.at[2]),
        pltpu.make_async_copy(c.at[:, :, 0:8, :], rim_j.at[1], sem.at[3]),
    ]
    for copy in copies:
        copy.start()
    ents, rows = cells.shape
    ne = rows * ents
    devices = 2 * NCHIP
    tile_e = lax.broadcasted_iota(jnp.int32, (ents, ne), 1) // rows == lax.broadcasted_iota(
        jnp.int32, (ents, ne), 0
    )
    tile_r = lax.broadcasted_iota(jnp.int32, (rows, ne), 1) % rows == lax.broadcasted_iota(
        jnp.int32, (rows, ne), 0
    )
    tile_rf = tile_r.astype(F32)
    lon_i = (cells[...] // 256).astype(F32)
    lat_i = (cells[...] % 256).astype(F32)
    r_hi, r_rest = split(resid[...])
    r_mid, r_lo = split(r_rest)
    few = jnp.concatenate([count[...].astype(F32), r_hi, r_mid, r_lo, jnp.zeros((1, rows), F32)], axis=0)
    wide = nn(
        jnp.concatenate([lon_i, lat_i, few], axis=0).astype(BF16), tile_rf.astype(BF16)
    )

    def flat(x):
        return jnp.sum(jnp.where(tile_e, x, 0.0), axis=0, keepdims=True)

    i_row = flat(wide[:ents]).astype(jnp.int32)
    j_row = flat(wide[ents : 2 * ents]).astype(jnp.int32)
    few = wide[2 * ents :]
    n_row = few[0:1]
    r_row = few[1:3] + few[3:5] + few[5:7]
    entry = (lax.broadcasted_iota(jnp.int32, (1, ne), 1) // rows).astype(F32)
    vals = jnp.where(entry < n_row, r_row, 0.0)
    lon = i_row // CI
    owner = (lon % 2) * NCHIP + (lon // 2) * 8 + j_row // CJ
    mine = lax.broadcasted_iota(jnp.int32, (devices, ne), 0) == owner
    mine_b = mine.astype(F32).astype(BF16)
    before = (
        lax.broadcasted_iota(jnp.int32, (ne, ne), 0) < lax.broadcasted_iota(jnp.int32, (ne, ne), 1)
    )
    ahead = nn(mine_b, before.astype(F32).astype(BF16))
    rank = jnp.sum(jnp.where(mine, ahead, 0.0), axis=0, keepdims=True).astype(jnp.int32)
    slot = lax.broadcasted_iota(jnp.int32, (SLOTS, ne), 0) == rank
    h0, l0 = split(vals[0:1])
    h1, l1 = split(vals[1:2])
    a_row = ((i_row % CI) * CJ).astype(F32)
    b_row = (j_row % CJ).astype(F32)

    def rows_of(parts):
        put = [jnp.where(slot, jnp.broadcast_to(p, (SLOTS, ne)), 0.0) for p in parts]
        put.append(jnp.zeros((128 - SLOTS * len(parts), ne), F32))
        return jnp.concatenate(put, axis=0).astype(BF16)

    sorted_ = nt(mine_b, rows_of((h0, h1, a_row))) + nt(mine_b, rows_of((l0, l1, b_row)))
    pay[...] = jnp.concatenate([sorted_[:NCHIP, :64], sorted_[NCHIP:, :64]], axis=1)

    oc = ocean[...].astype(F32)
    edge_i = (column(oc[CI - 1 : CI, :], CJ, Z), column(oc[0:1, :], CJ, Z))
    edge_j = (
        jnp.broadcast_to(oc[:, CJ - 1 : CJ], (CI, Z)),
        jnp.broadcast_to(oc[:, 0:1], (CI, Z)),
    )
    for copy in copies:
        copy.wait()

    def rims(odd, a, b, value):
        for n, (even_to, odd_to) in enumerate(((a, b), (b, a))):
            for g in range(G + 1):
                v = value(n, g)

                @pl.when(odd == 0)
                def _():
                    even_to[g] = v

                @pl.when(odd == 1)
                def _():
                    odd_to[g] = v

    rims(par_i, la, lb, lambda n, g: edge_i[n] if g == G else rim_i[n, g] * edge_i[n])
    rims(
        par_j,
        ta,
        tb,
        lambda n, g: edge_j[n] if g == G else rim_j[n, g, :, 7 if n == 0 else 0, :] * edge_j[n],
    )


def tables(ocean, eez, effort, ocol, ecol, zone):
    oc = ocean[...].astype(F32)
    ez = eez[...].astype(F32)
    lane = lax.broadcasted_iota(jnp.int32, (CJ, 128), 1)
    eff = jnp.concatenate([effort[...], jnp.zeros((1, 128 - EEZS), F32)], axis=1)
    for i in range(CI):
        rows = slice(i * CJ, (i + 1) * CJ)
        ocol[rows] = column(oc[i : i + 1, :], CJ, 128)
        here = (column(ez[i : i + 1, :], CJ, 128).astype(jnp.int32) == lane).astype(F32)
        zone[rows] = here.astype(BF16)
        ecol[rows] = jnp.broadcast_to(jnp.sum(here * eff, axis=1, keepdims=True), (CJ, 128))


def gather_catch(own, other, hot, hi, lo):
    core = lax.axis_index("c")
    both = jnp.concatenate([own[...], other[...]], axis=0)
    flip = both.T
    flip = jnp.where(core == 0, flip[:64], flip[64:])
    got = jnp.where(core == 0, both[:, :64], both[:, 64:])
    for k in range(SLOTS):
        where = flip[2 * SLOTS + k : 2 * SLOTS + k + 1, :].astype(jnp.int32)
        cell = lax.broadcasted_iota(jnp.int32, (N, 128), 0)
        hot[:, k * 128 : (k + 1) * 128] = (cell == where).astype(F32).astype(BF16)
        pair = jnp.concatenate(
            [
                jnp.broadcast_to(got[:, k : k + 1], (128, 128)),
                jnp.broadcast_to(got[:, SLOTS + k : SLOTS + k + 1], (128, 128)),
            ],
            axis=1,
        )
        top, rest = split(pair)
        hi[k * 128 : (k + 1) * 128, :] = top.astype(BF16)
        lo[k * 128 : (k + 1) * 128, :] = rest.astype(BF16)
    return nn(hot[...], hi[...]) + nn(hot[...], lo[...])


def by_zone(y, zone):
    top, rest = split(y[...])
    parts = jnp.concatenate([top, rest], axis=1).astype(BF16)
    return jnp.sum(tn(parts, zone[...]), axis=0, keepdims=True)


R = 128
CHUNKS = N // R


def recip(d):
    r = pltpu.reciprocal(d, approx=True)
    return r * (2.0 - d * r)


def mixed(rows_of, mix, k, turned=False):
    tot = None
    for g in range(G):
        term = (mix[g, k] if turned else mix[k, g]) * rows_of[g]
        tot = term if tot is None else tot + term
    return tot


def gain_of(k, mix, assim, mort, sel, ef, feed, rem):
    tot = (1.0 - H * mort[k : k + 1, :]) - (H * sel[k : k + 1, :]) * ef + (H * assim[k]) * feed
    for g in range(G):
        tot = tot + (-H * mix[g, k]) * rem[g]
    return tot


def forward_rows(rows, mix, st, turn, sel, wt, prey, eaten, feed, gs):
    s = [st[k, rows, :].astype(F32) for k in range(G)]
    part = None
    for k in range(G):
        term = (sel[k : k + 1, :] * wt[...]) * s[k]
        part = term if part is None else part + term
    gs[rows, :] = part[:, :128] + part[:, 128:]
    for g in range(G):
        prey[g, rows, :] = mixed(s, mix, g).astype(BF16)
    for g in range(G):
        enc = nn(prey[g, rows, :], turn[g])
        fd = enc * recip(enc + 1.0)
        feed[g, rows, :] = fd
        eaten[g, rows, :] = (st[g, rows, :].astype(F32) * fd).astype(BF16)


def first_body(*refs):
    mix, assim, saved, c_far, ker, mort, sel, wt, ocean, eez, effort = refs[:11]
    ocol, ecol, zone, turn, st, prey, eaten, feed, gs, gain, c, rem, sem = refs[11:]
    copies = []
    for n in range(CHUNKS):
        rows = slice(n * R, (n + 1) * R)
        copies.append(pltpu.make_async_copy(saved.at[:, rows, :], st.at[:, rows, :], sem.at[n]))
        copies[-1].start()
    copies.append(pltpu.make_async_copy(c_far, c, sem.at[CHUNKS]))
    copies[-1].start()
    for g in range(G):
        turn[g] = ker[g].T
    tables(ocean, eez, effort, ocol, ecol, zone)
    for n in range(CHUNKS):
        rows = slice(n * R, (n + 1) * R)
        copies[n].wait()
        forward_rows(rows, mix, st, turn, sel, wt, prey, eaten, feed, gs)
        for g in range(G):
            rem[g, rows, :] = nn(eaten[g, rows, :], ker[g])
        parts = [rem[g, rows, :] for g in range(G)]
        ef = two(ecol[rows, :])
        for k in range(G):
            gain[k, rows, :] = gain_of(k, mix, assim, mort, sel, ef, feed[k, rows, :], parts)
    copies[CHUNKS].wait()


def second_body(mix, st, turn, sel, wt, prey, eaten, feed, gs):
    for n in range(CHUNKS):
        forward_rows(slice(n * R, (n + 1) * R), mix, st, turn, sel, wt, prey, eaten, feed, gs)


def fill(pad, opad, c, la, lb, ta, tb, ocol):
    par_i, par_j = lax.axis_index("c"), lax.axis_index("zh")
    at_a = jnp.where(par_i == 0, CI + 1, 0)
    at_b = CI + 1 - at_a
    row_a = jnp.where(par_j == 0, CJ + 8, 7)
    row_b = CJ + 15 - row_a
    for g in range(G):
        pad[g, at_a, 8 : 8 + CJ, :] = la[g]
        pad[g, at_b, 8 : 8 + CJ, :] = lb[g]
        for i in range(CI):
            pad[g, i + 1, pl.ds(row_a, 1), :] = ta[g, i : i + 1, :]
            pad[g, i + 1, pl.ds(row_b, 1), :] = tb[g, i : i + 1, :]
    if opad is not None:
        opad[at_a, 8 : 8 + CJ, :] = la[G, :, :128]
        opad[at_b, 8 : 8 + CJ, :] = lb[G, :, :128]
        for i in range(CI):
            opad[i + 1, pl.ds(row_a, 1), :] = ta[G, i : i + 1, :128]
            opad[i + 1, pl.ds(row_b, 1), :] = tb[G, i : i + 1, :128]
    for i in range(CI):
        o = ocol[i * CJ : (i + 1) * CJ, :]
        if opad is not None:
            opad[i + 1, 8 : 8 + CJ, :] = o
        for g in range(G):
            pad[g, i + 1, 8 : 8 + CJ, :] = c[g, i] * two(o)


def around(pad, i, lanes):
    return (pad[i + 2, 8 : 8 + CJ, lanes] + pad[i, 8 : 8 + CJ, lanes]) + (
        pad[i + 1, 9 : 9 + CJ, lanes] + pad[i + 1, 7 : 7 + CJ, lanes]
    )


def spread_row(i, pad, s4, mix, ocol, catch, gs, st, sel, spr, m_out, grm, y):
    rows = slice(i * CJ, (i + 1) * CJ)
    o = ocol[rows, :]
    acc = None
    for z in range(2):
        lanes = slice(z * 128, (z + 1) * 128)
        ms = []
        for g in range(G):
            mid = pad[g, i + 1, 8 : 8 + CJ, lanes]
            m = mid + spr[:, lanes] * (o * around(pad.at[g], i, lanes) - s4 * mid)
            m_out[g, rows, lanes] = m
            ms.append(m * st[g, rows, lanes].astype(F32))
            term = sel[g : g + 1, lanes] * ms[-1]
            acc = term if acc is None else acc + term
        for g in range(G):
            tot = None
            for k in range(G):
                term = (-H * mix[g, k]) * ms[k]
                tot = term if tot is None else tot + term
            grm[g, rows, lanes] = tot.astype(BF16)
    y[rows, :] = H * ((o * catch[rows, :]) * gs[rows, :] - acc)


def enc_grad(g, assim, m, s, ge, fd):
    inv = 1.0 - fd
    return (((H * assim[g]) * (m * s) + ge * s) * (inv * inv)).astype(BF16)


def adj_body(*refs):
    mix, assim, c, la, lb, ta, tb, ocol, ecol, own, other, gs, zone, st, feed, gain, ker, turn, sel, wt, spr = refs[:21]
    c_out, grm, genc, eff, near, later, ola, olb, ota, otb, opad, pad, m_scr, t_scr, y, catch, hot, hi, lo = refs[21:]
    par_i, par_j = lax.axis_index("c"), lax.axis_index("zh")
    fill(pad, opad, c, la, lb, ta, tb, ocol)
    caught = gather_catch(own, other, hot, hi, lo)
    later[...] = caught[:, :128]
    catch[...] = caught[:, 128:]
    for n in range(CHUNKS):
        rows = slice(n * R, (n + 1) * R)
        for i in range(n * R // CJ, (n + 1) * R // CJ):
            s4 = around(opad, i, slice(None))
            near[i * CJ : (i + 1) * CJ, :] = s4
            spread_row(i, pad, s4, mix, ocol, catch, gs, st, sel, spr, m_scr, grm, y)
        q = two(H * ocol[rows, :] * ecol[rows, :] * catch[rows, :])
        for g in range(G):
            ge = nn(grm[g, rows, :], turn[g])
            m, fd = m_scr[g, rows, :], feed[g, rows, :]
            genc[g, rows, :] = enc_grad(g, assim, m, st[g, rows, :].astype(F32), ge, fd)
            m_scr[g, rows, :] = m * gain[g, rows, :] + ge * fd + q * (sel[g : g + 1, :] * wt[...])
        for g in range(G):
            t_scr[g, rows, :] = nn(genc[g, rows, :], ker[g])
        for i in range(n * R // CJ, (n + 1) * R // CJ):
            here = slice(i * CJ, (i + 1) * CJ)
            gp = [t_scr[g, here, :] for g in range(G)]
            for k in range(G):
                c_out[k, i] = m_scr[k, here, :] + mixed(gp, mix, k, True)
    eff[...] = jnp.broadcast_to(by_zone(y, zone), (8, 128))

    def lon_rims(hi, lo):
        for g in range(G):
            hi[g] = c_out[g, CI - 1] * two(ocol[N - CJ : N, :])
            lo[g] = c_out[g, 0] * two(ocol[0:CJ, :])

    def lat_rims(hi, lo):
        for g in range(G):
            for i in range(CI):
                at = i * CJ
                hi[g, i : i + 1, :] = c_out[g, i, CJ - 1 : CJ, :] * two(ocol[at + CJ - 1 : at + CJ, :])
                lo[g, i : i + 1, :] = c_out[g, i, 0:1, :] * two(ocol[at : at + 1, :])

    pl.when(par_i == 0)(lambda: lon_rims(ola, olb))
    pl.when(par_i == 1)(lambda: lon_rims(olb, ola))
    pl.when(par_j == 0)(lambda: lat_rims(ota, otb))
    pl.when(par_j == 1)(lambda: lat_rims(otb, ota))


def part_body(eaten, grm, genc, prey, kp):
    for g in range(G):
        kp[g] = tn(eaten[g], grm[g]) + tn(genc[g], prey[g])


def kernel_half(dst, half, kp, eaten, grm, genc, prey):
    for s in range(2):
        g = 2 * half + s
        dst[s * Z : (s + 1) * Z, :] = kp[g] + tn(eaten[g], grm[g]) + tn(genc[g], prey[g])


def keep_body(kp, eaten, grm, genc, prey, keep):
    kernel_half(keep, lax.axis_index("c"), kp, eaten, grm, genc, prey)


def last_body(*refs):
    mix, assim, c, la, lb, ta, tb, ocol, ecol, catch, gs, zone, st, prey, eaten, feed, turn, sel, spr, near, kp, eff = refs[:22]
    m_hbm, ge_hbm, q_hbm, e_hbm, send, grm, genc, pad, m_scr, ge_scr, y, q_scr, sem = refs[22:]
    core = lax.axis_index("c")
    fill(pad, None, c, la, lb, ta, tb, ocol)
    q_scr[...] = H * ocol[...] * ecol[...] * catch[...]
    copies = [
        pltpu.make_async_copy(q_scr, q_hbm, sem.at[0]),
        pltpu.make_async_copy(ecol, e_hbm, sem.at[1]),
    ]
    for copy in copies:
        copy.start()
    for n in range(CHUNKS):
        rows = slice(n * R, (n + 1) * R)
        for i in range(n * R // CJ, (n + 1) * R // CJ):
            s4 = near[i * CJ : (i + 1) * CJ, :]
            spread_row(i, pad, s4, mix, ocol, catch, gs, st, sel, spr, m_scr, grm, y)
        for g in range(G):
            ge = nn(grm[g, rows, :], turn[g])
            ge_scr[g, rows, :] = ge
            genc[g, rows, :] = enc_grad(
                g, assim, m_scr[g, rows, :], st[g, rows, :].astype(F32), ge, feed[g, rows, :]
            )
        for k, (src, dst) in enumerate(((m_scr, m_hbm), (ge_scr, ge_hbm))):
            copies.append(
                pltpu.make_async_copy(src.at[:, rows, :], dst.at[:, rows, :], sem.at[2 + 2 * n + k])
            )
            copies[-1].start()
    send[2 * Z :, :] = two(eff[...] + by_zone(y, zone))
    kernel_half(send, 1 - core, kp, eaten, grm, genc, prey)
    for copy in copies:
        copy.wait()


def rest_body(mix, assim, saved, m_in, ge_in, q_in, ecol, ker, mort, sel, wt, out, feed, rem, turn):
    @pl.when(pl.program_id(0) == 0)
    def _():
        for g in range(G):
            turn[g] = ker[g].T

    s = [saved[k].astype(F32) for k in range(G)]
    for g in range(G):
        enc = nn(mixed(s, mix, g).astype(BF16), turn[g])
        fd = enc * recip(enc + 1.0)
        feed[g] = fd
        rem[g] = nn((s[g] * fd).astype(BF16), ker[g])
    parts = [rem[g] for g in range(G)]
    ef, q = two(ecol[...]), two(q_in[...])
    for k in range(G):
        fd = feed[k]
        gain = gain_of(k, mix, assim, mort, sel, ef, fd, parts)
        out[k] = m_in[k] * gain + ge_in[k] * fd + q * (sel[k : k + 1, :] * wt[...])
    for g in range(G):
        rem[g] = nn(enc_grad(g, assim, m_in[g], saved[g].astype(F32), ge_in[g], feed[g]), ker[g])
    parts = [rem[g] for g in range(G)]
    for k in range(G):
        out[k] = out[k] + mixed(parts, mix, k, True)


CH = 17


def merge_body(keep, send, got, out):
    eff = send[2 * Z : 2 * Z + 1, :128] + got[2 * Z : 2 * Z + 1, :128]
    for p in range(NCHIP):
        rows = slice(p * 8, p * 8 + 8)
        tot = keep[rows, :] + got[rows, :]
        out[p * CH : p * CH + 8, :] = tot[:, :128]
        out[p * CH + 8 : p * CH + 16, :] = tot[:, 128:]
        out[p * CH + 16 : p * CH + 17, :] = eff


def sum_body(parts, out, eff):
    tot = [None, None, None]
    for p in range(NCHIP):
        new = (
            parts[p * CH : p * CH + 8, :],
            parts[p * CH + 8 : p * CH + 16, :],
            parts[p * CH + 16 : p * CH + 17, :],
        )
        tot = [n if o is None else o + n for o, n in zip(tot, new)]
    both = jnp.concatenate(tot[:2], axis=1)
    eff[...] = tot[2]
    for p in range(NCHIP):
        out[p] = both


def join_body(own, got, out, sem):
    core = lax.axis_index("c")
    copies = []
    for n, (half, src) in enumerate(((core, own), (1 - core, got))):
        for s in range(2):
            copies.append(
                pltpu.make_async_copy(
                    src.at[s * Z : (s + 1) * Z, :], out.at[2 * half + s], sem.at[2 * n + s]
                )
            )
            copies[-1].start()
    for copy in copies:
        copy.wait()


def exchange(la, lb, ta, tb):
    return (
        lax.ppermute(la, LON, LON_A),
        lax.ppermute(lb, LON, LON_B),
        lax.ppermute(ta, LAT, LAT_A),
        lax.ppermute(tb, LAT, LAT_B),
    )


def body(
    final_cotangent,
    saved_start,
    saved_middle,
    residuals,
    row_cells,
    row_count,
    ocean_mask,
    cell_eez,
    effort,
    kernel,
    mix,
    assim,
    mortality,
    select,
    weight,
    spread,
):
    wt, spr = weight.reshape(1, Z), spread.reshape(1, Z)
    any_ = pl.BlockSpec(memory_space=pl.ANY)
    field = (G, N, Z)
    rims = [vmem((G + 1, CJ, Z))] * 2 + [vmem((G + 1, CI, Z))] * 2
    *rim, pay = call(
        prep_body,
        rims + [vmem((NCHIP, 128))],
        [any_] + [vm()] * 4,
        [
            pltpu.VMEM((2, G, CJ, Z), F32),
            pltpu.VMEM((2, G, CI, 8, Z), F32),
            pltpu.SemaphoreType.DMA((4,)),
        ],
        flops=2**27,
        nbytes=3 * MIB,
        place=False,
    )(final_cotangent, ocean_mask, row_cells.T, row_count.reshape(1, -1), residuals)
    rim = exchange(*rim)
    own = lax.all_to_all(pay, CHIPS, 0, 0, tiled=True)
    own, middle = lax.optimization_barrier((own, saved_middle))
    other = lax.ppermute(own, "c", CORE)

    ocol, ecol, zone, turn, st, prey, eaten, feed, gs, gain, cot = call(
        first_body,
        [vmem((N, 128))] * 2
        + [vmem((N, 128), BF16), vmem((G, Z, Z), BF16)]
        + [vmem(field, BF16)] * 3
        + [vmem(field), vmem((N, 128)), vmem(field), vmem((G, CI, CJ, Z))],
        [sm(), sm(), any_, any_] + [vm()] * 7,
        [pltpu.VMEM(field, F32), pltpu.SemaphoreType.DMA((CHUNKS + 1,))],
        flops=2**29,
        nbytes=8 * MIB,
        vmem=8,
        far=(2, 3),
    )(
        *(mix, assim, middle.reshape(field), final_cotangent, kernel, mortality, select, wt),
        *(ocean_mask, cell_eez, effort.reshape(1, EEZS)),
    )
    pads = pltpu.VMEM((G, CI + 2, CJ + 16, Z), F32)
    cot, grm, genc, eff, near, catch, *rim = call(
        adj_body,
        [vmem((G, CI, CJ, Z))]
        + [vmem(field, BF16)] * 2
        + [vmem((8, 128)), vmem((N, 128)), vmem((N, 128))]
        + [vmem((G, CJ, Z))] * 2
        + [vmem((G, CI, Z))] * 2,
        [sm(), sm()] + [vm()] * 19,
        [pltpu.VMEM((CI + 2, CJ + 16, 128), F32), pads]
        + [pltpu.VMEM(field, F32)] * 2
        + [pltpu.VMEM((N, 128), F32)] * 2
        + [pltpu.VMEM((N, SLOTS * 128), BF16)]
        + [pltpu.VMEM((SLOTS * 128, 256), BF16)] * 2,
        flops=2**30,
        nbytes=16 * MIB,
        vmem=16,
    )(
        *(mix, assim, cot, *rim, ocol, ecol, own, other, gs, zone, st, feed, gain),
        *(kernel, turn, select, wt, spr),
    )
    rim = exchange(*rim)
    kp = call(part_body, vmem((G, Z, Z)), [vm()] * 4, flops=2**29, nbytes=5 * MIB)(
        eaten, grm, genc, prey
    )
    st = saved_start.reshape(field)
    prey, eaten, feed, gs = call(
        second_body,
        [vmem(field, BF16)] * 2 + [vmem(field), vmem((N, 128))],
        [sm()] + [vm()] * 4,
        flops=2**28,
        nbytes=4 * MIB,
    )(mix, st, turn, select, wt)
    m, ge, q, ef, send, grm, genc = call(
        last_body,
        [pltpu.HBM(field, F32)] * 2 + [pltpu.HBM((N, 128), F32)] * 2 + [vmem((2 * Z + 8, Z))] + [vmem(field, BF16)] * 2,
        [sm(), sm()] + [vm()] * 20,
        [pads]
        + [pltpu.VMEM(field, F32)] * 2
        + [pltpu.VMEM((N, 128), F32)] * 2
        + [pltpu.SemaphoreType.DMA((2 + 2 * CHUNKS,))],
        flops=2**30,
        nbytes=16 * MIB,
        vmem=16,
        out_far=4,
    )(
        *(mix, assim, cot, *rim, ocol, ecol, catch, gs, zone, st, prey, eaten, feed),
        *(turn, select, spr, near, kp, eff),
    )
    block = pl.BlockSpec((G, R, Z), lambda n: (0, n, 0))
    cells = pl.BlockSpec((R, 128), lambda n: (n, 0))
    whole = pl.BlockSpec((G, Z), lambda n: (0, 0))
    cot = pl.pallas_call(
        rest_body,
        grid=(CHUNKS,),
        out_shape=sds(field),
        in_specs=[sm(), sm(), block, block, block, cells, cells]
        + [pl.BlockSpec((G, Z, Z), lambda n: (0, 0, 0)), whole, whole]
        + [pl.BlockSpec((1, Z), lambda n: (0, 0))],
        out_specs=block,
        scratch_shapes=[pltpu.VMEM((G, R, Z), F32)] * 2 + [pltpu.VMEM((G, Z, Z), BF16)],
        compiler_params=pltpu.CompilerParams(vmem_limit_bytes=16 * MIB),
        cost_estimate=pl.CostEstimate(flops=2**30, bytes_accessed=12 * MIB, transcendentals=0),
    )(mix, assim, *map(in_hbm, (saved_start.reshape(field), m, ge, q, ef, kernel)), mortality, select, wt)
    cot = cot.reshape(G, CI, CJ, Z)

    got = lax.ppermute(send, "c", CORE)
    keep = call(keep_body, vmem((2 * Z, Z)), [vm()] * 5, flops=2**28, nbytes=4 * MIB)(
        kp, eaten, grm, genc, prey
    )
    chunks = call(merge_body, vmem((NCHIP * CH, 128)), [vm()] * 3, nbytes=2 * MIB)(keep, send, got)
    chunks = lax.all_to_all(chunks.reshape(NCHIP, 1, CH * 128), CHIPS, 0, 0, tiled=True)
    chunks = chunks.reshape(NCHIP * CH, 128)
    own, eff = call(sum_body, [vmem((NCHIP, 8, Z)), vmem((1, 128))], [vm()], nbytes=MIB)(chunks)
    own, cot = lax.optimization_barrier((own, cot))
    own = lax.all_to_all(own, CHIPS, 0, 0, tiled=True).reshape(2 * Z, Z)
    got = lax.ppermute(own, "c", CORE)
    total = call(
        join_body,
        [pltpu.HBM((G, Z, Z), F32)],
        [vm()] * 2,
        [pltpu.SemaphoreType.DMA((4,))],
        nbytes=2 * MIB,
        out_far=1,
    )(own, got)[0]
    return cot, total, eff[0, :EEZS]


def solution(mesh):
    fine = Mesh(mesh.devices.reshape(2, 4, 2, 4, 2), ("zl", "x", "c", "y", "zh"))
    field = P(None, LON, LAT, None)
    placed = (
        field,
        field,
        field,
        P(None, ALL),
        P(ALL, None),
        P(ALL),
        P(LON, LAT),
        P(LON, LAT),
    ) + (P(),) * 8
    return jax.shard_map(
        body,
        mesh=fine,
        in_specs=placed,
        out_specs=(field, P(), P()),
        check_vma=False,
    )
```

```python
import functools

import jax
import jax.numpy as jnp
from jax import lax
from jax.experimental import pallas as pl
from jax.experimental.pallas import tpu as pltpu
from jax.sharding import Mesh, PartitionSpec as P

G, Z = 4, 256
CI, CJ = 16, 32
N = CI * CJ
EEZS = 64
H = 0.5
SLOTS = 8
F32, BF16 = jnp.float32, jnp.bfloat16
LON, LAT = ("zl", "x", "c"), ("y", "zh")
ALL = LON + LAT
CHIPS = ("zl", "x", "y", "zh")
NCHIP = 64
MIB = 1024 * 1024
HI = lax.Precision.HIGHEST

LON_A = [(i, i ^ 1) for i in range(16)]
LON_B = [(i, (i + 1) % 16 if i % 2 else (i - 1) % 16) for i in range(16)]
LAT_A = [(i, i ^ 1) for i in range(8)]
LAT_B = [(i, i + 1 if i % 2 else i - 1) for i in range(1, 7)]
CORE = [(0, 1), (1, 0)]


def sds(shape, dtype=F32):
    return jax.ShapeDtypeStruct(shape, dtype)


def vmem(shape, dtype=F32):
    return pltpu.VMEM(shape, dtype)


def vm():
    return pl.BlockSpec(memory_space=pltpu.VMEM)


def sm():
    return pl.BlockSpec(memory_space=pltpu.SMEM)


def call(body, outs, ins, scratch=(), flops=0, nbytes=0, vmem=6, place=True, far=(), out_far=0):
    many = isinstance(outs, list)
    spots = [pl.BlockSpec(memory_space=pl.ANY) if n < out_far else vm() for n in range(len(outs) if many else 1)]
    run = pl.pallas_call(
        body,
        out_shape=outs,
        in_specs=ins,
        out_specs=spots if many else vm(),
        scratch_shapes=list(scratch),
        compiler_params=pltpu.CompilerParams(vmem_limit_bytes=vmem * MIB),
        cost_estimate=pl.CostEstimate(flops=flops, bytes_accessed=nbytes, transcendentals=0),
    )

    def go(*args):
        return run(
            *[
                in_hbm(a) if not place or n in far else near_core(a) if a.size >= 8192 else a
                for n, a in enumerate(args)
            ]
        )

    return go


def near_core(x):
    return pltpu.with_memory_space_constraint(x, pltpu.VMEM)


def in_hbm(x):
    return pltpu.with_memory_space_constraint(x, pltpu.HBM)


def nt(a, b, **kw):
    return lax.dot_general(a, b, (((1,), (1,)), ((), ())), preferred_element_type=F32, **kw)


def nn(a, b, **kw):
    return lax.dot_general(a, b, (((1,), (0,)), ((), ())), preferred_element_type=F32, **kw)


def tn(a, b, **kw):
    return lax.dot_general(a, b, (((0,), (0,)), ((), ())), preferred_element_type=F32, **kw)


def split(x):
    hi = x.astype(BF16).astype(F32)
    return hi, x - hi


def two(x):
    return jnp.concatenate([x, x], axis=1)


def column(row, n, width):
    eye = lax.broadcasted_iota(jnp.int32, (n, n), 0) == lax.broadcasted_iota(jnp.int32, (n, n), 1)
    col = jnp.sum(jnp.where(eye, jnp.broadcast_to(row, (n, n)), 0.0), axis=1, keepdims=True)
    return jnp.broadcast_to(col, (n, width))


def prep_body(c, ocean, cells, count, resid, la, lb, ta, tb, pay, rim_i, rim_j, sem):
    par_i, par_j = lax.axis_index("c"), lax.axis_index("zh")
    copies = [
        pltpu.make_async_copy(c.at[:, CI - 1], rim_i.at[0], sem.at[0]),
        pltpu.make_async_copy(c.at[:, 0], rim_i.at[1], sem.at[1]),
        pltpu.make_async_copy(c.at[:, :, CJ - 8 : CJ, :], rim_j.at[0], sem.at[2]),
        pltpu.make_async_copy(c.at[:, :, 0:8, :], rim_j.at[1], sem.at[3]),
    ]
    for copy in copies:
        copy.start()
    ents, rows = cells.shape
    ne = rows * ents
    devices = 2 * NCHIP
    tile_e = lax.broadcasted_iota(jnp.int32, (ents, ne), 1) // rows == lax.broadcasted_iota(
        jnp.int32, (ents, ne), 0
    )
    tile_r = lax.broadcasted_iota(jnp.int32, (rows, ne), 1) % rows == lax.broadcasted_iota(
        jnp.int32, (rows, ne), 0
    )
    tile_rf = tile_r.astype(F32)
    lon_i = (cells[...] // 256).astype(F32)
    lat_i = (cells[...] % 256).astype(F32)
    r_hi, r_rest = split(resid[...])
    r_mid, r_lo = split(r_rest)
    few = jnp.concatenate([count[...].astype(F32), r_hi, r_mid, r_lo, jnp.zeros((1, rows), F32)], axis=0)
    wide = nn(
        jnp.concatenate([lon_i, lat_i, few], axis=0).astype(BF16), tile_rf.astype(BF16)
    )

    def flat(x):
        return jnp.sum(jnp.where(tile_e, x, 0.0), axis=0, keepdims=True)

    i_row = flat(wide[:ents]).astype(jnp.int32)
    j_row = flat(wide[ents : 2 * ents]).astype(jnp.int32)
    few = wide[2 * ents :]
    n_row = few[0:1]
    r_row = few[1:3] + few[3:5] + few[5:7]
    entry = (lax.broadcasted_iota(jnp.int32, (1, ne), 1) // rows).astype(F32)
    vals = jnp.where(entry < n_row, r_row, 0.0)
    lon = i_row // CI
    owner = (lon % 2) * NCHIP + (lon // 2) * 8 + j_row // CJ
    mine = lax.broadcasted_iota(jnp.int32, (devices, ne), 0) == owner
    mine_b = mine.astype(F32).astype(BF16)
    before = (
        lax.broadcasted_iota(jnp.int32, (ne, ne), 0) < lax.broadcasted_iota(jnp.int32, (ne, ne), 1)
    )
    ahead = nn(mine_b, before.astype(F32).astype(BF16))
    rank = jnp.sum(jnp.where(mine, ahead, 0.0), axis=0, keepdims=True).astype(jnp.int32)
    slot = lax.broadcasted_iota(jnp.int32, (SLOTS, ne), 0) == rank
    h0, l0 = split(vals[0:1])
    h1, l1 = split(vals[1:2])
    a_row = ((i_row % CI) * CJ).astype(F32)
    b_row = (j_row % CJ).astype(F32)

    def rows_of(parts):
        put = [jnp.where(slot, jnp.broadcast_to(p, (SLOTS, ne)), 0.0) for p in parts]
        put.append(jnp.zeros((128 - SLOTS * len(parts), ne), F32))
        return jnp.concatenate(put, axis=0).astype(BF16)

    sorted_ = nt(mine_b, rows_of((h0, h1, a_row))) + nt(mine_b, rows_of((l0, l1, b_row)))
    pay[...] = jnp.concatenate([sorted_[:NCHIP, :64], sorted_[NCHIP:, :64]], axis=1)

    oc = ocean[...].astype(F32)
    edge_i = (column(oc[CI - 1 : CI, :], CJ, Z), column(oc[0:1, :], CJ, Z))
    edge_j = (
        jnp.broadcast_to(oc[:, CJ - 1 : CJ], (CI, Z)),
        jnp.broadcast_to(oc[:, 0:1], (CI, Z)),
    )
    for copy in copies:
        copy.wait()

    def rims(odd, a, b, value):
        for n, (even_to, odd_to) in enumerate(((a, b), (b, a))):
            for g in range(G + 1):
                v = value(n, g)

                @pl.when(odd == 0)
                def _():
                    even_to[g] = v

                @pl.when(odd == 1)
                def _():
                    odd_to[g] = v

    rims(par_i, la, lb, lambda n, g: edge_i[n] if g == G else rim_i[n, g] * edge_i[n])
    rims(
        par_j,
        ta,
        tb,
        lambda n, g: edge_j[n] if g == G else rim_j[n, g, :, 7 if n == 0 else 0, :] * edge_j[n],
    )


def tables(ocean, eez, effort, ocol, ecol, zone):
    oc = ocean[...].astype(F32)
    ez = eez[...].astype(F32)
    lane = lax.broadcasted_iota(jnp.int32, (CJ, 128), 1)
    eff = jnp.concatenate([effort[...], jnp.zeros((1, 128 - EEZS), F32)], axis=1)
    for i in range(CI):
        rows = slice(i * CJ, (i + 1) * CJ)
        ocol[rows] = column(oc[i : i + 1, :], CJ, 128)
        here = (column(ez[i : i + 1, :], CJ, 128).astype(jnp.int32) == lane).astype(F32)
        zone[rows] = here.astype(BF16)
        ecol[rows] = jnp.broadcast_to(jnp.sum(here * eff, axis=1, keepdims=True), (CJ, 128))


def gather_catch(own, other, hot, hi, lo):
    core = lax.axis_index("c")
    both = jnp.concatenate([own[...], other[...]], axis=0)
    flip = both.T
    flip = jnp.where(core == 0, flip[:64], flip[64:])
    got = jnp.where(core == 0, both[:, :64], both[:, 64:])
    for k in range(SLOTS):
        where = flip[2 * SLOTS + k : 2 * SLOTS + k + 1, :].astype(jnp.int32)
        cell = lax.broadcasted_iota(jnp.int32, (N, 128), 0)
        hot[:, k * 128 : (k + 1) * 128] = (cell == where).astype(F32).astype(BF16)
        pair = jnp.concatenate(
            [
                jnp.broadcast_to(got[:, k : k + 1], (128, 128)),
                jnp.broadcast_to(got[:, SLOTS + k : SLOTS + k + 1], (128, 128)),
            ],
            axis=1,
        )
        top, rest = split(pair)
        hi[k * 128 : (k + 1) * 128, :] = top.astype(BF16)
        lo[k * 128 : (k + 1) * 128, :] = rest.astype(BF16)
    return nn(hot[...], hi[...]) + nn(hot[...], lo[...])


def by_zone(y, zone):
    top, rest = split(y[...])
    parts = jnp.concatenate([top, rest], axis=1).astype(BF16)
    return jnp.sum(tn(parts, zone[...]), axis=0, keepdims=True)


R = 128
CHUNKS = N // R


def recip(d):
    r = pltpu.reciprocal(d, approx=True)
    return r * (2.0 - d * r)


def mixed(rows_of, mix, k, turned=False):
    tot = None
    for g in range(G):
        term = (mix[g, k] if turned else mix[k, g]) * rows_of[g]
        tot = term if tot is None else tot + term
    return tot


def gain_of(k, mix, assim, mort, sel, ef, feed, rem):
    tot = (1.0 - H * mort[k : k + 1, :]) - (H * sel[k : k + 1, :]) * ef + (H * assim[k]) * feed
    for g in range(G):
        tot = tot + (-H * mix[g, k]) * rem[g]
    return tot


def forward_rows(rows, mix, st, turn, sel, wt, prey, eaten, feed, gs):
    s = [st[k, rows, :].astype(F32) for k in range(G)]
    part = None
    for k in range(G):
        term = (sel[k : k + 1, :] * wt[...]) * s[k]
        part = term if part is None else part + term
    gs[rows, :] = part[:, :128] + part[:, 128:]
    for g in range(G):
        prey[g, rows, :] = mixed(s, mix, g).astype(BF16)
    for g in range(G):
        enc = nn(prey[g, rows, :], turn[g])
        fd = enc * recip(enc + 1.0)
        feed[g, rows, :] = fd
        eaten[g, rows, :] = (st[g, rows, :].astype(F32) * fd).astype(BF16)


def first_body(*refs):
    mix, assim, saved, c_far, ker, mort, sel, wt, ocean, eez, effort = refs[:11]
    ocol, ecol, zone, turn, st, prey, eaten, feed, gs, gain, c, rem, sem = refs[11:]
    copies = []
    for n in range(CHUNKS):
        rows = slice(n * R, (n + 1) * R)
        copies.append(pltpu.make_async_copy(saved.at[:, rows, :], st.at[:, rows, :], sem.at[n]))
        copies[-1].start()
    copies.append(pltpu.make_async_copy(c_far, c, sem.at[CHUNKS]))
    copies[-1].start()
    for g in range(G):
        turn[g] = ker[g].T
    tables(ocean, eez, effort, ocol, ecol, zone)
    for n in range(CHUNKS):
        rows = slice(n * R, (n + 1) * R)
        copies[n].wait()
        forward_rows(rows, mix, st, turn, sel, wt, prey, eaten, feed, gs)
        for g in range(G):
            rem[g, rows, :] = nn(eaten[g, rows, :], ker[g])
        parts = [rem[g, rows, :] for g in range(G)]
        ef = two(ecol[rows, :])
        for k in range(G):
            gain[k, rows, :] = gain_of(k, mix, assim, mort, sel, ef, feed[k, rows, :], parts)
    copies[CHUNKS].wait()


def second_body(mix, st, turn, sel, wt, prey, eaten, feed, gs):
    for n in range(CHUNKS):
        forward_rows(slice(n * R, (n + 1) * R), mix, st, turn, sel, wt, prey, eaten, feed, gs)


def fill(pad, opad, c, la, lb, ta, tb, ocol):
    par_i, par_j = lax.axis_index("c"), lax.axis_index("zh")
    at_a = jnp.where(par_i == 0, CI + 1, 0)
    at_b = CI + 1 - at_a
    row_a = jnp.where(par_j == 0, CJ + 8, 7)
    row_b = CJ + 15 - row_a
    for g in range(G):
        pad[g, at_a, 8 : 8 + CJ, :] = la[g]
        pad[g, at_b, 8 : 8 + CJ, :] = lb[g]
        for i in range(CI):
            pad[g, i + 1, pl.ds(row_a, 1), :] = ta[g, i : i + 1, :]
            pad[g, i + 1, pl.ds(row_b, 1), :] = tb[g, i : i + 1, :]
    if opad is not None:
        opad[at_a, 8 : 8 + CJ, :] = la[G, :, :128]
        opad[at_b, 8 : 8 + CJ, :] = lb[G, :, :128]
        for i in range(CI):
            opad[i + 1, pl.ds(row_a, 1), :] = ta[G, i : i + 1, :128]
            opad[i + 1, pl.ds(row_b, 1), :] = tb[G, i : i + 1, :128]
    for i in range(CI):
        o = ocol[i * CJ : (i + 1) * CJ, :]
        if opad is not None:
            opad[i + 1, 8 : 8 + CJ, :] = o
        for g in range(G):
            pad[g, i + 1, 8 : 8 + CJ, :] = c[g, i] * two(o)


def around(pad, i, lanes):
    return (pad[i + 2, 8 : 8 + CJ, lanes] + pad[i, 8 : 8 + CJ, lanes]) + (
        pad[i + 1, 9 : 9 + CJ, lanes] + pad[i + 1, 7 : 7 + CJ, lanes]
    )


def spread_row(i, pad, s4, mix, ocol, catch, gs, st, sel, spr, m_out, grm, y):
    rows = pl.ds(i * CJ, CJ)
    o = ocol[rows, :]
    acc = None
    for z in range(2):
        lanes = slice(z * 128, (z + 1) * 128)
        ms = []
        for g in range(G):
            mid = pad[g, i + 1, 8 : 8 + CJ, lanes]
            m = mid + spr[:, lanes] * (o * around(pad.at[g], i, lanes) - s4 * mid)
            m_out[g, rows, lanes] = m
            ms.append(m * st[g, rows, lanes].astype(F32))
            term = sel[g : g + 1, lanes] * ms[-1]
            acc = term if acc is None else acc + term
        for g in range(G):
            tot = None
            for k in range(G):
                term = (-H * mix[g, k]) * ms[k]
                tot = term if tot is None else tot + term
            grm[g, rows, lanes] = tot.astype(BF16)
    y[rows, :] = H * ((o * catch[rows, :]) * gs[rows, :] - acc)


def enc_grad(g, assim, m, s, ge, fd):
    inv = 1.0 - fd
    return (((H * assim[g]) * (m * s) + ge * s) * (inv * inv)).astype(BF16)


def adj_body(*refs):
    mix, assim, c, tb, ta, lb, la, ocol, ecol, own, other, gs, zone, st, feed, gain, ker, turn, sel, wt, spr = refs[:21]
    c_out, grm, genc, eff, near, later, ola, olb, ota, otb, opad, pad, m_scr, t_scr, y, catch, hot, hi, lo = refs[21:]
    par_i, par_j = lax.axis_index("c"), lax.axis_index("zh")
    fill(pad, opad, c, la, lb, ta, tb, ocol)
    caught = gather_catch(own, other, hot, hi, lo)
    later[...] = caught[:, :128]
    catch[...] = caught[:, 128:]
    for n in range(CHUNKS):
        rows = slice(n * R, (n + 1) * R)
        for i in range(n * R // CJ, (n + 1) * R // CJ):
            s4 = around(opad, i, slice(None))
            near[i * CJ : (i + 1) * CJ, :] = s4
            spread_row(i, pad, s4, mix, ocol, catch, gs, st, sel, spr, m_scr, grm, y)
        q = two(H * ocol[rows, :] * ecol[rows, :] * catch[rows, :])
        for g in range(G):
            ge = nn(grm[g, rows, :], turn[g])
            m, fd = m_scr[g, rows, :], feed[g, rows, :]
            genc[g, rows, :] = enc_grad(g, assim, m, st[g, rows, :].astype(F32), ge, fd)
            m_scr[g, rows, :] = m * gain[g, rows, :] + ge * fd + q * (sel[g : g + 1, :] * wt[...])
        for g in range(G):
            t_scr[g, rows, :] = nn(genc[g, rows, :], ker[g])
        for i in range(n * R // CJ, (n + 1) * R // CJ):
            here = slice(i * CJ, (i + 1) * CJ)
            gp = [t_scr[g, here, :] for g in range(G)]
            for k in range(G):
                c_out[k, i] = m_scr[k, here, :] + mixed(gp, mix, k, True)
    eff[...] = jnp.broadcast_to(by_zone(y, zone), (8, 128))

    def lon_rims(hi, lo):
        for g in range(G):
            hi[g] = c_out[g, CI - 1] * two(ocol[N - CJ : N, :])
            lo[g] = c_out[g, 0] * two(ocol[0:CJ, :])

    def lat_rims(hi, lo):
        for g in range(G):
            for i in range(CI):
                at = i * CJ
                hi[g, i : i + 1, :] = c_out[g, i, CJ - 1 : CJ, :] * two(ocol[at + CJ - 1 : at + CJ, :])
                lo[g, i : i + 1, :] = c_out[g, i, 0:1, :] * two(ocol[at : at + 1, :])

    pl.when(par_i == 0)(lambda: lon_rims(ola, olb))
    pl.when(par_i == 1)(lambda: lon_rims(olb, ola))
    pl.when(par_j == 0)(lambda: lat_rims(ota, otb))
    pl.when(par_j == 1)(lambda: lat_rims(otb, ota))


def part_body(eaten, grm, genc, prey, kp):
    for g in range(G):
        kp[g] = tn(eaten[g], grm[g]) + tn(genc[g], prey[g])


def kernel_half(dst, half, kp, eaten, grm, genc, prey):
    for s in range(2):
        g = 2 * half + s
        dst[s * Z : (s + 1) * Z, :] = kp[g] + tn(eaten[g], grm[g]) + tn(genc[g], prey[g])


def keep_body(kp, eaten, grm, genc, prey, keep):
    kernel_half(keep, lax.axis_index("c"), kp, eaten, grm, genc, prey)


def last_body(*refs):
    mix, assim, c, tb, ta, lb, la, ocol, ecol, catch, gs, zone, st, prey, eaten, feed, turn, sel, spr, near, kp, eff = refs[:22]
    m_hbm, ge_hbm, q_hbm, e_hbm, send, grm, genc, pad, m_scr, ge_scr, y, q_scr, sem = refs[22:]
    core = lax.axis_index("c")
    fill(pad, None, c, la, lb, ta, tb, ocol)
    q_scr[...] = H * ocol[...] * ecol[...] * catch[...]
    copies = [
        pltpu.make_async_copy(q_scr, q_hbm, sem.at[0]),
        pltpu.make_async_copy(ecol, e_hbm, sem.at[1]),
    ]
    for copy in copies:
        copy.start()

    @pl.loop(0, CI)
    def _(i):
        s4 = near[pl.ds(i * CJ, CJ), :]
        spread_row(i, pad, s4, mix, ocol, catch, gs, st, sel, spr, m_scr, grm, y)

    copies.append(pltpu.make_async_copy(m_scr, m_hbm, sem.at[2]))
    copies[-1].start()
    for g in range(G):
        ge_scr[g] = nn(grm[g], turn[g])
    copies.append(pltpu.make_async_copy(ge_scr, ge_hbm, sem.at[3]))
    copies[-1].start()

    @pl.loop(0, CI)
    def _(i):
        rows = pl.ds(i * CJ, CJ)
        for g in range(G):
            genc[g, rows, :] = enc_grad(
                g,
                assim,
                m_scr[g, rows, :],
                st[g, rows, :].astype(F32),
                ge_scr[g, rows, :],
                feed[g, rows, :],
            )

    send[2 * Z :, :] = two(eff[...] + by_zone(y, zone))
    kernel_half(send, 1 - core, kp, eaten, grm, genc, prey)
    for copy in copies:
        copy.wait()


def rest_body(mix, assim, saved, m_in, ge_in, q_in, ecol, ker, mort, sel, wt, out, feed, rem, turn):
    @pl.when(pl.program_id(0) == 0)
    def _():
        for g in range(G):
            turn[g] = ker[g].T

    s = [saved[k].astype(F32) for k in range(G)]
    for g in range(G):
        enc = nn(mixed(s, mix, g).astype(BF16), turn[g])
        fd = enc * recip(enc + 1.0)
        feed[g] = fd
        rem[g] = nn((s[g] * fd).astype(BF16), ker[g])
    parts = [rem[g] for g in range(G)]
    ef, q = two(ecol[...]), two(q_in[...])
    for k in range(G):
        fd = feed[k]
        gain = gain_of(k, mix, assim, mort, sel, ef, fd, parts)
        out[k] = m_in[k] * gain + ge_in[k] * fd + q * (sel[k : k + 1, :] * wt[...])
    for g in range(G):
        rem[g] = nn(enc_grad(g, assim, m_in[g], saved[g].astype(F32), ge_in[g], feed[g]), ker[g])
    parts = [rem[g] for g in range(G)]
    for k in range(G):
        out[k] = out[k] + mixed(parts, mix, k, True)


CH = 17


def merge_body(keep, send, got, out):
    eff = send[2 * Z : 2 * Z + 1, :128] + got[2 * Z : 2 * Z + 1, :128]
    for p in range(NCHIP):
        rows = slice(p * 8, p * 8 + 8)
        tot = keep[rows, :] + got[rows, :]
        out[p * CH : p * CH + 8, :] = tot[:, :128]
        out[p * CH + 8 : p * CH + 16, :] = tot[:, 128:]
        out[p * CH + 16 : p * CH + 17, :] = eff


def sum_body(parts, out, eff):
    tot = [None, None, None]
    for p in range(NCHIP):
        new = (
            parts[p * CH : p * CH + 8, :],
            parts[p * CH + 8 : p * CH + 16, :],
            parts[p * CH + 16 : p * CH + 17, :],
        )
        tot = [n if o is None else o + n for o, n in zip(tot, new)]
    both = jnp.concatenate(tot[:2], axis=1)
    eff[...] = tot[2]
    for p in range(NCHIP):
        out[p] = both


def join_body(own, got, out, sem):
    core = lax.axis_index("c")
    copies = []
    for n, (half, src) in enumerate(((core, own), (1 - core, got))):
        for s in range(2):
            copies.append(
                pltpu.make_async_copy(
                    src.at[s * Z : (s + 1) * Z, :], out.at[2 * half + s], sem.at[2 * n + s]
                )
            )
            copies[-1].start()
    for copy in copies:
        copy.wait()


def exchange(la, lb, ta, tb):
    tb = lax.ppermute(tb, LAT, LAT_B)
    ta = lax.ppermute(ta, LAT, LAT_A)
    lb = lax.ppermute(lb, LON, LON_B)
    la = lax.ppermute(la, LON, LON_A)
    return la, lb, ta, tb


def body(
    final_cotangent,
    saved_start,
    saved_middle,
    residuals,
    row_cells,
    row_count,
    ocean_mask,
    cell_eez,
    effort,
    kernel,
    mix,
    assim,
    mortality,
    select,
    weight,
    spread,
):
    wt, spr = weight.reshape(1, Z), spread.reshape(1, Z)
    any_ = pl.BlockSpec(memory_space=pl.ANY)
    field = (G, N, Z)
    rims = [vmem((G + 1, CJ, Z))] * 2 + [vmem((G + 1, CI, Z))] * 2
    *rim, pay = call(
        prep_body,
        rims + [vmem((NCHIP, 128))],
        [any_] + [vm()] * 4,
        [
            pltpu.VMEM((2, G, CJ, Z), F32),
            pltpu.VMEM((2, G, CI, 8, Z), F32),
            pltpu.SemaphoreType.DMA((4,)),
        ],
        flops=2**27,
        nbytes=3 * MIB,
        place=False,
    )(final_cotangent, ocean_mask, row_cells.T, row_count.reshape(1, -1), residuals)
    rim = exchange(*rim)
    own = lax.all_to_all(pay, CHIPS, 0, 0, tiled=True)
    own, middle = lax.optimization_barrier((own, saved_middle))
    other = lax.ppermute(own, "c", CORE)

    ocol, ecol, zone, turn, st, prey, eaten, feed, gs, gain, cot = call(
        first_body,
        [vmem((N, 128))] * 2
        + [vmem((N, 128), BF16), vmem((G, Z, Z), BF16)]
        + [vmem(field, BF16)] * 3
        + [vmem(field), vmem((N, 128)), vmem(field), vmem((G, CI, CJ, Z))],
        [sm(), sm(), any_, any_] + [vm()] * 7,
        [pltpu.VMEM(field, F32), pltpu.SemaphoreType.DMA((CHUNKS + 1,))],
        flops=2**32,
        nbytes=16 * MIB,
        vmem=8,
        far=(2, 3),
    )(
        *(mix, assim, middle.reshape(field), final_cotangent, kernel, mortality, select, wt),
        *(ocean_mask, cell_eez, effort.reshape(1, EEZS)),
    )
    pads = pltpu.VMEM((G, CI + 2, CJ + 16, Z), F32)
    cot, grm, genc, eff, near, catch, *rim = call(
        adj_body,
        [vmem((G, CI, CJ, Z))]
        + [vmem(field, BF16)] * 2
        + [vmem((8, 128)), vmem((N, 128)), vmem((N, 128))]
        + [vmem((G, CJ, Z))] * 2
        + [vmem((G, CI, Z))] * 2,
        [sm(), sm()] + [vm()] * 19,
        [pltpu.VMEM((CI + 2, CJ + 16, 128), F32), pads]
        + [pltpu.VMEM(field, F32)] * 2
        + [pltpu.VMEM((N, 128), F32)] * 2
        + [pltpu.VMEM((N, SLOTS * 128), BF16)]
        + [pltpu.VMEM((SLOTS * 128, 256), BF16)] * 2,
        flops=2**30,
        nbytes=16 * MIB,
        vmem=16,
    )(
        *(mix, assim, cot, *reversed(rim), ocol, ecol, own, other, gs, zone, st, feed, gain),
        *(kernel, turn, select, wt, spr),
    )
    rim = exchange(*rim)
    kp = call(part_body, vmem((G, Z, Z)), [vm()] * 4, flops=2**29, nbytes=5 * MIB)(
        eaten, grm, genc, prey
    )
    st = saved_start.reshape(field)
    prey, eaten, feed, gs = call(
        second_body,
        [vmem(field, BF16)] * 2 + [vmem(field), vmem((N, 128))],
        [sm()] + [vm()] * 4,
        flops=2**32,
        nbytes=16 * MIB,
    )(mix, st, turn, select, wt)
    m, ge, q, ef, send, grm, genc = call(
        last_body,
        [pltpu.HBM(field, F32)] * 2 + [pltpu.HBM((N, 128), F32)] * 2 + [vmem((2 * Z + 8, Z))] + [vmem(field, BF16)] * 2,
        [sm(), sm()] + [vm()] * 20,
        [pads]
        + [pltpu.VMEM(field, F32)] * 2
        + [pltpu.VMEM((N, 128), F32)] * 2
        + [pltpu.SemaphoreType.DMA((4,))],
        flops=2**30,
        nbytes=16 * MIB,
        vmem=16,
        out_far=4,
    )(
        *(mix, assim, cot, *reversed(rim), ocol, ecol, catch, gs, zone, st, prey, eaten, feed),
        *(turn, select, spr, near, kp, eff),
    )
    block = pl.BlockSpec((G, R, Z), lambda n: (0, n, 0))
    cells = pl.BlockSpec((R, 128), lambda n: (n, 0))
    whole = pl.BlockSpec((G, Z), lambda n: (0, 0))
    cot = pl.pallas_call(
        rest_body,
        grid=(CHUNKS,),
        out_shape=sds(field),
        in_specs=[sm(), sm(), block, block, block, cells, cells]
        + [pl.BlockSpec((G, Z, Z), lambda n: (0, 0, 0)), whole, whole]
        + [pl.BlockSpec((1, Z), lambda n: (0, 0))],
        out_specs=block,
        scratch_shapes=[pltpu.VMEM((G, R, Z), F32)] * 2 + [pltpu.VMEM((G, Z, Z), BF16)],
        compiler_params=pltpu.CompilerParams(vmem_limit_bytes=16 * MIB),
        cost_estimate=pl.CostEstimate(flops=2**30, bytes_accessed=12 * MIB, transcendentals=0),
    )(mix, assim, *map(in_hbm, (saved_start.reshape(field), m, ge, q, ef, kernel)), mortality, select, wt)
    cot = cot.reshape(G, CI, CJ, Z)

    got = lax.ppermute(send, "c", CORE)
    keep = call(keep_body, vmem((2 * Z, Z)), [vm()] * 5, flops=2**28, nbytes=4 * MIB)(
        kp, eaten, grm, genc, prey
    )
    chunks = call(merge_body, vmem((NCHIP * CH, 128)), [vm()] * 3, nbytes=2 * MIB)(keep, send, got)
    chunks = lax.all_to_all(chunks.reshape(NCHIP, 1, CH * 128), CHIPS, 0, 0, tiled=True)
    chunks = chunks.reshape(NCHIP * CH, 128)
    own, eff = call(sum_body, [vmem((NCHIP, 8, Z)), vmem((1, 128))], [vm()], nbytes=MIB)(chunks)
    own, cot = lax.optimization_barrier((own, cot))
    own = lax.all_to_all(own, CHIPS, 0, 0, tiled=True).reshape(2 * Z, Z)
    got = lax.ppermute(own, "c", CORE)
    total = call(
        join_body,
        [pltpu.HBM((G, Z, Z), F32)],
        [vm()] * 2,
        [pltpu.SemaphoreType.DMA((4,))],
        nbytes=2 * MIB,
        out_far=1,
    )(own, got)[0]
    return cot, total, eff[0, :EEZS]


def solution(mesh):
    fine = Mesh(mesh.devices.reshape(2, 4, 2, 4, 2), ("zl", "x", "c", "y", "zh"))
    field = P(None, LON, LAT, None)
    placed = (
        field,
        field,
        field,
        P(None, ALL),
        P(ALL, None),
        P(ALL),
        P(LON, LAT),
        P(LON, LAT),
    ) + (P(),) * 8
    return jax.shard_map(
        body,
        mesh=fine,
        in_specs=placed,
        out_specs=(field, P(), P()),
        check_vma=False,
    )
```

```python
import functools

import jax
import jax.numpy as jnp
from jax import lax
from jax.experimental import pallas as pl
from jax.experimental.pallas import tpu as pltpu
from jax.sharding import Mesh, PartitionSpec as P

G, Z = 4, 256
CI, CJ = 16, 32
N = CI * CJ
EEZS = 64
H = 0.5
SLOTS = 8
F32, BF16 = jnp.float32, jnp.bfloat16
LON, LAT = ("zl", "x", "c"), ("y", "zh")
ALL = LON + LAT
CHIPS = ("zl", "x", "y", "zh")
NCHIP = 64
MIB = 1024 * 1024
HI = lax.Precision.HIGHEST

LON_A = [(i, i ^ 1) for i in range(16)]
LON_B = [(i, (i + 1) % 16 if i % 2 else (i - 1) % 16) for i in range(16)]
LAT_A = [(i, i ^ 1) for i in range(8)]
LAT_B = [(i, i + 1 if i % 2 else i - 1) for i in range(1, 7)]
CORE = [(0, 1), (1, 0)]


def sds(shape, dtype=F32):
    return jax.ShapeDtypeStruct(shape, dtype)


def vmem(shape, dtype=F32):
    return pltpu.VMEM(shape, dtype)


def vm():
    return pl.BlockSpec(memory_space=pltpu.VMEM)


def sm():
    return pl.BlockSpec(memory_space=pltpu.SMEM)


def call(body, outs, ins, scratch=(), flops=0, nbytes=0, vmem=6, place=True, far=(), out_far=0, aliases={}):
    many = isinstance(outs, list)
    spots = [pl.BlockSpec(memory_space=pl.ANY) if n < out_far else vm() for n in range(len(outs) if many else 1)]
    run = pl.pallas_call(
        body,
        out_shape=outs,
        in_specs=ins,
        out_specs=spots if many else vm(),
        scratch_shapes=list(scratch),
        input_output_aliases=aliases,
        compiler_params=pltpu.CompilerParams(vmem_limit_bytes=vmem * MIB),
        cost_estimate=pl.CostEstimate(flops=flops, bytes_accessed=nbytes, transcendentals=0),
    )

    def go(*args):
        return run(
            *[
                in_hbm(a) if not place or n in far else near_core(a) if a.size >= 8192 else a
                for n, a in enumerate(args)
            ]
        )

    return go


def near_core(x):
    return pltpu.with_memory_space_constraint(x, pltpu.VMEM)


def in_hbm(x):
    return pltpu.with_memory_space_constraint(x, pltpu.HBM)


def nt(a, b, **kw):
    return lax.dot_general(a, b, (((1,), (1,)), ((), ())), preferred_element_type=F32, **kw)


def nn(a, b, **kw):
    return lax.dot_general(a, b, (((1,), (0,)), ((), ())), preferred_element_type=F32, **kw)


def tn(a, b, **kw):
    return lax.dot_general(a, b, (((0,), (0,)), ((), ())), preferred_element_type=F32, **kw)


def split(x):
    hi = x.astype(BF16).astype(F32)
    return hi, x - hi


def two(x):
    return jnp.concatenate([x, x], axis=1)


def column(row, n, width):
    eye = lax.broadcasted_iota(jnp.int32, (n, n), 0) == lax.broadcasted_iota(jnp.int32, (n, n), 1)
    col = jnp.sum(jnp.where(eye, jnp.broadcast_to(row, (n, n)), 0.0), axis=1, keepdims=True)
    return jnp.broadcast_to(col, (n, width))


def prep_body(c, ocean, cells, count, resid, la, lb, ta, tb, pay, rim_i, rim_j, sem):
    par_i, par_j = lax.axis_index("c"), lax.axis_index("zh")
    copies = [
        pltpu.make_async_copy(c.at[:, CI - 1], rim_i.at[0], sem.at[0]),
        pltpu.make_async_copy(c.at[:, 0], rim_i.at[1], sem.at[1]),
        pltpu.make_async_copy(c.at[:, :, CJ - 8 : CJ, :], rim_j.at[0], sem.at[2]),
        pltpu.make_async_copy(c.at[:, :, 0:8, :], rim_j.at[1], sem.at[3]),
    ]
    for copy in copies:
        copy.start()
    ents, rows = cells.shape
    ne = rows * ents
    devices = 2 * NCHIP
    tile_e = lax.broadcasted_iota(jnp.int32, (ents, ne), 1) // rows == lax.broadcasted_iota(
        jnp.int32, (ents, ne), 0
    )
    tile_r = lax.broadcasted_iota(jnp.int32, (rows, ne), 1) % rows == lax.broadcasted_iota(
        jnp.int32, (rows, ne), 0
    )
    tile_rf = tile_r.astype(F32)
    lon_i = (cells[...] // 256).astype(F32)
    lat_i = (cells[...] % 256).astype(F32)
    r_hi, r_rest = split(resid[...])
    r_mid, r_lo = split(r_rest)
    few = jnp.concatenate([count[...].astype(F32), r_hi, r_mid, r_lo, jnp.zeros((1, rows), F32)], axis=0)
    wide = nn(
        jnp.concatenate([lon_i, lat_i, few], axis=0).astype(BF16), tile_rf.astype(BF16)
    )

    def flat(x):
        return jnp.sum(jnp.where(tile_e, x, 0.0), axis=0, keepdims=True)

    i_row = flat(wide[:ents]).astype(jnp.int32)
    j_row = flat(wide[ents : 2 * ents]).astype(jnp.int32)
    few = wide[2 * ents :]
    n_row = few[0:1]
    r_row = few[1:3] + few[3:5] + few[5:7]
    entry = (lax.broadcasted_iota(jnp.int32, (1, ne), 1) // rows).astype(F32)
    vals = jnp.where(entry < n_row, r_row, 0.0)
    owner = (i_row // CI) * 8 + j_row // CJ
    mine = lax.broadcasted_iota(jnp.int32, (devices, ne), 0) == owner
    mine_b = mine.astype(F32).astype(BF16)
    before = (
        lax.broadcasted_iota(jnp.int32, (ne, ne), 0) < lax.broadcasted_iota(jnp.int32, (ne, ne), 1)
    )
    ahead = nn(mine_b, before.astype(F32).astype(BF16))
    rank = jnp.sum(jnp.where(mine, ahead, 0.0), axis=0, keepdims=True).astype(jnp.int32)
    slot = lax.broadcasted_iota(jnp.int32, (SLOTS, ne), 0) == rank
    h0, l0 = split(vals[0:1])
    h1, l1 = split(vals[1:2])
    a_row = ((i_row % CI) * CJ).astype(F32)
    b_row = (j_row % CJ).astype(F32)

    def rows_of(parts):
        put = [jnp.where(slot, jnp.broadcast_to(p, (SLOTS, ne)), 0.0) for p in parts]
        put.append(jnp.zeros((128 - SLOTS * len(parts), ne), F32))
        return jnp.concatenate(put, axis=0).astype(BF16)

    pay[...] = nt(mine_b, rows_of((h0, h1, a_row))) + nt(mine_b, rows_of((l0, l1, b_row)))

    oc = ocean[...].astype(F32)
    edge_i = (column(oc[CI - 1 : CI, :], CJ, Z), column(oc[0:1, :], CJ, Z))
    edge_j = (
        jnp.broadcast_to(oc[:, CJ - 1 : CJ], (CI, Z)),
        jnp.broadcast_to(oc[:, 0:1], (CI, Z)),
    )
    for copy in copies:
        copy.wait()

    def rims(odd, a, b, value):
        for n, (even_to, odd_to) in enumerate(((a, b), (b, a))):
            for g in range(G + 1):
                v = value(n, g)

                @pl.when(odd == 0)
                def _():
                    even_to[g] = v

                @pl.when(odd == 1)
                def _():
                    odd_to[g] = v

    rims(par_i, la, lb, lambda n, g: edge_i[n] if g == G else rim_i[n, g] * edge_i[n])
    rims(
        par_j,
        ta,
        tb,
        lambda n, g: edge_j[n] if g == G else rim_j[n, g, :, 7 if n == 0 else 0, :] * edge_j[n],
    )


def tables(ocean, eez, effort, ocol, ecol, zone):
    oc = ocean[...].astype(F32)
    ez = eez[...].astype(F32)
    lane = lax.broadcasted_iota(jnp.int32, (CJ, 128), 1)
    eff = jnp.concatenate([effort[...], jnp.zeros((1, 128 - EEZS), F32)], axis=1)
    for i in range(CI):
        rows = slice(i * CJ, (i + 1) * CJ)
        ocol[rows] = column(oc[i : i + 1, :], CJ, 128)
        here = (column(ez[i : i + 1, :], CJ, 128).astype(jnp.int32) == lane).astype(F32)
        zone[rows] = here.astype(BF16)
        ecol[rows] = jnp.broadcast_to(jnp.sum(here * eff, axis=1, keepdims=True), (CJ, 128))


def gather_catch(pay, hot, hi, lo):
    got = pay[...]
    flip = got.T
    for k in range(SLOTS):
        where = flip[2 * SLOTS + k : 2 * SLOTS + k + 1, :].astype(jnp.int32)
        cell = lax.broadcasted_iota(jnp.int32, (N, 128), 0)
        hot[:, k * 128 : (k + 1) * 128] = (cell == where).astype(F32).astype(BF16)
        pair = jnp.concatenate(
            [
                jnp.broadcast_to(got[:, k : k + 1], (128, 128)),
                jnp.broadcast_to(got[:, SLOTS + k : SLOTS + k + 1], (128, 128)),
            ],
            axis=1,
        )
        top, rest = split(pair)
        hi[k * 128 : (k + 1) * 128, :] = top.astype(BF16)
        lo[k * 128 : (k + 1) * 128, :] = rest.astype(BF16)
    return nn(hot[...], hi[...]) + nn(hot[...], lo[...])


def by_zone(y, zone):
    top, rest = split(y[...])
    parts = jnp.concatenate([top, rest], axis=1).astype(BF16)
    return jnp.sum(tn(parts, zone[...]), axis=0, keepdims=True)


R = 128
CHUNKS = N // R


def recip(d):
    r = pltpu.reciprocal(d, approx=True)
    return r * (2.0 - d * r)


def mixed(rows_of, mix, k, turned=False):
    tot = None
    for g in range(G):
        term = (mix[g, k] if turned else mix[k, g]) * rows_of[g]
        tot = term if tot is None else tot + term
    return tot


def gain_of(k, mix, assim, mort, sel, ef, feed, rem):
    tot = (1.0 - H * mort[k : k + 1, :]) - (H * sel[k : k + 1, :]) * ef + (H * assim[k]) * feed
    for g in range(G):
        tot = tot + (-H * mix[g, k]) * rem[g]
    return tot


def forward_rows(rows, mix, st, turn, sel, wt, prey, eaten, feed, gs):
    s = [st[k, rows, :].astype(F32) for k in range(G)]
    part = None
    for k in range(G):
        term = (sel[k : k + 1, :] * wt[...]) * s[k]
        part = term if part is None else part + term
    gs[rows, :] = part[:, :128] + part[:, 128:]
    for g in range(G):
        prey[g, rows, :] = mixed(s, mix, g).astype(BF16)
    for g in range(G):
        enc = nn(prey[g, rows, :], turn[g])
        fd = enc * recip(enc + 1.0)
        feed[g, rows, :] = fd
        eaten[g, rows, :] = (st[g, rows, :].astype(F32) * fd).astype(BF16)


def first_body(*refs):
    mix, assim, saved, c_far, ker, mort, sel, wt, ocean, eez, effort = refs[:11]
    ocol, ecol, zone, turn, st, prey, eaten, feed, gs, gain, c, rem, sem = refs[11:]
    copies = []
    for n in range(CHUNKS):
        rows = slice(n * R, (n + 1) * R)
        copies.append(pltpu.make_async_copy(saved.at[:, rows, :], st.at[:, rows, :], sem.at[n]))
        copies[-1].start()
    copies.append(pltpu.make_async_copy(c_far, c, sem.at[CHUNKS]))
    copies[-1].start()
    for g in range(G):
        turn[g] = ker[g].T
    tables(ocean, eez, effort, ocol, ecol, zone)
    for n in range(CHUNKS):
        rows = slice(n * R, (n + 1) * R)
        copies[n].wait()
        forward_rows(rows, mix, st, turn, sel, wt, prey, eaten, feed, gs)
        for g in range(G):
            rem[g, rows, :] = nn(eaten[g, rows, :], ker[g])
        parts = [rem[g, rows, :] for g in range(G)]
        ef = two(ecol[rows, :])
        for k in range(G):
            gain[k, rows, :] = gain_of(k, mix, assim, mort, sel, ef, feed[k, rows, :], parts)
    copies[CHUNKS].wait()


def second_body(mix, st, turn, sel, wt, prey, eaten, feed, gs):
    for n in range(CHUNKS):
        forward_rows(slice(n * R, (n + 1) * R), mix, st, turn, sel, wt, prey, eaten, feed, gs)


def fill(pad, opad, c, la, lb, ta, tb, ocol):
    par_i, par_j = lax.axis_index("c"), lax.axis_index("zh")
    at_a = jnp.where(par_i == 0, CI + 1, 0)
    at_b = CI + 1 - at_a
    row_a = jnp.where(par_j == 0, CJ + 8, 7)
    row_b = CJ + 15 - row_a
    for g in range(G):
        pad[g, at_a, 8 : 8 + CJ, :] = la[g]
        pad[g, at_b, 8 : 8 + CJ, :] = lb[g]
        for i in range(CI):
            pad[g, i + 1, pl.ds(row_a, 1), :] = ta[g, i : i + 1, :]
            pad[g, i + 1, pl.ds(row_b, 1), :] = tb[g, i : i + 1, :]
    if opad is not None:
        opad[at_a, 8 : 8 + CJ, :] = la[G, :, :128]
        opad[at_b, 8 : 8 + CJ, :] = lb[G, :, :128]
        for i in range(CI):
            opad[i + 1, pl.ds(row_a, 1), :] = ta[G, i : i + 1, :128]
            opad[i + 1, pl.ds(row_b, 1), :] = tb[G, i : i + 1, :128]
    for i in range(CI):
        o = ocol[i * CJ : (i + 1) * CJ, :]
        if opad is not None:
            opad[i + 1, 8 : 8 + CJ, :] = o
        for g in range(G):
            pad[g, i + 1, 8 : 8 + CJ, :] = c[g, i] * two(o)


def around(pad, i, lanes):
    return (pad[i + 2, 8 : 8 + CJ, lanes] + pad[i, 8 : 8 + CJ, lanes]) + (
        pad[i + 1, 9 : 9 + CJ, lanes] + pad[i + 1, 7 : 7 + CJ, lanes]
    )


def spread_row(i, pad, s4, mix, ocol, catch, gs, st, sel, spr, m_out, grm, y):
    rows = pl.ds(i * CJ, CJ)
    o = ocol[rows, :]
    acc = None
    for z in range(2):
        lanes = slice(z * 128, (z + 1) * 128)
        ms = []
        for g in range(G):
            mid = pad[g, i + 1, 8 : 8 + CJ, lanes]
            m = mid + spr[:, lanes] * (o * around(pad.at[g], i, lanes) - s4 * mid)
            m_out[g, rows, lanes] = m
            ms.append(m * st[g, rows, lanes].astype(F32))
            term = sel[g : g + 1, lanes] * ms[-1]
            acc = term if acc is None else acc + term
        for g in range(G):
            tot = None
            for k in range(G):
                term = (-H * mix[g, k]) * ms[k]
                tot = term if tot is None else tot + term
            grm[g, rows, lanes] = tot.astype(BF16)
    y[rows, :] = H * ((o * catch[rows, :]) * gs[rows, :] - acc)


def enc_grad(g, assim, m, s, ge, fd):
    inv = 1.0 - fd
    return (((H * assim[g]) * (m * s) + ge * s) * (inv * inv)).astype(BF16)


def adj_body(*refs):
    mix, assim, c, tb, ta, lb, la, ocol, ecol, pay, gs, zone, st, feed, gain, ker, turn, sel, wt, spr = refs[:20]
    c_out, grm, genc, eff, near, later, ola, olb, ota, otb, opad, pad, m_scr, t_scr, y, catch, hot, hi, lo = refs[20:]
    par_i, par_j = lax.axis_index("c"), lax.axis_index("zh")
    fill(pad, opad, c, la, lb, ta, tb, ocol)
    caught = gather_catch(pay, hot, hi, lo)
    later[...] = caught[:, :128]
    catch[...] = caught[:, 128:]
    for n in range(CHUNKS):
        rows = slice(n * R, (n + 1) * R)
        for i in range(n * R // CJ, (n + 1) * R // CJ):
            s4 = around(opad, i, slice(None))
            near[i * CJ : (i + 1) * CJ, :] = s4
            spread_row(i, pad, s4, mix, ocol, catch, gs, st, sel, spr, m_scr, grm, y)
        q = two(H * ocol[rows, :] * ecol[rows, :] * catch[rows, :])
        for g in range(G):
            ge = nn(grm[g, rows, :], turn[g])
            m, fd = m_scr[g, rows, :], feed[g, rows, :]
            genc[g, rows, :] = enc_grad(g, assim, m, st[g, rows, :].astype(F32), ge, fd)
            m_scr[g, rows, :] = m * gain[g, rows, :] + ge * fd + q * (sel[g : g + 1, :] * wt[...])
        for g in range(G):
            t_scr[g, rows, :] = nn(genc[g, rows, :], ker[g])
        for i in range(n * R // CJ, (n + 1) * R // CJ):
            here = slice(i * CJ, (i + 1) * CJ)
            gp = [t_scr[g, here, :] for g in range(G)]
            for k in range(G):
                c_out[k, i] = m_scr[k, here, :] + mixed(gp, mix, k, True)
    eff[...] = jnp.broadcast_to(by_zone(y, zone), (8, 128))

    def lon_rims(hi, lo):
        for g in range(G):
            hi[g] = c_out[g, CI - 1] * two(ocol[N - CJ : N, :])
            lo[g] = c_out[g, 0] * two(ocol[0:CJ, :])

    def lat_rims(hi, lo):
        for g in range(G):
            for i in range(CI):
                at = i * CJ
                hi[g, i : i + 1, :] = c_out[g, i, CJ - 1 : CJ, :] * two(ocol[at + CJ - 1 : at + CJ, :])
                lo[g, i : i + 1, :] = c_out[g, i, 0:1, :] * two(ocol[at : at + 1, :])

    pl.when(par_i == 0)(lambda: lon_rims(ola, olb))
    pl.when(par_i == 1)(lambda: lon_rims(olb, ola))
    pl.when(par_j == 0)(lambda: lat_rims(ota, otb))
    pl.when(par_j == 1)(lambda: lat_rims(otb, ota))


def part_body(eaten, grm, genc, prey, kp):
    for g in range(G):
        kp[g] = tn(eaten[g], grm[g]) + tn(genc[g], prey[g])


def kernel_half(dst, half, kp, eaten, grm, genc, prey):
    for s in range(2):
        g = 2 * half + s
        dst[s * Z : (s + 1) * Z, :] = kp[g] + tn(eaten[g], grm[g]) + tn(genc[g], prey[g])


def keep_body(kp, eaten, grm, genc, prey, keep):
    kernel_half(keep, lax.axis_index("c"), kp, eaten, grm, genc, prey)


def last_body(*refs):
    mix, assim, c, tb, ta, lb, la, ocol, ecol, catch, gs, zone, st, prey, eaten, feed, turn, sel, spr, near, kp, eff = refs[:22]
    m_hbm, ge_hbm, q_hbm, e_hbm, send, grm, genc, pad, m_scr, ge_scr, y, q_scr, sem = refs[22:]
    core = lax.axis_index("c")
    fill(pad, None, c, la, lb, ta, tb, ocol)
    q_scr[...] = H * ocol[...] * ecol[...] * catch[...]
    copies = [
        pltpu.make_async_copy(q_scr, q_hbm, sem.at[0]),
        pltpu.make_async_copy(ecol, e_hbm, sem.at[1]),
    ]
    for copy in copies:
        copy.start()

    @pl.loop(0, CI)
    def _(i):
        s4 = near[pl.ds(i * CJ, CJ), :]
        spread_row(i, pad, s4, mix, ocol, catch, gs, st, sel, spr, m_scr, grm, y)

    copies.append(pltpu.make_async_copy(m_scr, m_hbm, sem.at[2]))
    copies[-1].start()
    for g in range(G):
        ge_scr[g] = nn(grm[g], turn[g])
    copies.append(pltpu.make_async_copy(ge_scr, ge_hbm, sem.at[3]))
    copies[-1].start()

    @pl.loop(0, CI)
    def _(i):
        rows = pl.ds(i * CJ, CJ)
        for g in range(G):
            genc[g, rows, :] = enc_grad(
                g,
                assim,
                m_scr[g, rows, :],
                st[g, rows, :].astype(F32),
                ge_scr[g, rows, :],
                feed[g, rows, :],
            )

    send[2 * Z :, :] = two(eff[...] + by_zone(y, zone))
    kernel_half(send, 1 - core, kp, eaten, grm, genc, prey)
    for copy in copies:
        copy.wait()


def rest_body(mix, assim, saved, m_in, ge_in, q_in, ecol, ker, mort, sel, wt, out, feed, rem, turn):
    @pl.when(pl.program_id(0) == 0)
    def _():
        for g in range(G):
            turn[g] = ker[g].T

    s = [saved[k].astype(F32) for k in range(G)]
    for g in range(G):
        enc = nn(mixed(s, mix, g).astype(BF16), turn[g])
        fd = enc * recip(enc + 1.0)
        feed[g] = fd
        rem[g] = nn((s[g] * fd).astype(BF16), ker[g])
    parts = [rem[g] for g in range(G)]
    ef, q = two(ecol[...]), two(q_in[...])
    for k in range(G):
        fd = feed[k]
        gain = gain_of(k, mix, assim, mort, sel, ef, fd, parts)
        out[k] = m_in[k] * gain + ge_in[k] * fd + q * (sel[k : k + 1, :] * wt[...])
    for g in range(G):
        rem[g] = nn(enc_grad(g, assim, m_in[g], saved[g].astype(F32), ge_in[g], feed[g]), ker[g])
    parts = [rem[g] for g in range(G)]
    for k in range(G):
        out[k] = out[k] + mixed(parts, mix, k, True)


CH = 17


def merge_body(keep, send, got, out):
    eff = send[2 * Z : 2 * Z + 1, :128] + got[2 * Z : 2 * Z + 1, :128]
    for p in range(NCHIP):
        rows = slice(p * 8, p * 8 + 8)
        tot = keep[rows, :] + got[rows, :]
        out[p * CH : p * CH + 8, :] = tot[:, :128]
        out[p * CH + 8 : p * CH + 16, :] = tot[:, 128:]
        out[p * CH + 16 : p * CH + 17, :] = eff


def sum_body(parts, out, eff):
    tot = [None, None, None]
    for p in range(NCHIP):
        new = (
            parts[p * CH : p * CH + 8, :],
            parts[p * CH + 8 : p * CH + 16, :],
            parts[p * CH + 16 : p * CH + 17, :],
        )
        tot = [n if o is None else o + n for o, n in zip(tot, new)]
    both = jnp.concatenate(tot[:2], axis=1)
    eff[...] = tot[2]
    for p in range(NCHIP):
        out[p] = both


def place_half(half, src, out, sem):
    copies = []
    for s in range(2):
        copies.append(
            pltpu.make_async_copy(src.at[s * Z : (s + 1) * Z, :], out.at[2 * half + s], sem.at[s])
        )
        copies[-1].start()
    for copy in copies:
        copy.wait()


def own_body(own, out, sem):
    place_half(lax.axis_index("c"), own, out, sem)


def other_body(got, _, out, sem):
    place_half(1 - lax.axis_index("c"), got, out, sem)


def exchange(la, lb, ta, tb):
    tb = lax.ppermute(tb, LAT, LAT_B)
    ta = lax.ppermute(ta, LAT, LAT_A)
    lb = lax.ppermute(lb, LON, LON_B)
    la = lax.ppermute(la, LON, LON_A)
    return la, lb, ta, tb


def body(
    final_cotangent,
    saved_start,
    saved_middle,
    residuals,
    row_cells,
    row_count,
    ocean_mask,
    cell_eez,
    effort,
    kernel,
    mix,
    assim,
    mortality,
    select,
    weight,
    spread,
):
    wt, spr = weight.reshape(1, Z), spread.reshape(1, Z)
    any_ = pl.BlockSpec(memory_space=pl.ANY)
    field = (G, N, Z)
    rims = [vmem((G + 1, CJ, Z))] * 2 + [vmem((G + 1, CI, Z))] * 2
    *rim, pay = call(
        prep_body,
        rims + [vmem((2 * NCHIP, 128))],
        [any_] + [vm()] * 4,
        [
            pltpu.VMEM((2, G, CJ, Z), F32),
            pltpu.VMEM((2, G, CI, 8, Z), F32),
            pltpu.SemaphoreType.DMA((4,)),
        ],
        flops=2**27,
        nbytes=3 * MIB,
        place=False,
    )(final_cotangent, ocean_mask, row_cells.T, row_count.reshape(1, -1), residuals)
    rim = exchange(*rim)
    pay = lax.all_to_all(pay, ALL, 0, 0, tiled=True)
    pay, middle = lax.optimization_barrier((pay, saved_middle))

    ocol, ecol, zone, turn, st, prey, eaten, feed, gs, gain, cot = call(
        first_body,
        [vmem((N, 128))] * 2
        + [vmem((N, 128), BF16), vmem((G, Z, Z), BF16)]
        + [vmem(field, BF16)] * 3
        + [vmem(field), vmem((N, 128)), vmem(field), vmem((G, CI, CJ, Z))],
        [sm(), sm(), any_, any_] + [vm()] * 7,
        [pltpu.VMEM(field, F32), pltpu.SemaphoreType.DMA((CHUNKS + 1,))],
        flops=2**32,
        nbytes=16 * MIB,
        vmem=8,
        far=(2, 3),
    )(
        *(mix, assim, middle.reshape(field), final_cotangent, kernel, mortality, select, wt),
        *(ocean_mask, cell_eez, effort.reshape(1, EEZS)),
    )
    pads = pltpu.VMEM((G, CI + 2, CJ + 16, Z), F32)
    cot, grm, genc, eff, near, catch, *rim = call(
        adj_body,
        [vmem((G, CI, CJ, Z))]
        + [vmem(field, BF16)] * 2
        + [vmem((8, 128)), vmem((N, 128)), vmem((N, 128))]
        + [vmem((G, CJ, Z))] * 2
        + [vmem((G, CI, Z))] * 2,
        [sm(), sm()] + [vm()] * 18,
        [pltpu.VMEM((CI + 2, CJ + 16, 128), F32), pads]
        + [pltpu.VMEM(field, F32)] * 2
        + [pltpu.VMEM((N, 128), F32)] * 2
        + [pltpu.VMEM((N, SLOTS * 128), BF16)]
        + [pltpu.VMEM((SLOTS * 128, 256), BF16)] * 2,
        flops=2**30,
        nbytes=16 * MIB,
        vmem=16,
    )(
        *(mix, assim, cot, *reversed(rim), ocol, ecol, pay, gs, zone, st, feed, gain),
        *(kernel, turn, select, wt, spr),
    )
    rim = exchange(*rim)
    kp = call(part_body, vmem((G, Z, Z)), [vm()] * 4, flops=2**29, nbytes=5 * MIB)(
        eaten, grm, genc, prey
    )
    st = saved_start.reshape(field)
    prey, eaten, feed, gs = call(
        second_body,
        [vmem(field, BF16)] * 2 + [vmem(field), vmem((N, 128))],
        [sm()] + [vm()] * 4,
        flops=2**32,
        nbytes=16 * MIB,
    )(mix, st, turn, select, wt)
    m, ge, q, ef, send, grm, genc = call(
        last_body,
        [pltpu.HBM(field, F32)] * 2 + [pltpu.HBM((N, 128), F32)] * 2 + [vmem((2 * Z + 8, Z))] + [vmem(field, BF16)] * 2,
        [sm(), sm()] + [vm()] * 20,
        [pads]
        + [pltpu.VMEM(field, F32)] * 2
        + [pltpu.VMEM((N, 128), F32)] * 2
        + [pltpu.SemaphoreType.DMA((4,))],
        flops=2**30,
        nbytes=16 * MIB,
        vmem=16,
        out_far=4,
    )(
        *(mix, assim, cot, *reversed(rim), ocol, ecol, catch, gs, zone, st, prey, eaten, feed),
        *(turn, select, spr, near, kp, eff),
    )
    block = pl.BlockSpec((G, R, Z), lambda n: (0, n, 0))
    cells = pl.BlockSpec((R, 128), lambda n: (n, 0))
    whole = pl.BlockSpec((G, Z), lambda n: (0, 0))
    cot = pl.pallas_call(
        rest_body,
        grid=(CHUNKS,),
        out_shape=sds(field),
        in_specs=[sm(), sm(), block, block, block, cells, cells]
        + [pl.BlockSpec((G, Z, Z), lambda n: (0, 0, 0)), whole, whole]
        + [pl.BlockSpec((1, Z), lambda n: (0, 0))],
        out_specs=block,
        scratch_shapes=[pltpu.VMEM((G, R, Z), F32)] * 2 + [pltpu.VMEM((G, Z, Z), BF16)],
        compiler_params=pltpu.CompilerParams(vmem_limit_bytes=16 * MIB),
        cost_estimate=pl.CostEstimate(flops=2**30, bytes_accessed=12 * MIB, transcendentals=0),
    )(mix, assim, *map(in_hbm, (saved_start.reshape(field), m, ge, q, ef, kernel)), mortality, select, wt)
    cot = cot.reshape(G, CI, CJ, Z)

    got = lax.ppermute(send, "c", CORE)
    keep = call(keep_body, vmem((2 * Z, Z)), [vm()] * 5, flops=2**28, nbytes=4 * MIB)(
        kp, eaten, grm, genc, prey
    )
    chunks = call(merge_body, vmem((NCHIP * CH, 128)), [vm()] * 3, nbytes=2 * MIB)(keep, send, got)
    chunks = lax.all_to_all(chunks.reshape(NCHIP, 1, CH * 128), CHIPS, 0, 0, tiled=True)
    chunks = chunks.reshape(NCHIP * CH, 128)
    own, eff = call(sum_body, [vmem((NCHIP, 8, Z)), vmem((1, 128))], [vm()], nbytes=MIB)(chunks)
    own, cot = lax.optimization_barrier((own, cot))
    own = lax.all_to_all(own, CHIPS, 0, 0, tiled=True).reshape(2 * Z, Z)
    got = lax.ppermute(own, "c", CORE)
    whole = [pltpu.HBM((G, Z, Z), F32)]
    sems = [pltpu.SemaphoreType.DMA((2,))]
    total = call(own_body, whole, [vm()], sems, nbytes=MIB, out_far=1)(own)[0]
    total = call(
        other_body, whole, [vm(), any_], sems, nbytes=MIB, out_far=1, far=(1,), aliases={1: 0}
    )(got, total)[0]
    return cot, total, eff[0, :EEZS]


def solution(mesh):
    fine = Mesh(mesh.devices.reshape(2, 4, 2, 4, 2), ("zl", "x", "c", "y", "zh"))
    field = P(None, LON, LAT, None)
    placed = (
        field,
        field,
        field,
        P(None, ALL),
        P(ALL, None),
        P(ALL),
        P(LON, LAT),
        P(LON, LAT),
    ) + (P(),) * 8
    return jax.shard_map(
        body,
        mesh=fine,
        in_specs=placed,
        out_specs=(field, P(), P()),
        check_vma=False,
    )
```

```python
import functools

import jax
import jax.numpy as jnp
from jax import lax
from jax.experimental import pallas as pl
from jax.experimental.pallas import tpu as pltpu
from jax.sharding import Mesh, PartitionSpec as P

G, Z = 4, 256
CI, CJ = 16, 32
N = CI * CJ
EEZS = 64
H = 0.5
SLOTS = 8
F32, BF16 = jnp.float32, jnp.bfloat16
LON, LAT = ("zl", "x", "c"), ("y", "zh")
ALL = LON + LAT
CHIPS = ("zl", "x", "y", "zh")
NCHIP = 64
MIB = 1024 * 1024
HI = lax.Precision.HIGHEST

LON_A = [(i, i ^ 1) for i in range(16)]
LON_B = [(i, (i + 1) % 16 if i % 2 else (i - 1) % 16) for i in range(16)]
LAT_A = [(i, i ^ 1) for i in range(8)]
LAT_B = [(i, i + 1 if i % 2 else i - 1) for i in range(1, 7)]
CORE = [(0, 1), (1, 0)]


def sds(shape, dtype=F32):
    return jax.ShapeDtypeStruct(shape, dtype)


def vmem(shape, dtype=F32):
    return pltpu.VMEM(shape, dtype)


def vm():
    return pl.BlockSpec(memory_space=pltpu.VMEM)


def sm():
    return pl.BlockSpec(memory_space=pltpu.SMEM)


def call(body, outs, ins, scratch=(), flops=0, nbytes=0, vmem=6, place=True, far=(), out_far=0, aliases={}):
    many = isinstance(outs, list)
    spots = [pl.BlockSpec(memory_space=pl.ANY) if n < out_far else vm() for n in range(len(outs) if many else 1)]
    run = pl.pallas_call(
        body,
        out_shape=outs,
        in_specs=ins,
        out_specs=spots if many else vm(),
        scratch_shapes=list(scratch),
        input_output_aliases=aliases,
        compiler_params=pltpu.CompilerParams(vmem_limit_bytes=vmem * MIB),
        cost_estimate=pl.CostEstimate(flops=flops, bytes_accessed=nbytes, transcendentals=0),
    )

    def go(*args):
        return run(
            *[
                in_hbm(a) if not place or n in far else near_core(a) if a.size >= 8192 else a
                for n, a in enumerate(args)
            ]
        )

    return go


def near_core(x):
    return pltpu.with_memory_space_constraint(x, pltpu.VMEM)


def in_hbm(x):
    return pltpu.with_memory_space_constraint(x, pltpu.HBM)


def nt(a, b, **kw):
    return lax.dot_general(a, b, (((1,), (1,)), ((), ())), preferred_element_type=F32, **kw)


def nn(a, b, **kw):
    return lax.dot_general(a, b, (((1,), (0,)), ((), ())), preferred_element_type=F32, **kw)


def tn(a, b, **kw):
    return lax.dot_general(a, b, (((0,), (0,)), ((), ())), preferred_element_type=F32, **kw)


def split(x):
    hi = x.astype(BF16).astype(F32)
    return hi, x - hi


def two(x):
    return jnp.concatenate([x, x], axis=1)


def column(row, n, width):
    eye = lax.broadcasted_iota(jnp.int32, (n, n), 0) == lax.broadcasted_iota(jnp.int32, (n, n), 1)
    col = jnp.sum(jnp.where(eye, jnp.broadcast_to(row, (n, n)), 0.0), axis=1, keepdims=True)
    return jnp.broadcast_to(col, (n, width))


def prep_body(c, ocean, cells, count, resid, la, lb, ta, tb, pay, rim_i, rim_j, sem):
    par_i, par_j = lax.axis_index("c"), lax.axis_index("zh")
    copies = [
        pltpu.make_async_copy(c.at[:, CI - 1], rim_i.at[0], sem.at[0]),
        pltpu.make_async_copy(c.at[:, 0], rim_i.at[1], sem.at[1]),
        pltpu.make_async_copy(c.at[:, :, CJ - 8 : CJ, :], rim_j.at[0], sem.at[2]),
        pltpu.make_async_copy(c.at[:, :, 0:8, :], rim_j.at[1], sem.at[3]),
    ]
    for copy in copies:
        copy.start()
    ents, rows = cells.shape
    ne = rows * ents
    devices = 2 * NCHIP
    tile_e = lax.broadcasted_iota(jnp.int32, (ents, ne), 1) // rows == lax.broadcasted_iota(
        jnp.int32, (ents, ne), 0
    )
    tile_r = lax.broadcasted_iota(jnp.int32, (rows, ne), 1) % rows == lax.broadcasted_iota(
        jnp.int32, (rows, ne), 0
    )
    tile_rf = tile_r.astype(F32)
    lon_i = (cells[...] // 256).astype(F32)
    lat_i = (cells[...] % 256).astype(F32)
    r_hi, r_rest = split(resid[...])
    r_mid, r_lo = split(r_rest)
    few = jnp.concatenate([count[...].astype(F32), r_hi, r_mid, r_lo, jnp.zeros((1, rows), F32)], axis=0)
    wide = nn(
        jnp.concatenate([lon_i, lat_i, few], axis=0).astype(BF16), tile_rf.astype(BF16)
    )

    def flat(x):
        return jnp.sum(jnp.where(tile_e, x, 0.0), axis=0, keepdims=True)

    i_row = flat(wide[:ents]).astype(jnp.int32)
    j_row = flat(wide[ents : 2 * ents]).astype(jnp.int32)
    few = wide[2 * ents :]
    n_row = few[0:1]
    r_row = few[1:3] + few[3:5] + few[5:7]
    entry = (lax.broadcasted_iota(jnp.int32, (1, ne), 1) // rows).astype(F32)
    vals = jnp.where(entry < n_row, r_row, 0.0)
    owner = (i_row // CI) * 8 + j_row // CJ
    mine = lax.broadcasted_iota(jnp.int32, (devices, ne), 0) == owner
    mine_b = mine.astype(F32).astype(BF16)
    before = (
        lax.broadcasted_iota(jnp.int32, (ne, ne), 0) < lax.broadcasted_iota(jnp.int32, (ne, ne), 1)
    )
    ahead = nn(mine_b, before.astype(F32).astype(BF16))
    rank = jnp.sum(jnp.where(mine, ahead, 0.0), axis=0, keepdims=True).astype(jnp.int32)
    slot = lax.broadcasted_iota(jnp.int32, (SLOTS, ne), 0) == rank
    h0, l0 = split(vals[0:1])
    h1, l1 = split(vals[1:2])
    a_row = ((i_row % CI) * CJ).astype(F32)
    b_row = (j_row % CJ).astype(F32)

    def rows_of(parts):
        put = [jnp.where(slot, jnp.broadcast_to(p, (SLOTS, ne)), 0.0) for p in parts]
        put.append(jnp.zeros((128 - SLOTS * len(parts), ne), F32))
        return jnp.concatenate(put, axis=0).astype(BF16)

    pay[...] = nt(mine_b, rows_of((h0, h1, a_row))) + nt(mine_b, rows_of((l0, l1, b_row)))

    oc = ocean[...].astype(F32)
    edge_i = (column(oc[CI - 1 : CI, :], CJ, Z), column(oc[0:1, :], CJ, Z))
    edge_j = (
        jnp.broadcast_to(oc[:, CJ - 1 : CJ], (CI, Z)),
        jnp.broadcast_to(oc[:, 0:1], (CI, Z)),
    )
    for copy in copies:
        copy.wait()

    def rims(odd, a, b, value):
        for n, (even_to, odd_to) in enumerate(((a, b), (b, a))):
            for g in range(G + 1):
                v = value(n, g)

                @pl.when(odd == 0)
                def _():
                    even_to[g] = v

                @pl.when(odd == 1)
                def _():
                    odd_to[g] = v

    rims(par_i, la, lb, lambda n, g: edge_i[n] if g == G else rim_i[n, g] * edge_i[n])
    rims(
        par_j,
        ta,
        tb,
        lambda n, g: edge_j[n] if g == G else rim_j[n, g, :, 7 if n == 0 else 0, :] * edge_j[n],
    )


def tables(ocean, eez, effort, ocol, ecol, zone):
    oc = ocean[...].astype(F32)
    ez = eez[...].astype(F32)
    lane = lax.broadcasted_iota(jnp.int32, (CJ, 128), 1)
    eff = jnp.concatenate([effort[...], jnp.zeros((1, 128 - EEZS), F32)], axis=1)
    for i in range(CI):
        rows = slice(i * CJ, (i + 1) * CJ)
        ocol[rows] = column(oc[i : i + 1, :], CJ, 128)
        here = (column(ez[i : i + 1, :], CJ, 128).astype(jnp.int32) == lane).astype(F32)
        zone[rows] = here.astype(BF16)
        ecol[rows] = jnp.broadcast_to(jnp.sum(here * eff, axis=1, keepdims=True), (CJ, 128))


def gather_catch(pay, hot, hi, lo):
    got = pay[...]
    flip = got.T
    for k in range(SLOTS):
        where = flip[2 * SLOTS + k : 2 * SLOTS + k + 1, :].astype(jnp.int32)
        cell = lax.broadcasted_iota(jnp.int32, (N, 128), 0)
        hot[:, k * 128 : (k + 1) * 128] = (cell == where).astype(F32).astype(BF16)
        pair = jnp.concatenate(
            [
                jnp.broadcast_to(got[:, k : k + 1], (128, 128)),
                jnp.broadcast_to(got[:, SLOTS + k : SLOTS + k + 1], (128, 128)),
            ],
            axis=1,
        )
        top, rest = split(pair)
        hi[k * 128 : (k + 1) * 128, :] = top.astype(BF16)
        lo[k * 128 : (k + 1) * 128, :] = rest.astype(BF16)
    return nn(hot[...], hi[...]) + nn(hot[...], lo[...])


def by_zone(y, zone):
    top, rest = split(y[...])
    parts = jnp.concatenate([top, rest], axis=1).astype(BF16)
    return jnp.sum(tn(parts, zone[...]), axis=0, keepdims=True)


R = 128
CHUNKS = N // R


def recip(d):
    r = pltpu.reciprocal(d, approx=True)
    return r * (2.0 - d * r)


def mixed(rows_of, mix, k, turned=False):
    tot = None
    for g in range(G):
        term = (mix[g, k] if turned else mix[k, g]) * rows_of[g]
        tot = term if tot is None else tot + term
    return tot


def gain_of(k, mix, assim, mort, sel, ef, feed, rem):
    tot = (1.0 - H * mort[k : k + 1, :]) - (H * sel[k : k + 1, :]) * ef + (H * assim[k]) * feed
    for g in range(G):
        tot = tot + (-H * mix[g, k]) * rem[g]
    return tot


def forward_rows(rows, mix, st, turn, sel, wt, prey, eaten, feed, gs):
    s = [st[k, rows, :].astype(F32) for k in range(G)]
    part = None
    for k in range(G):
        term = (sel[k : k + 1, :] * wt[...]) * s[k]
        part = term if part is None else part + term
    gs[rows, :] = part[:, :128] + part[:, 128:]
    for g in range(G):
        prey[g, rows, :] = mixed(s, mix, g).astype(BF16)
    for g in range(G):
        enc = nn(prey[g, rows, :], turn[g])
        fd = enc * recip(enc + 1.0)
        feed[g, rows, :] = fd
        eaten[g, rows, :] = (st[g, rows, :].astype(F32) * fd).astype(BF16)


def first_body(*refs):
    mix, assim, saved, c_far, ker, mort, sel, wt, ocean, eez, effort = refs[:11]
    ocol, ecol, zone, turn, st, prey, eaten, feed, gs, gain, c, rem, sem = refs[11:]
    copies = []
    for n in range(CHUNKS):
        rows = slice(n * R, (n + 1) * R)
        copies.append(pltpu.make_async_copy(saved.at[:, rows, :], st.at[:, rows, :], sem.at[n]))
        copies[-1].start()
    copies.append(pltpu.make_async_copy(c_far, c, sem.at[CHUNKS]))
    copies[-1].start()
    for g in range(G):
        turn[g] = ker[g].T
    tables(ocean, eez, effort, ocol, ecol, zone)
    for n in range(CHUNKS):
        rows = slice(n * R, (n + 1) * R)
        copies[n].wait()
        forward_rows(rows, mix, st, turn, sel, wt, prey, eaten, feed, gs)
        for g in range(G):
            rem[g, rows, :] = nn(eaten[g, rows, :], ker[g])
        parts = [rem[g, rows, :] for g in range(G)]
        ef = two(ecol[rows, :])
        for k in range(G):
            gain[k, rows, :] = gain_of(k, mix, assim, mort, sel, ef, feed[k, rows, :], parts)
    copies[CHUNKS].wait()


def second_body(mix, st, turn, sel, wt, prey, eaten, feed, gs):
    for n in range(CHUNKS):
        forward_rows(slice(n * R, (n + 1) * R), mix, st, turn, sel, wt, prey, eaten, feed, gs)


def fill(pad, opad, c, la, lb, ta, tb, ocol):
    par_i, par_j = lax.axis_index("c"), lax.axis_index("zh")
    at_a = jnp.where(par_i == 0, CI + 1, 0)
    at_b = CI + 1 - at_a
    row_a = jnp.where(par_j == 0, CJ + 8, 7)
    row_b = CJ + 15 - row_a
    for g in range(G):
        pad[g, at_a, 8 : 8 + CJ, :] = la[g]
        pad[g, at_b, 8 : 8 + CJ, :] = lb[g]
        for i in range(CI):
            pad[g, i + 1, pl.ds(row_a, 1), :] = ta[g, i : i + 1, :]
            pad[g, i + 1, pl.ds(row_b, 1), :] = tb[g, i : i + 1, :]
    if opad is not None:
        opad[at_a, 8 : 8 + CJ, :] = la[G, :, :128]
        opad[at_b, 8 : 8 + CJ, :] = lb[G, :, :128]
        for i in range(CI):
            opad[i + 1, pl.ds(row_a, 1), :] = ta[G, i : i + 1, :128]
            opad[i + 1, pl.ds(row_b, 1), :] = tb[G, i : i + 1, :128]
    for i in range(CI):
        o = ocol[i * CJ : (i + 1) * CJ, :]
        if opad is not None:
            opad[i + 1, 8 : 8 + CJ, :] = o
        for g in range(G):
            pad[g, i + 1, 8 : 8 + CJ, :] = c[g, i] * two(o)


def around(pad, i, lanes):
    return (pad[i + 2, 8 : 8 + CJ, lanes] + pad[i, 8 : 8 + CJ, lanes]) + (
        pad[i + 1, 9 : 9 + CJ, lanes] + pad[i + 1, 7 : 7 + CJ, lanes]
    )


def spread_row(i, pad, s4, mix, ocol, catch, gs, st, sel, spr, m_out, grm, y):
    rows = pl.ds(i * CJ, CJ)
    o = ocol[rows, :]
    acc = None
    for z in range(2):
        lanes = slice(z * 128, (z + 1) * 128)
        ms = []
        for g in range(G):
            mid = pad[g, i + 1, 8 : 8 + CJ, lanes]
            m = mid + spr[:, lanes] * (o * around(pad.at[g], i, lanes) - s4 * mid)
            m_out[g, rows, lanes] = m
            ms.append(m * st[g, rows, lanes].astype(F32))
            term = sel[g : g + 1, lanes] * ms[-1]
            acc = term if acc is None else acc + term
        for g in range(G):
            tot = None
            for k in range(G):
                term = (-H * mix[g, k]) * ms[k]
                tot = term if tot is None else tot + term
            grm[g, rows, lanes] = tot.astype(BF16)
    y[rows, :] = H * ((o * catch[rows, :]) * gs[rows, :] - acc)


def enc_grad(g, assim, m, s, ge, fd):
    inv = 1.0 - fd
    return (((H * assim[g]) * (m * s) + ge * s) * (inv * inv)).astype(BF16)


def adj_body(*refs):
    mix, assim, c, la, lb, ta, tb, ocol, ecol, pay, gs, zone, st, feed, gain, ker, turn, sel, wt, spr = refs[:20]
    c_out, grm, genc, eff, near, later, ola, olb, ota, otb, opad, pad, m_scr, t_scr, y, catch, hot, hi, lo = refs[20:]
    par_i, par_j = lax.axis_index("c"), lax.axis_index("zh")
    fill(pad, opad, c, la, lb, ta, tb, ocol)
    caught = gather_catch(pay, hot, hi, lo)
    later[...] = caught[:, :128]
    catch[...] = caught[:, 128:]
    for n in range(CHUNKS):
        rows = slice(n * R, (n + 1) * R)
        for i in range(n * R // CJ, (n + 1) * R // CJ):
            s4 = around(opad, i, slice(None))
            near[i * CJ : (i + 1) * CJ, :] = s4
            spread_row(i, pad, s4, mix, ocol, catch, gs, st, sel, spr, m_scr, grm, y)
        q = two(H * ocol[rows, :] * ecol[rows, :] * catch[rows, :])
        for g in range(G):
            ge = nn(grm[g, rows, :], turn[g])
            m, fd = m_scr[g, rows, :], feed[g, rows, :]
            genc[g, rows, :] = enc_grad(g, assim, m, st[g, rows, :].astype(F32), ge, fd)
            m_scr[g, rows, :] = m * gain[g, rows, :] + ge * fd + q * (sel[g : g + 1, :] * wt[...])
        for g in range(G):
            t_scr[g, rows, :] = nn(genc[g, rows, :], ker[g])
        for i in range(n * R // CJ, (n + 1) * R // CJ):
            here = slice(i * CJ, (i + 1) * CJ)
            gp = [t_scr[g, here, :] for g in range(G)]
            for k in range(G):
                c_out[k, i] = m_scr[k, here, :] + mixed(gp, mix, k, True)
    eff[...] = jnp.broadcast_to(by_zone(y, zone), (8, 128))

    def lon_rims(hi, lo):
        for g in range(G):
            hi[g] = c_out[g, CI - 1] * two(ocol[N - CJ : N, :])
            lo[g] = c_out[g, 0] * two(ocol[0:CJ, :])

    def lat_rims(hi, lo):
        for g in range(G):
            for i in range(CI):
                at = i * CJ
                hi[g, i : i + 1, :] = c_out[g, i, CJ - 1 : CJ, :] * two(ocol[at + CJ - 1 : at + CJ, :])
                lo[g, i : i + 1, :] = c_out[g, i, 0:1, :] * two(ocol[at : at + 1, :])

    pl.when(par_i == 0)(lambda: lon_rims(ola, olb))
    pl.when(par_i == 1)(lambda: lon_rims(olb, ola))
    pl.when(par_j == 0)(lambda: lat_rims(ota, otb))
    pl.when(par_j == 1)(lambda: lat_rims(otb, ota))


def part_body(eaten, grm, genc, prey, kp):
    for g in range(G):
        kp[g] = tn(eaten[g], grm[g]) + tn(genc[g], prey[g])


def kernel_half(dst, half, kp, eaten, grm, genc, prey):
    for s in range(2):
        g = 2 * half + s
        dst[s * Z : (s + 1) * Z, :] = kp[g] + tn(eaten[g], grm[g]) + tn(genc[g], prey[g])


def keep_body(kp, eaten, grm, genc, prey, keep):
    kernel_half(keep, lax.axis_index("c"), kp, eaten, grm, genc, prey)


def last_body(*refs):
    mix, assim, c, la, lb, ta, tb, ocol, ecol, catch, gs, zone, st, prey, eaten, feed, turn, sel, spr, near, kp, eff = refs[:22]
    m_hbm, ge_hbm, q_hbm, e_hbm, send, grm, genc, pad, m_scr, ge_scr, y, q_scr, sem = refs[22:]
    core = lax.axis_index("c")
    fill(pad, None, c, la, lb, ta, tb, ocol)
    q_scr[...] = H * ocol[...] * ecol[...] * catch[...]
    copies = [
        pltpu.make_async_copy(q_scr, q_hbm, sem.at[0]),
        pltpu.make_async_copy(ecol, e_hbm, sem.at[1]),
    ]
    for copy in copies:
        copy.start()

    @pl.loop(0, CI)
    def _(i):
        s4 = near[pl.ds(i * CJ, CJ), :]
        spread_row(i, pad, s4, mix, ocol, catch, gs, st, sel, spr, m_scr, grm, y)

    copies.append(pltpu.make_async_copy(m_scr, m_hbm, sem.at[2]))
    copies[-1].start()
    for g in range(G):
        ge_scr[g] = nn(grm[g], turn[g])
    copies.append(pltpu.make_async_copy(ge_scr, ge_hbm, sem.at[3]))
    copies[-1].start()

    @pl.loop(0, CI)
    def _(i):
        rows = pl.ds(i * CJ, CJ)
        for g in range(G):
            genc[g, rows, :] = enc_grad(
                g,
                assim,
                m_scr[g, rows, :],
                st[g, rows, :].astype(F32),
                ge_scr[g, rows, :],
                feed[g, rows, :],
            )

    send[2 * Z :, :] = two(eff[...] + by_zone(y, zone))
    kernel_half(send, 1 - core, kp, eaten, grm, genc, prey)
    for copy in copies:
        copy.wait()


def rest_body(mix, assim, saved, m_in, ge_in, q_in, ecol, ker, mort, sel, wt, out, feed, rem, turn):
    @pl.when(pl.program_id(0) == 0)
    def _():
        for g in range(G):
            turn[g] = ker[g].T

    s = [saved[k].astype(F32) for k in range(G)]
    for g in range(G):
        enc = nn(mixed(s, mix, g).astype(BF16), turn[g])
        fd = enc * recip(enc + 1.0)
        feed[g] = fd
        rem[g] = nn((s[g] * fd).astype(BF16), ker[g])
    parts = [rem[g] for g in range(G)]
    ef, q = two(ecol[...]), two(q_in[...])
    for k in range(G):
        fd = feed[k]
        gain = gain_of(k, mix, assim, mort, sel, ef, fd, parts)
        out[k] = m_in[k] * gain + ge_in[k] * fd + q * (sel[k : k + 1, :] * wt[...])
    for g in range(G):
        rem[g] = nn(enc_grad(g, assim, m_in[g], saved[g].astype(F32), ge_in[g], feed[g]), ker[g])
    parts = [rem[g] for g in range(G)]
    for k in range(G):
        out[k] = out[k] + mixed(parts, mix, k, True)


CH = 17


def merge_body(keep, send, got, out):
    eff = send[2 * Z : 2 * Z + 1, :128] + got[2 * Z : 2 * Z + 1, :128]
    for p in range(NCHIP):
        rows = slice(p * 8, p * 8 + 8)
        tot = keep[rows, :] + got[rows, :]
        out[p * CH : p * CH + 8, :] = tot[:, :128]
        out[p * CH + 8 : p * CH + 16, :] = tot[:, 128:]
        out[p * CH + 16 : p * CH + 17, :] = eff


def sum_body(parts, out, eff):
    tot = [None, None, None]
    for p in range(NCHIP):
        new = (
            parts[p * CH : p * CH + 8, :],
            parts[p * CH + 8 : p * CH + 16, :],
            parts[p * CH + 16 : p * CH + 17, :],
        )
        tot = [n if o is None else o + n for o, n in zip(tot, new)]
    both = jnp.concatenate(tot[:2], axis=1)
    eff[...] = tot[2]
    for p in range(NCHIP):
        out[p] = both


def place_half(half, src, out, sem):
    copies = []
    for s in range(2):
        copies.append(
            pltpu.make_async_copy(src.at[s * Z : (s + 1) * Z, :], out.at[2 * half + s], sem.at[s])
        )
        copies[-1].start()
    for copy in copies:
        copy.wait()


def own_body(own, out, sem):
    place_half(lax.axis_index("c"), own, out, sem)


def other_body(got, _, out, sem):
    place_half(1 - lax.axis_index("c"), got, out, sem)


def exchange(la, lb, ta, tb):
    return (
        lax.ppermute(la, LON, LON_A),
        lax.ppermute(lb, LON, LON_B),
        lax.ppermute(ta, LAT, LAT_A),
        lax.ppermute(tb, LAT, LAT_B),
    )


def body(
    final_cotangent,
    saved_start,
    saved_middle,
    residuals,
    row_cells,
    row_count,
    ocean_mask,
    cell_eez,
    effort,
    kernel,
    mix,
    assim,
    mortality,
    select,
    weight,
    spread,
):
    wt, spr = weight.reshape(1, Z), spread.reshape(1, Z)
    any_ = pl.BlockSpec(memory_space=pl.ANY)
    field = (G, N, Z)
    rims = [vmem((G + 1, CJ, Z))] * 2 + [vmem((G + 1, CI, Z))] * 2
    *rim, pay = call(
        prep_body,
        rims + [vmem((2 * NCHIP, 128))],
        [any_] + [vm()] * 4,
        [
            pltpu.VMEM((2, G, CJ, Z), F32),
            pltpu.VMEM((2, G, CI, 8, Z), F32),
            pltpu.SemaphoreType.DMA((4,)),
        ],
        flops=2**27,
        nbytes=3 * MIB,
        place=False,
    )(final_cotangent, ocean_mask, row_cells.T, row_count.reshape(1, -1), residuals)
    rim = exchange(*rim)
    pay = lax.all_to_all(pay, ALL, 0, 0, tiled=True)
    pay, middle = lax.optimization_barrier((pay, saved_middle))

    ocol, ecol, zone, turn, st, prey, eaten, feed, gs, gain, cot = call(
        first_body,
        [vmem((N, 128))] * 2
        + [vmem((N, 128), BF16), vmem((G, Z, Z), BF16)]
        + [vmem(field, BF16)] * 3
        + [vmem(field), vmem((N, 128)), vmem(field), vmem((G, CI, CJ, Z))],
        [sm(), sm(), any_, any_] + [vm()] * 7,
        [pltpu.VMEM(field, F32), pltpu.SemaphoreType.DMA((CHUNKS + 1,))],
        flops=2**32,
        nbytes=16 * MIB,
        vmem=8,
        far=(2, 3),
    )(
        *(mix, assim, middle.reshape(field), final_cotangent, kernel, mortality, select, wt),
        *(ocean_mask, cell_eez, effort.reshape(1, EEZS)),
    )
    pads = pltpu.VMEM((G, CI + 2, CJ + 16, Z), F32)
    cot, grm, genc, eff, near, catch, *rim = call(
        adj_body,
        [vmem((G, CI, CJ, Z))]
        + [vmem(field, BF16)] * 2
        + [vmem((8, 128)), vmem((N, 128)), vmem((N, 128))]
        + [vmem((G, CJ, Z))] * 2
        + [vmem((G, CI, Z))] * 2,
        [sm(), sm()] + [vm()] * 18,
        [pltpu.VMEM((CI + 2, CJ + 16, 128), F32), pads]
        + [pltpu.VMEM(field, F32)] * 2
        + [pltpu.VMEM((N, 128), F32)] * 2
        + [pltpu.VMEM((N, SLOTS * 128), BF16)]
        + [pltpu.VMEM((SLOTS * 128, 256), BF16)] * 2,
        flops=2**30,
        nbytes=16 * MIB,
        vmem=16,
    )(
        *(mix, assim, cot, *rim, ocol, ecol, pay, gs, zone, st, feed, gain),
        *(kernel, turn, select, wt, spr),
    )
    rim = exchange(*rim)
    kp = call(part_body, vmem((G, Z, Z)), [vm()] * 4, flops=2**29, nbytes=5 * MIB)(
        eaten, grm, genc, prey
    )
    st = saved_start.reshape(field)
    prey, eaten, feed, gs = call(
        second_body,
        [vmem(field, BF16)] * 2 + [vmem(field), vmem((N, 128))],
        [sm()] + [vm()] * 4,
        flops=2**32,
        nbytes=16 * MIB,
    )(mix, st, turn, select, wt)
    m, ge, q, ef, send, grm, genc = call(
        last_body,
        [pltpu.HBM(field, F32)] * 2 + [pltpu.HBM((N, 128), F32)] * 2 + [vmem((2 * Z + 8, Z))] + [vmem(field, BF16)] * 2,
        [sm(), sm()] + [vm()] * 20,
        [pads]
        + [pltpu.VMEM(field, F32)] * 2
        + [pltpu.VMEM((N, 128), F32)] * 2
        + [pltpu.SemaphoreType.DMA((4,))],
        flops=2**30,
        nbytes=16 * MIB,
        vmem=16,
        out_far=4,
    )(
        *(mix, assim, cot, *rim, ocol, ecol, catch, gs, zone, st, prey, eaten, feed),
        *(turn, select, spr, near, kp, eff),
    )
    block = pl.BlockSpec((G, R, Z), lambda n: (0, n, 0))
    cells = pl.BlockSpec((R, 128), lambda n: (n, 0))
    whole = pl.BlockSpec((G, Z), lambda n: (0, 0))
    cot = pl.pallas_call(
        rest_body,
        grid=(CHUNKS,),
        out_shape=sds(field),
        in_specs=[sm(), sm(), block, block, block, cells, cells]
        + [pl.BlockSpec((G, Z, Z), lambda n: (0, 0, 0)), whole, whole]
        + [pl.BlockSpec((1, Z), lambda n: (0, 0))],
        out_specs=block,
        scratch_shapes=[pltpu.VMEM((G, R, Z), F32)] * 2 + [pltpu.VMEM((G, Z, Z), BF16)],
        compiler_params=pltpu.CompilerParams(vmem_limit_bytes=16 * MIB),
        cost_estimate=pl.CostEstimate(flops=2**30, bytes_accessed=12 * MIB, transcendentals=0),
    )(mix, assim, *map(in_hbm, (saved_start.reshape(field), m, ge, q, ef, kernel)), mortality, select, wt)
    cot = cot.reshape(G, CI, CJ, Z)

    got = lax.ppermute(send, "c", CORE)
    keep = call(keep_body, vmem((2 * Z, Z)), [vm()] * 5, flops=2**28, nbytes=4 * MIB)(
        kp, eaten, grm, genc, prey
    )
    chunks = call(merge_body, vmem((NCHIP * CH, 128)), [vm()] * 3, nbytes=2 * MIB)(keep, send, got)
    chunks = lax.all_to_all(chunks.reshape(NCHIP, 1, CH * 128), CHIPS, 0, 0, tiled=True)
    chunks = chunks.reshape(NCHIP * CH, 128)
    own, eff = call(sum_body, [vmem((NCHIP, 8, Z)), vmem((1, 128))], [vm()], nbytes=MIB)(chunks)
    own, cot = lax.optimization_barrier((own, cot))
    own = lax.all_to_all(own, CHIPS, 0, 0, tiled=True).reshape(2 * Z, Z)
    got = lax.ppermute(own, "c", CORE)
    whole = [pltpu.HBM((G, Z, Z), F32)]
    sems = [pltpu.SemaphoreType.DMA((2,))]
    total = call(own_body, whole, [vm()], sems, nbytes=MIB, out_far=1)(own)[0]
    total = call(
        other_body, whole, [vm(), any_], sems, nbytes=MIB, out_far=1, far=(1,), aliases={1: 0}
    )(got, total)[0]
    return cot, total, eff[0, :EEZS]


def solution(mesh):
    fine = Mesh(mesh.devices.reshape(2, 4, 2, 4, 2), ("zl", "x", "c", "y", "zh"))
    field = P(None, LON, LAT, None)
    placed = (
        field,
        field,
        field,
        P(None, ALL),
        P(ALL, None),
        P(ALL),
        P(LON, LAT),
        P(LON, LAT),
    ) + (P(),) * 8
    return jax.shard_map(
        body,
        mesh=fine,
        in_specs=placed,
        out_specs=(field, P(), P()),
        check_vma=False,
    )
```

```python
import functools

import jax
import jax.numpy as jnp
from jax import lax
from jax.experimental import pallas as pl
from jax.experimental.pallas import tpu as pltpu
from jax.sharding import Mesh, PartitionSpec as P

G, Z = 4, 256
CI, CJ = 16, 32
N = CI * CJ
EEZS = 64
H = 0.5
SLOTS = 8
F32, BF16 = jnp.float32, jnp.bfloat16
LON, LAT = ("zl", "x", "c"), ("y", "zh")
ALL = LON + LAT
CHIPS = ("zl", "x", "y", "zh")
NCHIP = 64
MIB = 1024 * 1024
HI = lax.Precision.HIGHEST

LON_A = [(i, i ^ 1) for i in range(16)]
LON_B = [(i, (i + 1) % 16 if i % 2 else (i - 1) % 16) for i in range(16)]
LAT_A = [(i, i ^ 1) for i in range(8)]
LAT_B = [(i, i + 1 if i % 2 else i - 1) for i in range(1, 7)]
CORE = [(0, 1), (1, 0)]


def sds(shape, dtype=F32):
    return jax.ShapeDtypeStruct(shape, dtype)


def vmem(shape, dtype=F32):
    return pltpu.VMEM(shape, dtype)


def vm():
    return pl.BlockSpec(memory_space=pltpu.VMEM)


def sm():
    return pl.BlockSpec(memory_space=pltpu.SMEM)


def call(body, outs, ins, scratch=(), flops=0, nbytes=0, vmem=6, place=True, far=(), out_far=0, aliases={}):
    many = isinstance(outs, list)
    spots = [pl.BlockSpec(memory_space=pl.ANY) if n < out_far else vm() for n in range(len(outs) if many else 1)]
    run = pl.pallas_call(
        body,
        out_shape=outs,
        in_specs=ins,
        out_specs=spots if many else vm(),
        scratch_shapes=list(scratch),
        input_output_aliases=aliases,
        compiler_params=pltpu.CompilerParams(vmem_limit_bytes=vmem * MIB),
        cost_estimate=pl.CostEstimate(flops=flops, bytes_accessed=nbytes, transcendentals=0),
    )

    def go(*args):
        return run(
            *[
                in_hbm(a) if not place or n in far else near_core(a) if a.size >= 8192 else a
                for n, a in enumerate(args)
            ]
        )

    return go


def near_core(x):
    return pltpu.with_memory_space_constraint(x, pltpu.VMEM)


def in_hbm(x):
    return pltpu.with_memory_space_constraint(x, pltpu.HBM)


def nt(a, b, **kw):
    return lax.dot_general(a, b, (((1,), (1,)), ((), ())), preferred_element_type=F32, **kw)


def nn(a, b, **kw):
    return lax.dot_general(a, b, (((1,), (0,)), ((), ())), preferred_element_type=F32, **kw)


def tn(a, b, **kw):
    return lax.dot_general(a, b, (((0,), (0,)), ((), ())), preferred_element_type=F32, **kw)


def split(x):
    hi = x.astype(BF16).astype(F32)
    return hi, x - hi


def two(x):
    return jnp.concatenate([x, x], axis=1)


def column(row, n, width):
    eye = lax.broadcasted_iota(jnp.int32, (n, n), 0) == lax.broadcasted_iota(jnp.int32, (n, n), 1)
    col = jnp.sum(jnp.where(eye, jnp.broadcast_to(row, (n, n)), 0.0), axis=1, keepdims=True)
    return jnp.broadcast_to(col, (n, width))


def prep_body(c, ocean, cells, count, resid, la, lb, ta, tb, pay, rim_i, rim_j, sem):
    par_i, par_j = lax.axis_index("c"), lax.axis_index("zh")
    copies = [
        pltpu.make_async_copy(c.at[:, CI - 1], rim_i.at[0], sem.at[0]),
        pltpu.make_async_copy(c.at[:, 0], rim_i.at[1], sem.at[1]),
        pltpu.make_async_copy(c.at[:, :, CJ - 8 : CJ, :], rim_j.at[0], sem.at[2]),
        pltpu.make_async_copy(c.at[:, :, 0:8, :], rim_j.at[1], sem.at[3]),
    ]
    for copy in copies:
        copy.start()
    ents, rows = cells.shape
    ne = rows * ents
    devices = 2 * NCHIP
    tile_e = lax.broadcasted_iota(jnp.int32, (ents, ne), 1) // rows == lax.broadcasted_iota(
        jnp.int32, (ents, ne), 0
    )
    tile_r = lax.broadcasted_iota(jnp.int32, (rows, ne), 1) % rows == lax.broadcasted_iota(
        jnp.int32, (rows, ne), 0
    )
    tile_rf = tile_r.astype(F32)
    lon_i = (cells[...] // 256).astype(F32)
    lat_i = (cells[...] % 256).astype(F32)
    r_hi, r_rest = split(resid[...])
    r_mid, r_lo = split(r_rest)
    few = jnp.concatenate([count[...].astype(F32), r_hi, r_mid, r_lo, jnp.zeros((1, rows), F32)], axis=0)
    wide = nn(
        jnp.concatenate([lon_i, lat_i, few], axis=0).astype(BF16), tile_rf.astype(BF16)
    )

    def flat(x):
        return jnp.sum(jnp.where(tile_e, x, 0.0), axis=0, keepdims=True)

    i_row = flat(wide[:ents]).astype(jnp.int32)
    j_row = flat(wide[ents : 2 * ents]).astype(jnp.int32)
    few = wide[2 * ents :]
    n_row = few[0:1]
    r_row = few[1:3] + few[3:5] + few[5:7]
    entry = (lax.broadcasted_iota(jnp.int32, (1, ne), 1) // rows).astype(F32)
    vals = jnp.where(entry < n_row, r_row, 0.0)
    owner = (i_row // CI) * 8 + j_row // CJ
    mine = lax.broadcasted_iota(jnp.int32, (devices, ne), 0) == owner
    mine_b = mine.astype(F32).astype(BF16)
    before = (
        lax.broadcasted_iota(jnp.int32, (ne, ne), 0) < lax.broadcasted_iota(jnp.int32, (ne, ne), 1)
    )
    ahead = nn(mine_b, before.astype(F32).astype(BF16))
    rank = jnp.sum(jnp.where(mine, ahead, 0.0), axis=0, keepdims=True).astype(jnp.int32)
    slot = lax.broadcasted_iota(jnp.int32, (SLOTS, ne), 0) == rank
    h0, l0 = split(vals[0:1])
    h1, l1 = split(vals[1:2])
    a_row = ((i_row % CI) * CJ).astype(F32)
    b_row = (j_row % CJ).astype(F32)

    def rows_of(parts):
        put = [jnp.where(slot, jnp.broadcast_to(p, (SLOTS, ne)), 0.0) for p in parts]
        put.append(jnp.zeros((128 - SLOTS * len(parts), ne), F32))
        return jnp.concatenate(put, axis=0).astype(BF16)

    pay[...] = nt(mine_b, rows_of((h0, h1, a_row))) + nt(mine_b, rows_of((l0, l1, b_row)))

    oc = ocean[...].astype(F32)
    edge_i = (column(oc[CI - 1 : CI, :], CJ, Z), column(oc[0:1, :], CJ, Z))
    edge_j = (
        jnp.broadcast_to(oc[:, CJ - 1 : CJ], (CI, Z)),
        jnp.broadcast_to(oc[:, 0:1], (CI, Z)),
    )
    for copy in copies:
        copy.wait()

    def rims(odd, a, b, value):
        for n, (even_to, odd_to) in enumerate(((a, b), (b, a))):
            for g in range(G + 1):
                v = value(n, g)

                @pl.when(odd == 0)
                def _():
                    even_to[g] = v

                @pl.when(odd == 1)
                def _():
                    odd_to[g] = v

    rims(par_i, la, lb, lambda n, g: edge_i[n] if g == G else rim_i[n, g] * edge_i[n])
    rims(
        par_j,
        ta,
        tb,
        lambda n, g: edge_j[n] if g == G else rim_j[n, g, :, 7 if n == 0 else 0, :] * edge_j[n],
    )


def tables(ocean, eez, effort, ocol, ecol, zone):
    oc = ocean[...].astype(F32)
    ez = eez[...].astype(F32)
    lane = lax.broadcasted_iota(jnp.int32, (CJ, 128), 1)
    eff = jnp.concatenate([effort[...], jnp.zeros((1, 128 - EEZS), F32)], axis=1)
    for i in range(CI):
        rows = slice(i * CJ, (i + 1) * CJ)
        ocol[rows] = column(oc[i : i + 1, :], CJ, 128)
        here = (column(ez[i : i + 1, :], CJ, 128).astype(jnp.int32) == lane).astype(F32)
        zone[rows] = here.astype(BF16)
        ecol[rows] = jnp.broadcast_to(jnp.sum(here * eff, axis=1, keepdims=True), (CJ, 128))


def gather_catch(pay, hot, hi, lo):
    got = pay[...]
    flip = got.T
    for k in range(SLOTS):
        where = flip[2 * SLOTS + k : 2 * SLOTS + k + 1, :].astype(jnp.int32)
        cell = lax.broadcasted_iota(jnp.int32, (N, 128), 0)
        hot[:, k * 128 : (k + 1) * 128] = (cell == where).astype(F32).astype(BF16)
        pair = jnp.concatenate(
            [
                jnp.broadcast_to(got[:, k : k + 1], (128, 128)),
                jnp.broadcast_to(got[:, SLOTS + k : SLOTS + k + 1], (128, 128)),
            ],
            axis=1,
        )
        top, rest = split(pair)
        hi[k * 128 : (k + 1) * 128, :] = top.astype(BF16)
        lo[k * 128 : (k + 1) * 128, :] = rest.astype(BF16)
    return nn(hot[...], hi[...]) + nn(hot[...], lo[...])


def by_zone(y, zone):
    top, rest = split(y[...])
    parts = jnp.concatenate([top, rest], axis=1).astype(BF16)
    return jnp.sum(tn(parts, zone[...]), axis=0, keepdims=True)


R = 128
CHUNKS = N // R


def recip(d):
    r = pltpu.reciprocal(d, approx=True)
    return r * (2.0 - d * r)


def mixed(rows_of, mix, k, turned=False):
    tot = None
    for g in range(G):
        term = (mix[g, k] if turned else mix[k, g]) * rows_of[g]
        tot = term if tot is None else tot + term
    return tot


def gain_of(k, mix, assim, mort, sel, ef, feed, rem):
    tot = (1.0 - H * mort[k : k + 1, :]) - (H * sel[k : k + 1, :]) * ef + (H * assim[k]) * feed
    for g in range(G):
        tot = tot + (-H * mix[g, k]) * rem[g]
    return tot


def forward_rows(rows, mix, st, turn, sel, wt, prey, eaten, feed, gs):
    s = [st[k, rows, :].astype(F32) for k in range(G)]
    part = None
    for k in range(G):
        term = (sel[k : k + 1, :] * wt[...]) * s[k]
        part = term if part is None else part + term
    gs[rows, :] = part[:, :128] + part[:, 128:]
    for g in range(G):
        prey[g, rows, :] = mixed(s, mix, g).astype(BF16)
    for g in range(G):
        enc = nn(prey[g, rows, :], turn[g])
        fd = enc * recip(enc + 1.0)
        feed[g, rows, :] = fd
        eaten[g, rows, :] = (st[g, rows, :].astype(F32) * fd).astype(BF16)


def first_body(*refs):
    mix, assim, saved, c_far, ker, mort, sel, wt, ocean, eez, effort = refs[:11]
    ocol, ecol, zone, turn, st, prey, eaten, feed, gs, gain, c, rem, sem = refs[11:]
    copies = []
    for n in range(CHUNKS):
        rows = slice(n * R, (n + 1) * R)
        copies.append(pltpu.make_async_copy(saved.at[:, rows, :], st.at[:, rows, :], sem.at[n]))
        copies[-1].start()
    copies.append(pltpu.make_async_copy(c_far, c, sem.at[CHUNKS]))
    copies[-1].start()
    for g in range(G):
        turn[g] = ker[g].T
    tables(ocean, eez, effort, ocol, ecol, zone)
    for n in range(CHUNKS):
        rows = slice(n * R, (n + 1) * R)
        copies[n].wait()
        forward_rows(rows, mix, st, turn, sel, wt, prey, eaten, feed, gs)
        for g in range(G):
            rem[g, rows, :] = nn(eaten[g, rows, :], ker[g])
        parts = [rem[g, rows, :] for g in range(G)]
        ef = two(ecol[rows, :])
        for k in range(G):
            gain[k, rows, :] = gain_of(k, mix, assim, mort, sel, ef, feed[k, rows, :], parts)
    copies[CHUNKS].wait()


def second_body(mix, st, turn, sel, wt, prey, eaten, feed, gs):
    for n in range(CHUNKS):
        forward_rows(slice(n * R, (n + 1) * R), mix, st, turn, sel, wt, prey, eaten, feed, gs)


def fill(pad, opad, c, la, lb, ta, tb, ocol):
    par_i, par_j = lax.axis_index("c"), lax.axis_index("zh")
    at_a = jnp.where(par_i == 0, CI + 1, 0)
    at_b = CI + 1 - at_a
    row_a = jnp.where(par_j == 0, CJ + 8, 7)
    row_b = CJ + 15 - row_a
    for g in range(G):
        pad[g, at_a, 8 : 8 + CJ, :] = la[g]
        pad[g, at_b, 8 : 8 + CJ, :] = lb[g]
        for i in range(CI):
            pad[g, i + 1, pl.ds(row_a, 1), :] = ta[g, i : i + 1, :]
            pad[g, i + 1, pl.ds(row_b, 1), :] = tb[g, i : i + 1, :]
    if opad is not None:
        opad[at_a, 8 : 8 + CJ, :] = la[G, :, :128]
        opad[at_b, 8 : 8 + CJ, :] = lb[G, :, :128]
        for i in range(CI):
            opad[i + 1, pl.ds(row_a, 1), :] = ta[G, i : i + 1, :128]
            opad[i + 1, pl.ds(row_b, 1), :] = tb[G, i : i + 1, :128]
    for i in range(CI):
        o = ocol[i * CJ : (i + 1) * CJ, :]
        if opad is not None:
            opad[i + 1, 8 : 8 + CJ, :] = o
        for g in range(G):
            pad[g, i + 1, 8 : 8 + CJ, :] = c[g, i] * two(o)


def around(pad, i, lanes):
    return (pad[i + 2, 8 : 8 + CJ, lanes] + pad[i, 8 : 8 + CJ, lanes]) + (
        pad[i + 1, 9 : 9 + CJ, lanes] + pad[i + 1, 7 : 7 + CJ, lanes]
    )


def spread_row(i, pad, s4, mix, ocol, catch, gs, st, sel, spr, m_out, grm, y):
    rows = pl.ds(i * CJ, CJ)
    o = ocol[rows, :]
    acc = None
    for z in range(2):
        lanes = slice(z * 128, (z + 1) * 128)
        ms = []
        for g in range(G):
            mid = pad[g, i + 1, 8 : 8 + CJ, lanes]
            m = mid + spr[:, lanes] * (o * around(pad.at[g], i, lanes) - s4 * mid)
            m_out[g, rows, lanes] = m
            ms.append(m * st[g, rows, lanes].astype(F32))
            term = sel[g : g + 1, lanes] * ms[-1]
            acc = term if acc is None else acc + term
        for g in range(G):
            tot = None
            for k in range(G):
                term = (-H * mix[g, k]) * ms[k]
                tot = term if tot is None else tot + term
            grm[g, rows, lanes] = tot.astype(BF16)
    y[rows, :] = H * ((o * catch[rows, :]) * gs[rows, :] - acc)


def enc_grad(g, assim, m, s, ge, fd):
    inv = 1.0 - fd
    return (((H * assim[g]) * (m * s) + ge * s) * (inv * inv)).astype(BF16)


def adj_body(*refs):
    mix, assim, c, la, lb, ta, tb, ocol, ecol, pay, gs, zone, st, feed, gain, ker, turn, sel, wt, spr = refs[:20]
    c_out, grm, genc, eff, near, later, ola, olb, ota, otb, opad, pad, m_scr, t_scr, y, catch, hot, hi, lo = refs[20:]
    par_i, par_j = lax.axis_index("c"), lax.axis_index("zh")
    fill(pad, opad, c, la, lb, ta, tb, ocol)
    caught = gather_catch(pay, hot, hi, lo)
    later[...] = caught[:, :128]
    catch[...] = caught[:, 128:]
    for n in range(CHUNKS):
        rows = slice(n * R, (n + 1) * R)
        for i in range(n * R // CJ, (n + 1) * R // CJ):
            s4 = around(opad, i, slice(None))
            near[i * CJ : (i + 1) * CJ, :] = s4
            spread_row(i, pad, s4, mix, ocol, catch, gs, st, sel, spr, m_scr, grm, y)
        q = two(H * ocol[rows, :] * ecol[rows, :] * catch[rows, :])
        for g in range(G):
            ge = nn(grm[g, rows, :], turn[g])
            m, fd = m_scr[g, rows, :], feed[g, rows, :]
            genc[g, rows, :] = enc_grad(g, assim, m, st[g, rows, :].astype(F32), ge, fd)
            m_scr[g, rows, :] = m * gain[g, rows, :] + ge * fd + q * (sel[g : g + 1, :] * wt[...])
        for g in range(G):
            t_scr[g, rows, :] = nn(genc[g, rows, :], ker[g])
        for i in range(n * R // CJ, (n + 1) * R // CJ):
            here = slice(i * CJ, (i + 1) * CJ)
            gp = [t_scr[g, here, :] for g in range(G)]
            for k in range(G):
                c_out[k, i] = m_scr[k, here, :] + mixed(gp, mix, k, True)
    eff[...] = jnp.broadcast_to(by_zone(y, zone), (8, 128))

    def lon_rims(hi, lo):
        for g in range(G):
            hi[g] = c_out[g, CI - 1] * two(ocol[N - CJ : N, :])
            lo[g] = c_out[g, 0] * two(ocol[0:CJ, :])

    def lat_rims(hi, lo):
        for g in range(G):
            for i in range(CI):
                at = i * CJ
                hi[g, i : i + 1, :] = c_out[g, i, CJ - 1 : CJ, :] * two(ocol[at + CJ - 1 : at + CJ, :])
                lo[g, i : i + 1, :] = c_out[g, i, 0:1, :] * two(ocol[at : at + 1, :])

    pl.when(par_i == 0)(lambda: lon_rims(ola, olb))
    pl.when(par_i == 1)(lambda: lon_rims(olb, ola))
    pl.when(par_j == 0)(lambda: lat_rims(ota, otb))
    pl.when(par_j == 1)(lambda: lat_rims(otb, ota))


def part_body(eaten, grm, genc, prey, kp):
    for g in range(G):
        kp[g] = tn(eaten[g], grm[g]) + tn(genc[g], prey[g])


def kernel_half(dst, half, kp, eaten, grm, genc, prey):
    for s in range(2):
        g = 2 * half + s
        dst[s * Z : (s + 1) * Z, :] = kp[g] + tn(eaten[g], grm[g]) + tn(genc[g], prey[g])


def keep_body(kp, eaten, grm, genc, prey, keep):
    kernel_half(keep, lax.axis_index("c"), kp, eaten, grm, genc, prey)


def last_body(*refs):
    mix, assim, c, la, lb, ta, tb, ocol, ecol, catch, gs, zone, st, prey, eaten, feed, turn, sel, spr, near, kp, eff = refs[:22]
    m_hbm, ge_hbm, q_hbm, e_hbm, send, grm, genc, pad, m_scr, ge_scr, y, q_scr, sem = refs[22:]
    core = lax.axis_index("c")
    fill(pad, None, c, la, lb, ta, tb, ocol)
    q_scr[...] = H * ocol[...] * ecol[...] * catch[...]
    copies = [
        pltpu.make_async_copy(q_scr, q_hbm, sem.at[0]),
        pltpu.make_async_copy(ecol, e_hbm, sem.at[1]),
    ]
    for copy in copies:
        copy.start()

    @pl.loop(0, CI)
    def _(i):
        s4 = near[pl.ds(i * CJ, CJ), :]
        spread_row(i, pad, s4, mix, ocol, catch, gs, st, sel, spr, m_scr, grm, y)

    copies.append(pltpu.make_async_copy(m_scr, m_hbm, sem.at[2]))
    copies[-1].start()
    for g in range(G):
        ge_scr[g] = nn(grm[g], turn[g])
    copies.append(pltpu.make_async_copy(ge_scr, ge_hbm, sem.at[3]))
    copies[-1].start()

    @pl.loop(0, CI)
    def _(i):
        rows = pl.ds(i * CJ, CJ)
        for g in range(G):
            genc[g, rows, :] = enc_grad(
                g,
                assim,
                m_scr[g, rows, :],
                st[g, rows, :].astype(F32),
                ge_scr[g, rows, :],
                feed[g, rows, :],
            )

    send[2 * Z :, :] = two(eff[...] + by_zone(y, zone))
    kernel_half(send, 1 - core, kp, eaten, grm, genc, prey)
    for copy in copies:
        copy.wait()


def rest_body(mix, assim, saved, m_in, ge_in, q_in, ecol, ker, mort, sel, wt, out, feed, rem, turn):
    @pl.when(pl.program_id(0) == 0)
    def _():
        for g in range(G):
            turn[g] = ker[g].T

    s = [saved[k].astype(F32) for k in range(G)]
    for g in range(G):
        enc = nn(mixed(s, mix, g).astype(BF16), turn[g])
        fd = enc * recip(enc + 1.0)
        feed[g] = fd
        rem[g] = nn((s[g] * fd).astype(BF16), ker[g])
    parts = [rem[g] for g in range(G)]
    ef, q = two(ecol[...]), two(q_in[...])
    for k in range(G):
        fd = feed[k]
        gain = gain_of(k, mix, assim, mort, sel, ef, fd, parts)
        out[k] = m_in[k] * gain + ge_in[k] * fd + q * (sel[k : k + 1, :] * wt[...])
    for g in range(G):
        rem[g] = nn(enc_grad(g, assim, m_in[g], saved[g].astype(F32), ge_in[g], feed[g]), ker[g])
    parts = [rem[g] for g in range(G)]
    for k in range(G):
        out[k] = out[k] + mixed(parts, mix, k, True)


CH = 17


def merge_body(keep, send, got, out):
    eff = send[2 * Z : 2 * Z + 1, :128] + got[2 * Z : 2 * Z + 1, :128]
    for p in range(NCHIP):
        rows = slice(p * 8, p * 8 + 8)
        tot = keep[rows, :] + got[rows, :]
        out[p * CH : p * CH + 8, :] = tot[:, :128]
        out[p * CH + 8 : p * CH + 16, :] = tot[:, 128:]
        out[p * CH + 16 : p * CH + 17, :] = eff


def sum_body(parts, out, eff):
    tot = [None, None, None]
    for p in range(NCHIP):
        new = (
            parts[p * CH : p * CH + 8, :],
            parts[p * CH + 8 : p * CH + 16, :],
            parts[p * CH + 16 : p * CH + 17, :],
        )
        tot = [n if o is None else o + n for o, n in zip(tot, new)]
    both = jnp.concatenate(tot[:2], axis=1)
    eff[...] = tot[2]
    for p in range(NCHIP):
        out[p] = both


def place_half(half, src, out, sem):
    copies = []
    for s in range(2):
        copies.append(
            pltpu.make_async_copy(src.at[s * Z : (s + 1) * Z, :], out.at[2 * half + s], sem.at[s])
        )
        copies[-1].start()
    for copy in copies:
        copy.wait()


def own_body(own, out, sem):
    place_half(lax.axis_index("c"), own, out, sem)


def other_body(got, _, out, sem):
    place_half(1 - lax.axis_index("c"), got, out, sem)


def exchange(la, lb, ta, tb):
    return (
        lax.ppermute(la, LON, LON_A),
        lax.ppermute(lb, LON, LON_B),
        lax.ppermute(ta, LAT, LAT_A),
        lax.ppermute(tb, LAT, LAT_B),
    )


def body(
    final_cotangent,
    saved_start,
    saved_middle,
    residuals,
    row_cells,
    row_count,
    ocean_mask,
    cell_eez,
    effort,
    kernel,
    mix,
    assim,
    mortality,
    select,
    weight,
    spread,
):
    wt, spr = weight.reshape(1, Z), spread.reshape(1, Z)
    any_ = pl.BlockSpec(memory_space=pl.ANY)
    field = (G, N, Z)
    rims = [vmem((G + 1, CJ, Z))] * 2 + [vmem((G + 1, CI, Z))] * 2
    *rim, pay = call(
        prep_body,
        rims + [vmem((2 * NCHIP, 128))],
        [any_] + [vm()] * 4,
        [
            pltpu.VMEM((2, G, CJ, Z), F32),
            pltpu.VMEM((2, G, CI, 8, Z), F32),
            pltpu.SemaphoreType.DMA((4,)),
        ],
        flops=2**27,
        nbytes=3 * MIB,
        place=False,
    )(final_cotangent, ocean_mask, row_cells.T, row_count.reshape(1, -1), residuals)
    rim = exchange(*rim)
    pay = lax.all_to_all(pay, ALL, 0, 0, tiled=True)
    pay, middle = lax.optimization_barrier((pay, saved_middle))

    ocol, ecol, zone, turn, st, prey, eaten, feed, gs, gain, cot = call(
        first_body,
        [vmem((N, 128))] * 2
        + [vmem((N, 128), BF16), vmem((G, Z, Z), BF16)]
        + [vmem(field, BF16)] * 3
        + [vmem(field), vmem((N, 128)), vmem(field), vmem((G, CI, CJ, Z))],
        [sm(), sm(), any_, any_] + [vm()] * 7,
        [pltpu.VMEM(field, F32), pltpu.SemaphoreType.DMA((CHUNKS + 1,))],
        flops=2**32,
        nbytes=16 * MIB,
        vmem=8,
        far=(2, 3),
    )(
        *(mix, assim, middle.reshape(field), final_cotangent, kernel, mortality, select, wt),
        *(ocean_mask, cell_eez, effort.reshape(1, EEZS)),
    )
    pads = pltpu.VMEM((G, CI + 2, CJ + 16, Z), F32)
    cot, grm, genc, eff, near, catch, *rim = call(
        adj_body,
        [vmem((G, CI, CJ, Z))]
        + [vmem(field, BF16)] * 2
        + [vmem((8, 128)), vmem((N, 128)), vmem((N, 128))]
        + [vmem((G, CJ, Z))] * 2
        + [vmem((G, CI, Z))] * 2,
        [sm(), sm()] + [vm()] * 18,
        [pltpu.VMEM((CI + 2, CJ + 16, 128), F32), pads]
        + [pltpu.VMEM(field, F32)] * 2
        + [pltpu.VMEM((N, 128), F32)] * 2
        + [pltpu.VMEM((N, SLOTS * 128), BF16)]
        + [pltpu.VMEM((SLOTS * 128, 256), BF16)] * 2,
        flops=2**30,
        nbytes=16 * MIB,
        vmem=16,
    )(
        *(mix, assim, cot, *rim, ocol, ecol, pay, gs, zone, st, feed, gain),
        *(kernel, turn, select, wt, spr),
    )
    rim = exchange(*rim)
    kp = call(part_body, vmem((G, Z, Z)), [vm()] * 4, flops=2**29, nbytes=5 * MIB)(
        eaten, grm, genc, prey
    )
    st = saved_start.reshape(field)
    prey, eaten, feed, gs = call(
        second_body,
        [vmem(field, BF16)] * 2 + [vmem(field), vmem((N, 128))],
        [sm()] + [vm()] * 4,
        flops=2**32,
        nbytes=16 * MIB,
    )(mix, st, turn, select, wt)
    m, ge, q, ef, send, grm, genc = call(
        last_body,
        [pltpu.HBM(field, F32)] * 2 + [pltpu.HBM((N, 128), F32)] * 2 + [vmem((2 * Z + 8, Z))] + [vmem(field, BF16)] * 2,
        [sm(), sm()] + [vm()] * 20,
        [pads]
        + [pltpu.VMEM(field, F32)] * 2
        + [pltpu.VMEM((N, 128), F32)] * 2
        + [pltpu.SemaphoreType.DMA((4,))],
        flops=2**30,
        nbytes=16 * MIB,
        vmem=16,
        out_far=4,
    )(
        *(mix, assim, cot, *rim, ocol, ecol, catch, gs, zone, st, prey, eaten, feed),
        *(turn, select, spr, near, kp, eff),
    )
    block = pl.BlockSpec((G, R, Z), lambda n: (0, n, 0))
    cells = pl.BlockSpec((R, 128), lambda n: (n, 0))
    whole = pl.BlockSpec((G, Z), lambda n: (0, 0))
    cot = pl.pallas_call(
        rest_body,
        grid=(CHUNKS,),
        out_shape=sds(field),
        in_specs=[sm(), sm(), block, block, block, cells, cells]
        + [pl.BlockSpec((G, Z, Z), lambda n: (0, 0, 0)), whole, whole]
        + [pl.BlockSpec((1, Z), lambda n: (0, 0))],
        out_specs=block,
        scratch_shapes=[pltpu.VMEM((G, R, Z), F32)] * 2 + [pltpu.VMEM((G, Z, Z), BF16)],
        compiler_params=pltpu.CompilerParams(vmem_limit_bytes=16 * MIB),
        cost_estimate=pl.CostEstimate(flops=2**30, bytes_accessed=12 * MIB, transcendentals=0),
    )(mix, assim, *map(in_hbm, (saved_start.reshape(field), m, ge, q, ef, kernel)), mortality, select, wt)
    cot = cot.reshape(G, CI, CJ, Z)

    got = lax.ppermute(send, "c", CORE)
    keep = call(keep_body, vmem((2 * Z, Z)), [vm()] * 5, flops=2**28, nbytes=4 * MIB)(
        kp, eaten, grm, genc, prey
    )
    chunks = call(merge_body, vmem((NCHIP * CH, 128)), [vm()] * 3, nbytes=2 * MIB)(keep, send, got)
    chunks = lax.all_to_all(chunks.reshape(NCHIP, 1, CH * 128), CHIPS, 0, 0, tiled=True)
    chunks = chunks.reshape(NCHIP * CH, 128)
    own, eff = call(sum_body, [vmem((NCHIP, 8, Z)), vmem((1, 128))], [vm()], nbytes=MIB)(chunks)
    own = lax.all_to_all(own, CHIPS, 0, 0, tiled=True).reshape(2 * Z, Z)
    own, cot = lax.optimization_barrier((own, cot))
    got = lax.ppermute(own, "c", CORE)
    whole = [pltpu.HBM((G, Z, Z), F32)]
    sems = [pltpu.SemaphoreType.DMA((2,))]
    total = call(own_body, whole, [vm()], sems, nbytes=MIB, out_far=1)(own)[0]
    total = call(
        other_body, whole, [vm(), any_], sems, nbytes=MIB, out_far=1, far=(1,), aliases={1: 0}
    )(got, total)[0]
    return cot, total, eff[0, :EEZS]


def solution(mesh):
    fine = Mesh(mesh.devices.reshape(2, 4, 2, 4, 2), ("zl", "x", "c", "y", "zh"))
    field = P(None, LON, LAT, None)
    placed = (
        field,
        field,
        field,
        P(None, ALL),
        P(ALL, None),
        P(ALL),
        P(LON, LAT),
        P(LON, LAT),
    ) + (P(),) * 8
    return jax.shard_map(
        body,
        mesh=fine,
        in_specs=placed,
        out_specs=(field, P(), P()),
        check_vma=False,
    )
```
